32 devices in a mesh: dp: 4 (over x, core), vocab: 8 (over z, y).
Axes of the slice: x: 2, y: 2, z: 4, core: 2. Of those that a mesh axis runs over, the one named last changes fastest.
Arguments:
- hidden: bfloat16 [512, 8192], P('dp', 'vocab'), may hold values from -500 to 500, as said below
- norm_gain: float32 [8192], replicated, may hold values from 0.5 to 1.5
- head_weight: bfloat16 [16384, 8192], P('vocab', 'dp'), may hold values from -1 to 1
- target_logits: bfloat16 [512, 16384], P('dp', 'vocab'), may hold values from -20 to 400
- valid_rows: int32 [512], P('dp'), may hold values from 0 to 1, as said below
- parents: int32 [512], P('dp'), may hold values from 0 to 62, as said below
- features: bfloat16 [512, 24576], P('dp', 'vocab'), may hold values from -0.29882812 to 0.29882812
Outputs:
- grad_hidden: bfloat16 [512, 8192], P('vocab', 'dp')
- grad_joining: float32 [8192, 24576], P('dp', 'vocab')
The draws below stay inside these ranges and needn't reach their ends.
Inputs may be any that keep to these rules, and one draw needn't show every extreme that they name: hidden is finite; in some draws a few rows are far from the others. `valid_rows`: row 0 is always valid. `parents`: rows form trees of 64 rows aligned on multiples of 64; a tree's first row has parent 0, every other row a parent before it in its tree, and the last row of each tree has parent 64 - 2.
All inputs are finite; a program needn't handle non-finite values.
Results may differ from the reference program's by a relative error of at most 0.007.
Values may be sent and summed in bfloat16 or wider, within the bound.
No kernel may reach another device: no remote copies, remote signals or barrier semaphores. Data moves between devices by JAX's collectives and lax.ppermute only.
A program may use at most 128 MiB of HBM per device.

```python
import math
import jax
import jax.numpy as jnp
from jax import lax

D = 8192
TREE = 64
ROWS_DEV = 128
VOCAB = 16384
ROWS = 512
JOINED = 24576


def draw_hidden(key, part):
    base_key = jax.random.fold_in(key, 1)
    key_noise, key_rows, key_cols = jax.random.split(base_key, 3)
    col_scale = jnp.exp(jax.random.uniform(key_cols, (1, D), jnp.float32) * math.log(10.0))
    row_scale = jnp.exp(jax.random.uniform(key_rows, (ROWS, 1), jnp.float32) * math.log(10.0))
    values = jax.random.normal(key_noise, (ROWS, D), jnp.float32) * col_scale * row_scale
    return jnp.clip(values, -500.0, 500.0).astype(jnp.bfloat16)


def draw_head_weight(key, part):
    key_noise = jax.random.fold_in(key, 2)
    spread = 3.0 / math.sqrt(D)
    values = jnp.clip(jax.random.normal(key_noise, (VOCAB, D), jnp.float32), -6.0, 6.0) * spread
    return jnp.clip(values, -0.3, 0.3).astype(jnp.bfloat16)


def draw_target_logits(key, part):
    key_noise = jax.random.fold_in(key, 3)
    values = jnp.clip(jax.random.normal(key_noise, (ROWS, VOCAB), jnp.float32) * 3.0, -18.0, 18.0)
    return values.astype(jnp.bfloat16)


def draw_valid_rows(key, part):
    picks = jax.random.randint(jax.random.fold_in(key, 4), (ROWS,), 0, 1000)
    positions = jnp.arange(ROWS, dtype=jnp.int32)
    threshold = 250 + 700 * positions // ROWS
    chosen = (picks < threshold).astype(jnp.int32)
    return jnp.where(positions == 0, 1, chosen).astype(jnp.int32)


def draw_parents(key, part):
    position = jnp.arange(ROWS, dtype=jnp.int32) % TREE
    upper = jnp.maximum(position, 1)
    picks = jax.random.randint(jax.random.fold_in(key, 5), (ROWS,), 0, upper)
    picks = jnp.where(position == TREE - 1, TREE - 2, picks)
    picks = jnp.where(position == 0, 0, picks)
    return picks.astype(jnp.int32)


def shard_levels(key, extent, cuts, smallest, high):
    gain = 1.0
    for dim, parts in cuts:
        steps = jax.random.uniform(jax.random.fold_in(jax.random.fold_in(key, 6), dim), (parts,), jnp.float32, smallest / len(cuts), high / len(cuts))
        gain = gain * jnp.repeat(jnp.exp(steps), extent[dim] // parts).reshape((-1,) + (1,) * (len(extent) - 1 - dim))
    return gain


def scatter_about(own_key, extent, scale, bound, shards=(), kind=jnp.bfloat16):
    gain = shard_levels(own_key, extent, shards, -0.22, 0.18) if shards else 1.0
    result = jax.random.normal(own_key, extent, jnp.float32) * scale * gain
    return jnp.minimum(jnp.maximum(result, -bound), bound).astype(kind)


def setup_inputs(seed: int = 0) -> dict:
    splits = jax.random.split(jax.random.key(seed), 8)
    hidden = draw_hidden(jax.random.fold_in(splits[7], 71), 0)
    norm_gain = jnp.clip(1.0 + 0.1 * jax.random.normal(splits[1], (D,), jnp.float32), 0.5, 1.5)
    head_weight = draw_head_weight(jax.random.fold_in(splits[7], 71), 0)
    target_logits = draw_target_logits(jax.random.fold_in(splits[7], 71), 0)
    valid_rows = draw_valid_rows(jax.random.fold_in(splits[7], 71), 0)
    parents = draw_parents(jax.random.fold_in(splits[7], 71), 0)
    features = scatter_about(splits[6], (ROWS, JOINED), 0.05, 0.29882812, ((0, 4), (1, 8)))
    return dict(hidden=hidden, norm_gain=norm_gain, head_weight=head_weight, target_logits=target_logits, valid_rows=valid_rows, parents=parents, features=features)


def reference(hidden, norm_gain, head_weight, target_logits, valid_rows, parents, features):
    values = hidden.astype(jnp.float32)
    row_factor = lax.rsqrt(lax.optimization_barrier(jnp.mean(values * values, axis=1)) + 1e-05)
    normed = (values * row_factor[:, None] * norm_gain).astype(jnp.bfloat16)
    live_rows = (valid_rows == 1).astype(jnp.float32)
    valid_count = jnp.sum(live_rows)
    row_weight = 1048576.0 * live_rows / valid_count
    block_count = ROWS // ROWS_DEV

    def one_block(inputs):
        normed_block, target_block, weight_block = inputs
        logits = lax.dot_general(normed_block, head_weight, (((1,), (1,)), ((), ())), preferred_element_type=jnp.float32)
        draft_max = lax.optimization_barrier(jnp.max(logits, axis=1, keepdims=True))
        draft_exp = jnp.exp(logits - draft_max)
        draft_probs = draft_exp / lax.optimization_barrier(jnp.sum(draft_exp, axis=1, keepdims=True))
        targets = target_block.astype(jnp.float32)
        target_max = lax.optimization_barrier(jnp.max(targets, axis=1, keepdims=True))
        target_exp = jnp.exp(targets - target_max)
        target_probs = target_exp / lax.optimization_barrier(jnp.sum(target_exp, axis=1, keepdims=True))
        logit_grad = (weight_block[:, None] * (draft_probs - target_probs)).astype(jnp.bfloat16)
        return jnp.dot(logit_grad, head_weight, preferred_element_type=jnp.float32)
    normed_grad = lax.map(one_block, (normed.reshape(block_count, ROWS_DEV, D), target_logits.reshape(block_count, ROWS_DEV, VOCAB), row_weight.reshape(block_count, ROWS_DEV)))
    normed_grad = normed_grad.reshape(ROWS, D)
    row_dot = lax.optimization_barrier(jnp.sum(norm_gain * values * normed_grad, axis=1))
    grad_hidden = (row_factor[:, None] * norm_gain * normed_grad - values * (row_factor ** 3 * row_dot / D)[:, None]).astype(jnp.bfloat16)
    source_rows = jnp.arange(ROWS, dtype=jnp.int32) // TREE * TREE + parents.astype(jnp.int32)
    chosen = jnp.take(features, source_rows, axis=0)
    grad_joining = jnp.dot(grad_hidden.T, chosen, preferred_element_type=jnp.float32)
    return (grad_hidden, grad_joining)
```

```python
import jax
import jax.numpy as jnp
from jax import lax
from jax.sharding import PartitionSpec as P

TREE = 64
CORES = 2
F32 = jnp.float32
BF16 = jnp.bfloat16


def ring_order(rows, columns):
    if columns == 1 or rows == 1:
        return list(range(rows * columns))
    order = [r * columns for r in range(rows)]
    for step in range(rows):
        r = rows - 1 - step
        line = [r * columns + c for c in range(1, columns)]
        order += line if step % 2 == 0 else line[::-1]
    return order


class Ring:
    def __init__(self, size, columns):
        self.size = size
        self.order = ring_order(size // columns, columns)
        place = [0] * size
        for position, index in enumerate(self.order):
            place[index] = position
        self.place = place
        self.position = jnp.asarray(place, jnp.int32)[lax.axis_index("vocab")]

    def shift(self, x, step):
        size, order = self.size, self.order
        return lax.ppermute(
            x, "vocab", [(order[p], order[(p + step) % size]) for p in range(size)]
        )

    def gather(self, block):
        size = self.size
        half = size // 2
        ahead, behind = [block], [block]
        for _ in range((size - 1) // 2):
            ahead.append(self.shift(ahead[-1], 1))
            behind.append(self.shift(behind[-1], -1))
        far = []
        if size % 2 == 0:
            cut = block.shape[0] // 2
            far = [
                jnp.concatenate(
                    [self.shift(ahead[-1][:cut], 1), self.shift(behind[-1][cut:], -1)], axis=0
                )
            ]
        near = ahead[1:][::-1] + [block] + behind[1:]
        line = jnp.stack(far + near)
        start = half if size % 2 == 0 else (size - 1) // 2
        return jnp.roll(line, self.position - start, axis=0)

    def scatter_sum(self, part):
        size = self.size
        steps = (size - 1) // 2
        if size % 2 == 0:
            far = part(size // 2)
            cut = far.shape[0] // 2
            got = self.shift(far[:cut].astype(BF16), 1).astype(F32)
            ahead = part(steps)
            ahead = jnp.concatenate([ahead[:cut] + got, ahead[cut:]], axis=0)
            got = self.shift(far[cut:].astype(BF16), -1).astype(F32)
            behind = part(-steps)
            behind = jnp.concatenate([behind[:cut], behind[cut:] + got], axis=0)
        else:
            ahead, behind = part(steps), part(-steps)
        for step in range(steps - 1, -1, -1):
            got_ahead = self.shift(ahead.astype(BF16), 1).astype(F32)
            got_behind = self.shift(behind.astype(BF16), -1).astype(F32)
            if step > 0:
                ahead = part(step) + got_ahead
                behind = part(-step) + got_behind
            else:
                return part(0) + got_ahead + got_behind


def swap_core(x, size):
    return lax.ppermute(x, "dp", [(i, i ^ 1) for i in range(size)])


def shift_chip(x, size, step):
    return lax.ppermute(x, "dp", [(i, (i + CORES * step) % size) for i in range(size)])


def gather_groups(block, size):
    chips = size // CORES
    mine = [block] + [shift_chip(block, size, -d) for d in range(1, chips)]
    mine = jnp.stack(mine)
    return jnp.stack([mine, swap_core(mine, size)], axis=1)


def body(hidden, norm_gain, head_weight, target_logits, valid_rows, parents, features):
    groups = lax.axis_size("dp")
    parts = lax.axis_size("vocab")
    chips = groups // CORES
    group_index = lax.axis_index("dp")
    vocab_index = lax.axis_index("vocab")
    chip, core = group_index // CORES, group_index % CORES
    group_rows, block_width = hidden.shape
    all_rows = groups * group_rows
    model_width = block_width * parts
    slice_blocks = parts // groups
    slice_width = block_width * slice_blocks
    share_rows = all_rows // parts
    ring = Ring(parts, chips)

    tree_rows = jnp.arange(group_rows, dtype=jnp.int32) // TREE * TREE + parents
    chosen = jnp.take(features, tree_rows, axis=0)
    chosen_all = gather_groups(chosen, groups).reshape(all_rows, -1)

    live_rows = (valid_rows == 1).astype(F32)
    square_part = jnp.sum(jnp.square(hidden.astype(F32)), axis=1)
    small = lax.all_gather(jnp.stack([square_part, live_rows]), ("dp", "vocab"))
    small = small.reshape(groups, parts, 2, group_rows)
    squares = jnp.sum(small[:, :, 0], axis=1)
    valid_count = jnp.sum(small[:, 0, 1])
    row_factor = lax.rsqrt(squares / model_width + 1e-05).reshape(all_rows)

    turned = lax.ppermute(
        hidden,
        ("dp", "vocab"),
        [
            (g * parts + v, (v // slice_blocks) * parts + g * slice_blocks + v % slice_blocks)
            for g in range(groups)
            for v in range(parts)
        ],
    )
    by_position = ring.gather(turned)
    by_index = by_position[jnp.asarray(ring.place)]
    slice_rows = (
        by_index.reshape(groups, slice_blocks, group_rows, block_width)
        .transpose(0, 2, 1, 3)
        .reshape(all_rows, slice_width)
    )
    gain_slice = lax.dynamic_slice_in_dim(norm_gain, group_index * slice_width, slice_width)
    normed = (slice_rows.astype(F32) * row_factor[:, None] * gain_slice).astype(BF16)

    partial = lax.dot_general(
        normed, head_weight, (((1,), (1,)), ((), ())), preferred_element_type=F32
    )
    partial = partial.reshape(chips, CORES, group_rows, -1)
    sent = lax.dynamic_index_in_dim(partial, 1 - core, 1, keepdims=False)
    partial = lax.dynamic_index_in_dim(partial, core, 1, keepdims=False) + swap_core(sent, groups)
    logits = lax.dynamic_index_in_dim(partial, chip, 0, keepdims=False)
    for d in range(1, chips):
        out = lax.dynamic_index_in_dim(partial, (chip + d) % chips, 0, keepdims=False)
        logits = logits + shift_chip(out, groups, d)

    def part_stats(x):
        top = jnp.max(x, axis=1)
        return top, jnp.sum(jnp.exp(x - top[:, None]), axis=1)

    def scale_of(top, total):
        mine = jnp.stack([top, total])
        others = [mine] + [ring.shift(mine, d) for d in range(1, parts)]
        pairs = jnp.stack(others)
        whole_top = jnp.max(pairs[:, 0], axis=0)
        whole = jnp.sum(pairs[:, 1] * jnp.exp(pairs[:, 0] - whole_top), axis=0)
        return jnp.exp(top - whole_top) / whole

    targets = target_logits.astype(F32)
    target_top, target_total = part_stats(targets)
    target_scale = scale_of(target_top, target_total)
    draft_top, draft_total = part_stats(logits)
    draft_scale = scale_of(draft_top, draft_total)
    row_weight = 1048576.0 * live_rows / valid_count
    draft_probs = jnp.exp(logits - draft_top[:, None]) * draft_scale[:, None]
    target_probs = jnp.exp(targets - target_top[:, None]) * target_scale[:, None]
    logit_grad = (row_weight[:, None] * (draft_probs - target_probs)).astype(BF16)

    dot_part = jnp.sum(logit_grad.astype(F32) * logits, axis=1)
    dots = lax.all_gather(dot_part, ("dp", "vocab")).reshape(groups, parts, group_rows)
    row_dot = jnp.sum(dots, axis=1).reshape(all_rows) / row_factor

    grads = gather_groups(logit_grad, groups).reshape(all_rows, -1)
    normed_grad = jnp.dot(grads, head_weight, preferred_element_type=F32)

    def share_start(position):
        return position % parts * share_rows

    def share(t):
        return lax.dynamic_slice_in_dim(
            normed_grad, share_start(ring.position + t), share_rows, 0
        )

    def whole_row(start):
        entry = start // group_rows
        group = (chip + entry // CORES) % chips * CORES + (core ^ (entry % CORES))
        return group * group_rows + start % group_rows

    normed_share = ring.scatter_sum(share)
    first = whole_row(share_start(ring.position))
    values = lax.dynamic_slice_in_dim(slice_rows, first, share_rows, 0).astype(F32)
    factor = lax.dynamic_slice_in_dim(row_factor, first, share_rows, 0)
    dot = lax.dynamic_slice_in_dim(row_dot, first, share_rows, 0)
    grad_part = (
        factor[:, None] * gain_slice * normed_share
        - values * (factor**3 * dot / model_width)[:, None]
    ).astype(BF16)
    grad_all = ring.gather(grad_part).reshape(all_rows, slice_width)

    row_start = vocab_index * share_rows
    row_group = row_start // group_rows
    entry = (row_group // CORES - chip) % chips * CORES + (row_group % CORES ^ core)
    grad_share = lax.dynamic_slice_in_dim(
        grad_all, entry * group_rows + row_start % group_rows, share_rows, 0
    )
    grad_joining = lax.dot_general(
        grad_all, chosen_all, (((0,), (0,)), ((), ())), preferred_element_type=F32
    )
    return (grad_share, grad_joining)


def solution(mesh):
    placed = (
        P("dp", "vocab"),
        P(),
        P("vocab", "dp"),
        P("dp", "vocab"),
        P("dp"),
        P("dp"),
        P("dp", "vocab"),
    )
    return jax.shard_map(
        body,
        mesh=mesh,
        in_specs=placed,
        out_specs=(P("vocab", "dp"), P("dp", "vocab")),
        check_vma=False,
    )
```

```python
import functools

import jax
import jax.numpy as jnp
from jax import lax
from jax.experimental import pallas as pl
from jax.experimental.pallas import tpu as pltpu
from jax.sharding import PartitionSpec as P

TREE = 64
CORES = 2
LANES = 128
CHUNKS = 2
F32 = jnp.float32
BF16 = jnp.bfloat16


def ring_order(rows, columns):
    if columns == 1 or rows == 1:
        return list(range(rows * columns))
    order = [r * columns for r in range(rows)]
    for step in range(rows):
        r = rows - 1 - step
        line = [r * columns + c for c in range(1, columns)]
        order += line if step % 2 == 0 else line[::-1]
    return order


class Ring:
    def __init__(self, size, columns):
        self.size = size
        self.half = size // 2
        self.order = ring_order(size // columns, columns)
        place = [0] * size
        for position, index in enumerate(self.order):
            place[index] = position
        self.place = place
        self.position = jnp.asarray(place, jnp.int32)[lax.axis_index("vocab")]

    def shift(self, x, step):
        size, order = self.size, self.order
        return lax.ppermute(
            x, "vocab", [(order[p], order[(p + step) % size]) for p in range(size)]
        )

    def partner(self, x, bit):
        return lax.ppermute(x, "vocab", [(v, v ^ bit) for v in range(self.size)])

    def meet(self, x, merge):
        bit = 1
        while bit < self.size:
            x = merge(x, self.partner(x, bit))
            bit *= 2
        return x

    def entry(self, position):
        return (position - self.position + self.half + self.size) % self.size

    def gather(self, block):
        ahead, behind = [block], [block]
        for _ in range(self.half - 1):
            ahead.append(self.shift(ahead[-1], 1))
            behind.append(self.shift(behind[-1], -1))
        cut = block.shape[0] // 2
        far = jnp.concatenate(
            [self.shift(ahead[-1][:cut], 1), self.shift(behind[-1][cut:], -1)], axis=0
        )
        return jnp.stack([far] + ahead[1:][::-1] + [block] + behind[1:])

    def by_position(self, line):
        return jnp.roll(line, self.position - self.half, axis=0)

    def scatter_sum(self, part):
        steps = self.half - 1
        far = part(self.half).astype(BF16)
        cut = far.shape[0] // 2
        got = self.shift(far[:cut], 1).astype(F32)
        ahead = part(steps)
        ahead = jnp.concatenate([ahead[:cut] + got, ahead[cut:]], axis=0)
        got = self.shift(far[cut:], -1).astype(F32)
        behind = part(-steps)
        behind = jnp.concatenate([behind[:cut], behind[cut:] + got], axis=0)
        for step in range(steps - 1, -1, -1):
            got_ahead = self.shift(ahead.astype(BF16), 1).astype(F32)
            got_behind = self.shift(behind.astype(BF16), -1).astype(F32)
            if step > 0:
                ahead = part(step) + got_ahead
                behind = part(-step) + got_behind
        return part(0) + got_ahead + got_behind


class Groups:
    def __init__(self, size):
        self.size = size
        self.chips = size // CORES
        index = lax.axis_index("dp")
        self.chip, self.core = index // CORES, index % CORES
        self.order = [
            (self.chip + d) % self.chips * CORES + (self.core ^ e)
            for e in range(CORES)
            for d in range(self.chips)
        ]

    def entry(self, group):
        return (group % CORES ^ self.core) * self.chips + (
            group // CORES - self.chip + self.chips
        ) % self.chips

    def swap(self, x):
        return lax.ppermute(x, "dp", [(i, i ^ 1) for i in range(self.size)])

    def shift(self, x, step):
        size = self.size
        return lax.ppermute(x, "dp", [(i, (i + CORES * step) % size) for i in range(size)])

    def gather(self, block):
        mine = jnp.stack([block] + [self.shift(block, -d) for d in range(1, self.chips)])
        return jnp.concatenate([mine, self.swap(mine)], axis=0)


def project_kernel(slots, index_ref, blocks_ref, factor_ref, gain_ref, weight_ref, keep_ref, send_ref, normed_ref):
    rows, width = blocks_ref.shape[1:]
    groups = factor_ref.shape[0]
    half = groups // CORES * rows

    @pl.when(pl.program_id(0) == 0)
    def _():
        for g in range(groups):
            factor = factor_ref[g]
            for k in range(slots):
                columns = pl.ds(k * width, width)
                values = blocks_ref[index_ref[g * slots + k]].astype(F32)
                normed_ref[pl.ds(g * rows, rows), columns] = (
                    values * factor * gain_ref[:, columns]
                ).astype(BF16)

    for ref, start in ((keep_ref, 0), (send_ref, half)):
        ref[...] = lax.dot_general(
            normed_ref[pl.ds(start, half), :],
            weight_ref[...],
            (((1,), (1,)), ((), ())),
            preferred_element_type=F32,
        )


def project(index, blocks, factor, gain, weight):
    count, rows, width = blocks.shape
    groups = factor.shape[0]
    vocab, depth = weight.shape
    slots = depth // width
    tile = min(vocab, 256)
    all_rows = groups * rows
    half = all_rows // CORES
    out = jax.ShapeDtypeStruct((half, vocab), F32)
    whole = lambda shape: pl.BlockSpec(shape, lambda n, index: (0,) * len(shape))
    return pl.pallas_call(
        functools.partial(project_kernel, slots),
        grid_spec=pltpu.PrefetchScalarGridSpec(
            num_scalar_prefetch=1,
            grid=(vocab // tile,),
            in_specs=[
                whole(blocks.shape),
                whole(factor.shape),
                whole(gain.shape),
                pl.BlockSpec((tile, depth), lambda n, index: (n, 0)),
            ],
            out_specs=[pl.BlockSpec((half, tile), lambda n, index: (0, n))] * 2,
            scratch_shapes=[pltpu.VMEM((all_rows, depth), BF16)],
        ),
        out_shape=[out, out],
        compiler_params=pltpu.CompilerParams(vmem_limit_bytes=24 * 2**20),
        cost_estimate=pl.CostEstimate(
            flops=2 * all_rows * depth * vocab,
            bytes_accessed=vocab * depth * 2 + all_rows * (depth * 2 + vocab * 4),
            transcendentals=0,
        ),
    )(index, blocks, factor, gain, weight)


def body(hidden, norm_gain, head_weight, target_logits, valid_rows, parents, features):
    groups = Groups(lax.axis_size("dp"))
    parts = lax.axis_size("vocab")
    vocab_index = lax.axis_index("vocab")
    ring = Ring(parts, groups.chips)
    group_rows, block_width = hidden.shape
    chunk_rows = group_rows // CHUNKS
    step_rows = groups.size * chunk_rows
    piece_rows = step_rows // parts
    model_width = block_width * parts
    slots = parts // groups.size
    slice_width = block_width * slots
    vocab_width = target_logits.shape[1]

    def chunk(x, h):
        return x[h * chunk_rows : (h + 1) * chunk_rows]

    def column_owner(g, v):
        far = g % CORES * groups.chips + g // CORES
        return v // slots * parts + far * slots + v % slots

    turn = [
        (g * parts + v, column_owner(g, v)) for g in range(groups.size) for v in range(parts)
    ]
    turned = [lax.ppermute(chunk(hidden, h), ("dp", "vocab"), turn) for h in range(CHUNKS)]

    live_rows = (valid_rows == 1).astype(F32)
    targets = target_logits.astype(F32)
    target_top = jnp.max(targets, axis=1)
    target_total = jnp.sum(jnp.exp(targets - target_top[:, None]), axis=1)
    square_part = jnp.sum(jnp.square(hidden.astype(F32)), axis=1)

    def merge_totals(a, b):
        top = jnp.maximum(a[-2], b[-2])
        total = a[-1] * jnp.exp(a[-2] - top) + b[-1] * jnp.exp(b[-2] - top)
        return jnp.concatenate([a[:-2] + b[:-2], jnp.stack([top, total])])

    met = ring.meet(jnp.stack([square_part, target_top, target_total]), merge_totals)
    target_scale = jnp.exp(target_top - met[1]) / met[2]
    both = groups.gather(jnp.stack([met[0], live_rows]))
    valid_count = jnp.sum(both[:, 1])
    row_factor = lax.rsqrt(both[:, 0] / model_width + 1e-05)

    tree_rows = jnp.arange(group_rows, dtype=jnp.int32) // TREE * TREE + parents
    chosen = features.at[tree_rows].get(mode="promise_in_bounds")
    chosen = groups.gather(chosen.reshape(CHUNKS, chunk_rows, -1))
    chosen = chosen.transpose(1, 0, 2, 3).reshape(CHUNKS * step_rows, -1)

    gain = lax.dynamic_slice_in_dim(
        norm_gain, lax.axis_index("dp") * slice_width, slice_width
    ).reshape(1, slice_width)

    def slot_entry(group, k):
        far = group % CORES * groups.chips + group // CORES
        place = jnp.asarray(ring.place, jnp.int32)
        return ring.entry(place[far * slots + k])

    index = jnp.stack([slot_entry(g, k) for g in groups.order for k in range(slots)])

    row_weight = 1048576.0 * live_rows / valid_count
    lane = lax.broadcasted_iota(jnp.int32, (chunk_rows, LANES), 1)

    grads = []
    for h in range(CHUNKS):
        blocks = ring.gather(turned[h])
        factor = row_factor[:, h * chunk_rows : (h + 1) * chunk_rows]
        keep, send = project(index, blocks, factor[:, :, None], gain, head_weight)
        summed = (keep + groups.swap(send)).reshape(groups.chips, chunk_rows, vocab_width)
        logits = summed[0]
        for d in range(1, groups.chips):
            logits = logits + groups.shift(summed[d], d)

        top = jnp.max(logits, axis=1)
        total = jnp.sum(jnp.exp(logits - top[:, None]), axis=1)
        met = ring.meet(jnp.stack([top, total]), merge_totals)
        scale = jnp.exp(top - met[0]) / met[1]
        draft_probs = jnp.exp(logits - top[:, None]) * scale[:, None]
        target_probs = (
            jnp.exp(chunk(targets, h) - chunk(target_top, h)[:, None])
            * chunk(target_scale, h)[:, None]
        )
        logit_grad = chunk(row_weight, h)[:, None] * (draft_probs - target_probs)
        logit_grad = lax.reduce_precision(logit_grad, 8, 7)
        dot_part = jnp.sum(logit_grad * logits, axis=1)
        dot_high = lax.reduce_precision(dot_part, 8, 7)
        dot_low = dot_part - dot_high
        lanes = jnp.where(lane == 2 * ring.position, dot_high[:, None], 0.0) + jnp.where(
            lane == 2 * ring.position + 1, dot_low[:, None], 0.0
        )
        message = jnp.concatenate([logit_grad.astype(BF16), lanes.astype(BF16)], axis=1)
        everyone = groups.gather(message).reshape(step_rows, vocab_width + LANES)
        normed_grad = jnp.dot(
            everyone[:, :vocab_width], head_weight, preferred_element_type=F32
        )
        dots = everyone[:, vocab_width:]

        def part(t):
            start = (ring.position + t + parts) % parts * piece_rows
            return jnp.concatenate(
                [
                    lax.dynamic_slice_in_dim(normed_grad, start, piece_rows, 0),
                    lax.dynamic_slice_in_dim(dots, start, piece_rows, 0).astype(F32),
                ],
                axis=1,
            )

        piece = ring.scatter_sum(part)
        start = ring.position * piece_rows
        group, first = start // chunk_rows, start % chunk_rows
        values = jnp.concatenate(
            [
                lax.dynamic_slice(
                    blocks, (index[group * slots + k], first, 0), (1, piece_rows, block_width)
                )[0]
                for k in range(slots)
            ],
            axis=1,
        ).astype(F32)
        piece_factor = lax.dynamic_slice(factor, (group, first), (1, piece_rows))[0]
        row_dot = jnp.sum(piece[:, slice_width:], axis=1) / piece_factor
        grad_piece = (
            piece_factor[:, None] * gain * piece[:, :slice_width]
            - values * (piece_factor**3 * row_dot / model_width)[:, None]
        ).astype(BF16)
        line = ring.gather(grad_piece)
        grads.append(ring.by_position(line).reshape(step_rows, slice_width))

    grad_all = jnp.concatenate(grads, axis=0)
    grad_joining = lax.dot_general(
        grad_all, chosen, (((0,), (0,)), ((), ())), preferred_element_type=F32
    )
    share_rows = group_rows // slots
    first = vocab_index * share_rows
    entry = groups.entry(first // group_rows)
    first = first % group_rows
    start = first // chunk_rows * step_rows + entry * chunk_rows + first % chunk_rows
    grad_share = lax.dynamic_slice_in_dim(grad_all, start, share_rows, 0)
    return (grad_share, grad_joining)


def solution(mesh):
    placed = (
        P("dp", "vocab"),
        P(),
        P("vocab", "dp"),
        P("dp", "vocab"),
        P("dp"),
        P("dp"),
        P("dp", "vocab"),
    )
    return jax.shard_map(
        body,
        mesh=mesh,
        in_specs=placed,
        out_specs=(P("vocab", "dp"), P("dp", "vocab")),
        check_vma=False,
    )
```

```python
import functools

import jax
import jax.numpy as jnp
from jax import lax
from jax.experimental import pallas as pl
from jax.experimental.pallas import tpu as pltpu
from jax.sharding import PartitionSpec as P

TREE = 64
CORES = 2
LANES = 128
CHUNKS = 2
F32 = jnp.float32
BF16 = jnp.bfloat16


def ring_order(rows, columns):
    if columns == 1 or rows == 1:
        return list(range(rows * columns))
    order = [r * columns for r in range(rows)]
    for step in range(rows):
        r = rows - 1 - step
        line = [r * columns + c for c in range(1, columns)]
        order += line if step % 2 == 0 else line[::-1]
    return order


class Ring:
    def __init__(self, size, columns):
        self.size = size
        self.half = size // 2
        self.order = ring_order(size // columns, columns)
        place = [0] * size
        for position, index in enumerate(self.order):
            place[index] = position
        self.place = place
        self.position = jnp.asarray(place, jnp.int32)[lax.axis_index("vocab")]

    def shift(self, x, step):
        size, order = self.size, self.order
        return lax.ppermute(
            x, "vocab", [(order[p], order[(p + step) % size]) for p in range(size)]
        )

    def partner(self, x, bit):
        return lax.ppermute(x, "vocab", [(v, v ^ bit) for v in range(self.size)])

    def meet(self, x, merge):
        bit = 1
        while bit < self.size:
            x = merge(x, self.partner(x, bit))
            bit *= 2
        return x

    def entry(self, position):
        return (position - self.position + self.half + self.size) % self.size

    def gather(self, block, waits=None):
        ahead, behind = [block], [block]
        for step in range(self.half - 1):
            if waits and step in waits:
                others = waits[step]()
                ahead[-1], behind[-1] = after(ahead[-1], others), after(behind[-1], others)
            ahead.append(self.shift(ahead[-1], 1))
            behind.append(self.shift(behind[-1], -1))
        cut = block.shape[0] // 2
        far = jnp.concatenate(
            [self.shift(ahead[-1][:cut], 1), self.shift(behind[-1][cut:], -1)], axis=0
        )
        return jnp.stack([far] + ahead[1:][::-1] + [block] + behind[1:])

    def by_position(self, line):
        return jnp.roll(line, self.position - self.half, axis=0)

    def scatter_sum(self, part):
        steps = self.half - 1
        far = part(self.half).astype(BF16)
        cut = far.shape[0] // 2
        got = self.shift(far[:cut], 1).astype(F32)
        ahead = part(steps)
        ahead = jnp.concatenate([ahead[:cut] + got, ahead[cut:]], axis=0)
        got = self.shift(far[cut:], -1).astype(F32)
        behind = part(-steps)
        behind = jnp.concatenate([behind[:cut], behind[cut:] + got], axis=0)
        for step in range(steps - 1, -1, -1):
            got_ahead = self.shift(ahead.astype(BF16), 1).astype(F32)
            got_behind = self.shift(behind.astype(BF16), -1).astype(F32)
            if step > 0:
                ahead = part(step) + got_ahead
                behind = part(-step) + got_behind
        return part(0) + got_ahead + got_behind


class Groups:
    def __init__(self, size):
        self.size = size
        self.chips = size // CORES
        index = lax.axis_index("dp")
        self.chip, self.core = index // CORES, index % CORES
        self.order = [
            (self.chip + d) % self.chips * CORES + (self.core ^ e)
            for e in range(CORES)
            for d in range(self.chips)
        ]

    def entry(self, group):
        return (group % CORES ^ self.core) * self.chips + (
            group // CORES - self.chip + self.chips
        ) % self.chips

    def swap(self, x):
        return lax.ppermute(x, "dp", [(i, i ^ 1) for i in range(self.size)])

    def shift(self, x, step):
        size = self.size
        return lax.ppermute(x, "dp", [(i, (i + CORES * step) % size) for i in range(size)])

    def gather(self, block):
        mine = jnp.stack([block] + [self.shift(block, -d) for d in range(1, self.chips)])
        return jnp.concatenate([mine, self.swap(mine)], axis=0)


def normalise_kernel(slots, index_ref, blocks_ref, factor_ref, gain_ref, normed_ref):
    rows, width = blocks_ref.shape[1:]
    for g in range(factor_ref.shape[0]):
        factor = factor_ref[g]
        for k in range(slots):
            columns = pl.ds(k * width, width)
            values = blocks_ref[index_ref[g * slots + k]].astype(F32)
            normed_ref[pl.ds(g * rows, rows), columns] = (
                values * factor * gain_ref[:, columns]
            ).astype(BF16)


def normalise(index, blocks, factor, gain):
    rows = blocks.shape[1]
    groups = factor.shape[0]
    depth = gain.shape[1]
    whole = pl.BlockSpec(memory_space=pltpu.VMEM)
    return pl.pallas_call(
        functools.partial(normalise_kernel, depth // blocks.shape[2]),
        in_specs=[pl.BlockSpec(memory_space=pltpu.SMEM), whole, whole, whole],
        out_specs=whole,
        out_shape=jax.ShapeDtypeStruct((groups * rows, depth), BF16),
        compiler_params=pltpu.CompilerParams(vmem_limit_bytes=12 * 2**20),
        cost_estimate=pl.CostEstimate(
            flops=3 * groups * rows * depth,
            bytes_accessed=4 * groups * rows * depth,
            transcendentals=0,
        ),
    )(index, blocks, factor, gain)


def after(x, *others):
    return lax.optimization_barrier((x, others))[0]


def body(hidden, norm_gain, head_weight, target_logits, valid_rows, parents, features):
    groups = Groups(lax.axis_size("dp"))
    parts = lax.axis_size("vocab")
    vocab_index = lax.axis_index("vocab")
    ring = Ring(parts, groups.chips)
    group_rows, block_width = hidden.shape
    chunk_rows = group_rows // CHUNKS
    step_rows = groups.size * chunk_rows
    piece_rows = step_rows // parts
    model_width = block_width * parts
    slots = parts // groups.size
    slice_width = block_width * slots
    vocab_width = target_logits.shape[1]

    def chunk(x, h):
        return x[h * chunk_rows : (h + 1) * chunk_rows]

    def column_owner(g, v):
        far = g % CORES * groups.chips + g // CORES
        return v // slots * parts + far * slots + v % slots

    turn = [
        (g * parts + v, column_owner(g, v)) for g in range(groups.size) for v in range(parts)
    ]
    turned = [lax.ppermute(chunk(hidden, h), ("dp", "vocab"), turn) for h in range(CHUNKS)]

    live_rows = (valid_rows == 1).astype(F32)
    targets = target_logits.astype(F32)
    target_top = jnp.max(targets, axis=1)
    target_total = jnp.sum(jnp.exp(targets - target_top[:, None]), axis=1)
    square_part = jnp.sum(jnp.square(hidden.astype(F32)), axis=1)

    def merge_totals(a, b):
        top = jnp.maximum(a[-2], b[-2])
        total = a[-1] * jnp.exp(a[-2] - top) + b[-1] * jnp.exp(b[-2] - top)
        return jnp.concatenate([a[:-2] + b[:-2], jnp.stack([top, total])])

    met = ring.meet(jnp.stack([square_part, target_top, target_total]), merge_totals)
    target_scale = jnp.exp(target_top - met[1]) / met[2]
    both = groups.gather(jnp.stack([met[0], live_rows]))
    valid_count = jnp.sum(both[:, 1])
    row_factor = lax.rsqrt(both[:, 0] / model_width + 1e-05)

    tree_rows = jnp.arange(group_rows, dtype=jnp.int32) // TREE * TREE + parents
    chosen = features.at[tree_rows].get(mode="promise_in_bounds")
    chosen = groups.gather(chosen.reshape(CHUNKS, chunk_rows, -1))
    chosen = chosen.transpose(1, 0, 2, 3).reshape(CHUNKS * step_rows, -1)

    gain = lax.dynamic_slice_in_dim(
        norm_gain, lax.axis_index("dp") * slice_width, slice_width
    ).reshape(1, slice_width)

    def slot_entry(group, k):
        far = group % CORES * groups.chips + group // CORES
        place = jnp.asarray(ring.place, jnp.int32)
        return ring.entry(place[far * slots + k])

    index = jnp.stack([slot_entry(g, k) for g in groups.order for k in range(slots)])

    row_weight = 1048576.0 * live_rows / valid_count
    lane = lax.broadcasted_iota(jnp.int32, (chunk_rows, LANES), 1)

    def group_logits(h, blocks):
        factor = row_factor[:, h * chunk_rows : (h + 1) * chunk_rows]
        normed = normalise(index, blocks, factor[:, :, None], gain)
        own = lax.dot_general(
            normed, head_weight, (((1,), (1,)), ((), ())), preferred_element_type=F32
        )
        yield own
        half = step_rows // CORES
        summed = own[:half] + groups.swap(own[half:])
        yield summed
        summed = summed.reshape(groups.chips, chunk_rows, vocab_width)
        logits = summed[0]
        for d in range(1, groups.chips):
            logits = logits + groups.shift(summed[d], d)
        yield logits

    gathered, logits_of = [], []
    for h in range(CHUNKS):
        waits = None
        if h > 0:
            stages = group_logits(h - 1, gathered[-1])
            waits = {
                0: lambda: (gathered[-1],),
                1: lambda: (next(stages),),
                2: lambda: (next(stages),),
            }
        gathered.append(ring.gather(turned[h], waits))
        if h > 0:
            logits_of.append(list(stages)[-1])
    logits_of.append(list(group_logits(CHUNKS - 1, gathered[-1]))[-1])

    grads = []
    for h in range(CHUNKS):
        blocks, logits = gathered[h], logits_of[h]
        factor = row_factor[:, h * chunk_rows : (h + 1) * chunk_rows]
        top = jnp.max(logits, axis=1)
        total = jnp.sum(jnp.exp(logits - top[:, None]), axis=1)
        met = ring.meet(jnp.stack([top, total]), merge_totals)
        scale = jnp.exp(top - met[0]) / met[1]
        draft_probs = jnp.exp(logits - top[:, None]) * scale[:, None]
        target_probs = (
            jnp.exp(chunk(targets, h) - chunk(target_top, h)[:, None])
            * chunk(target_scale, h)[:, None]
        )
        logit_grad = chunk(row_weight, h)[:, None] * (draft_probs - target_probs)
        logit_grad = lax.reduce_precision(logit_grad, 8, 7)
        dot_part = jnp.sum(logit_grad * logits, axis=1)
        dot_high = lax.reduce_precision(dot_part, 8, 7)
        dot_low = dot_part - dot_high
        lanes = jnp.where(lane == 2 * ring.position, dot_high[:, None], 0.0) + jnp.where(
            lane == 2 * ring.position + 1, dot_low[:, None], 0.0
        )
        message = jnp.concatenate([logit_grad.astype(BF16), lanes.astype(BF16)], axis=1)
        everyone = groups.gather(message).reshape(step_rows, vocab_width + LANES)
        normed_grad = jnp.dot(
            everyone[:, :vocab_width], head_weight, preferred_element_type=F32
        )
        dots = everyone[:, vocab_width:]

        def part(t):
            start = (ring.position + t + parts) % parts * piece_rows
            return jnp.concatenate(
                [
                    lax.dynamic_slice_in_dim(normed_grad, start, piece_rows, 0),
                    lax.dynamic_slice_in_dim(dots, start, piece_rows, 0).astype(F32),
                ],
                axis=1,
            )

        piece = ring.scatter_sum(part)
        start = ring.position * piece_rows
        group, first = start // chunk_rows, start % chunk_rows
        values = jnp.concatenate(
            [
                lax.dynamic_slice(
                    blocks, (index[group * slots + k], first, 0), (1, piece_rows, block_width)
                )[0]
                for k in range(slots)
            ],
            axis=1,
        ).astype(F32)
        piece_factor = lax.dynamic_slice(factor, (group, first), (1, piece_rows))[0]
        row_dot = jnp.sum(piece[:, slice_width:], axis=1) / piece_factor
        grad_piece = (
            piece_factor[:, None] * gain * piece[:, :slice_width]
            - values * (piece_factor**3 * row_dot / model_width)[:, None]
        ).astype(BF16)
        line = ring.gather(grad_piece)
        grads.append(ring.by_position(line).reshape(step_rows, slice_width))

    grad_all = jnp.concatenate(grads, axis=0)
    grad_joining = lax.dot_general(
        grad_all, chosen, (((0,), (0,)), ((), ())), preferred_element_type=F32
    )
    share_rows = group_rows // slots
    first = vocab_index * share_rows
    entry = groups.entry(first // group_rows)
    first = first % group_rows
    start = first // chunk_rows * step_rows + entry * chunk_rows + first % chunk_rows
    grad_share = lax.dynamic_slice_in_dim(grad_all, start, share_rows, 0)
    return (grad_share, grad_joining)


def solution(mesh):
    placed = (
        P("dp", "vocab"),
        P(),
        P("vocab", "dp"),
        P("dp", "vocab"),
        P("dp"),
        P("dp"),
        P("dp", "vocab"),
    )
    return jax.shard_map(
        body,
        mesh=mesh,
        in_specs=placed,
        out_specs=(P("vocab", "dp"), P("dp", "vocab")),
        check_vma=False,
    )
```

```python
import functools

import jax
import jax.numpy as jnp
import numpy as np
from jax import lax
from jax.experimental import pallas as pl
from jax.experimental.pallas import tpu as pltpu
from jax.sharding import PartitionSpec as P

TREE = 64
CORES = 2
LANES = 128
CHUNKS = 2
F32 = jnp.float32
BF16 = jnp.bfloat16


def ring_order(rows, columns):
    if columns == 1 or rows == 1:
        return list(range(rows * columns))
    order = [r * columns for r in range(rows)]
    for step in range(rows):
        r = rows - 1 - step
        line = [r * columns + c for c in range(1, columns)]
        order += line if step % 2 == 0 else line[::-1]
    return order


def half_width(x):
    return x.shape[1] // 2 // LANES * LANES


class Ring:
    def __init__(self, size, columns):
        self.size = size
        self.half = size // 2
        self.order = ring_order(size // columns, columns)
        self.place = [0] * size
        for position, index in enumerate(self.order):
            self.place[index] = position

    def shift(self, x, step):
        size, order = self.size, self.order
        return lax.ppermute(
            x, "vocab", [(order[p], order[(p + step) % size]) for p in range(size)]
        )

    def partner(self, x, bit):
        return lax.ppermute(x, "vocab", [(v, v ^ bit) for v in range(self.size)])

    def meet(self, x, merge):
        bit = 1
        while bit < self.size:
            x = merge(x, self.partner(x, bit))
            bit *= 2
        return x

    def gather(self, block, waits=None):
        ahead, behind = [block], [block]
        for step in range(self.half - 1):
            if waits and step in waits:
                others = waits[step]()
                ahead[-1], behind[-1] = after(ahead[-1], others), after(behind[-1], others)
            ahead.append(self.shift(ahead[-1], 1))
            behind.append(self.shift(behind[-1], -1))
        cut = half_width(block)
        far = [self.shift(ahead[-1][:, :cut], 1), self.shift(behind[-1][:, cut:], -1)]
        return far + ahead[1:][::-1] + [block] + behind[1:]

    def sources(self, vocab):
        p = self.place[vocab]
        return [(p + k - self.half) % self.size for k in range(self.size)]

    def scatter_sum(self, part):
        steps = self.half - 1
        far = part(self.half).astype(BF16)
        cut = half_width(far)
        got = self.shift(far[:, :cut], 1).astype(F32)
        ahead = part(steps)
        ahead = jnp.concatenate([ahead[:, :cut] + got, ahead[:, cut:]], axis=1)
        got = self.shift(far[:, cut:], -1).astype(F32)
        behind = part(-steps)
        behind = jnp.concatenate([behind[:, :cut], behind[:, cut:] + got], axis=1)
        for step in range(steps - 1, -1, -1):
            got_ahead = self.shift(ahead.astype(BF16), 1).astype(F32)
            got_behind = self.shift(behind.astype(BF16), -1).astype(F32)
            if step > 0:
                ahead = part(step) + got_ahead
                behind = part(-step) + got_behind
        return part(0) + got_ahead + got_behind


class Groups:
    def __init__(self, size):
        self.size = size
        self.chips = size // CORES

    def entry(self, index, group):
        chip = (group // CORES - index // CORES) % self.chips
        return (group % CORES ^ index % CORES) * self.chips + chip

    def swap(self, x):
        return lax.ppermute(x, "dp", [(i, i ^ 1) for i in range(self.size)])

    def shift(self, x, step):
        size = self.size
        return lax.ppermute(x, "dp", [(i, (i + CORES * step) % size) for i in range(size)])

    def gather(self, block):
        mine = jnp.stack([block] + [self.shift(block, -d) for d in range(1, self.chips)])
        return jnp.concatenate([mine, self.swap(mine)], axis=0)


def place_pieces(refs, put):
    put(0, refs[0], 0)
    put(0, refs[1], refs[0].shape[1])
    for k, ref in enumerate(refs[2:]):
        put(k + 1, ref, 0)


def normalise_kernel(count, index_ref, factor_ref, gain_ref, *refs):
    blocks, (normed_ref, piece_ref, raw_ref) = refs[: count + 1], refs[count + 1 :]
    rows, width = blocks[2].shape
    piece = piece_ref.shape[0]

    def put(k, ref, first):
        start = pl.multiple_of(index_ref[k] * rows, rows)
        column = pl.multiple_of(index_ref[count + k] * width + first, LANES)
        raw_ref[pl.ds(start, rows), pl.ds(column, ref.shape[1])] = ref[...]

    place_pieces(blocks, put)
    for g in range(factor_ref.shape[0]):
        group = pl.ds(g * rows, rows)
        normed_ref[group, :] = (
            raw_ref[group, :].astype(F32) * factor_ref[g] * gain_ref[...]
        ).astype(BF16)
    start = pl.multiple_of(index_ref[2 * count] * piece, piece)
    piece_ref[...] = raw_ref[pl.ds(start, piece), :]


def normalise(index, blocks, factor, gain, piece_rows):
    count = len(blocks) - 1
    rows = blocks[2].shape[0]
    groups = factor.shape[0]
    depth = gain.shape[1]
    whole = pl.BlockSpec(memory_space=pltpu.VMEM)
    return pl.pallas_call(
        functools.partial(normalise_kernel, count),
        in_specs=[pl.BlockSpec(memory_space=pltpu.SMEM)] + [whole] * (count + 3),
        out_specs=[whole, whole],
        out_shape=[
            jax.ShapeDtypeStruct((groups * rows, depth), BF16),
            jax.ShapeDtypeStruct((piece_rows, depth), BF16),
        ],
        scratch_shapes=[pltpu.VMEM((groups * rows, depth), BF16)],
        compiler_params=pltpu.CompilerParams(vmem_limit_bytes=16 * 2**20),
        cost_estimate=pl.CostEstimate(
            flops=3 * groups * rows * depth,
            bytes_accessed=4 * groups * rows * depth,
            transcendentals=0,
        ),
    )(index, factor, gain, *blocks)


def outer_kernel(count, chunks, tile, index_ref, chosen_ref, *refs):
    split = chunks * (count + 1)
    pieces, (out_ref, share_ref, grad_ref) = refs[:split], refs[split:]
    rows = pieces[2].shape[0]
    share = share_ref.shape[0]
    step = pl.program_id(0)

    @pl.when(step == 0)
    def _():
        for h in range(chunks):

            def put(k, ref, first):
                start = pl.multiple_of((h * count + index_ref[k]) * rows, rows)
                grad_ref[pl.ds(start, rows), pl.ds(first, ref.shape[1])] = ref[...]

            place_pieces(pieces[h * (count + 1) : (h + 1) * (count + 1)], put)
        start = pl.multiple_of(index_ref[count] * share, share)
        share_ref[...] = grad_ref[pl.ds(start, share), :]

    columns = pl.ds(pl.multiple_of(step * tile, tile), tile)
    out_ref[...] = lax.dot_general(
        grad_ref[:, columns], chosen_ref[...], (((0,), (0,)), ((), ())), preferred_element_type=F32
    )


def outer(index, chosen, chunks, share_rows):
    count = len(chunks[0]) - 1
    depth = chunks[0][2].shape[1]
    all_rows, joined = chosen.shape
    tile = min(depth, 256)
    whole = pl.BlockSpec(memory_space=pltpu.VMEM)
    return pl.pallas_call(
        functools.partial(outer_kernel, count, len(chunks), tile),
        grid=(depth // tile,),
        in_specs=[pl.BlockSpec(memory_space=pltpu.SMEM), whole]
        + [whole] * (len(chunks) * (count + 1)),
        out_specs=[
            pl.BlockSpec((tile, joined), lambda n: (n, 0)),
            pl.BlockSpec((share_rows, depth), lambda n: (0, 0)),
        ],
        out_shape=[
            jax.ShapeDtypeStruct((depth, joined), F32),
            jax.ShapeDtypeStruct((share_rows, depth), BF16),
        ],
        scratch_shapes=[pltpu.VMEM((all_rows, depth), BF16)],
        compiler_params=pltpu.CompilerParams(vmem_limit_bytes=40 * 2**20),
        cost_estimate=pl.CostEstimate(
            flops=2 * all_rows * depth * joined,
            bytes_accessed=4 * depth * joined + 2 * all_rows * (depth + joined),
            transcendentals=0,
        ),
    )(index, chosen, *[x for pieces in chunks for x in pieces])


def device_table(groups, ring, slots, widths):
    group_rows, chunk_rows, piece_rows, slice_width = widths
    parts = ring.size
    step_rows = piece_rows * parts
    share_rows = group_rows // slots
    rows = []
    for g in range(groups.size):
        for v in range(parts):
            p = ring.place[v]
            sources = ring.sources(v)
            held = [ring.order[q] for q in sources]
            group = [(i // slots % groups.chips) * CORES + i // slots // groups.chips for i in held]
            row = [groups.entry(g, i) for i in group] + [i % slots for i in held] + [p]
            row += sources
            entry = groups.entry(g, v * share_rows // group_rows)
            first = v * share_rows % group_rows
            start = first // chunk_rows * step_rows + entry * chunk_rows + first % chunk_rows
            row += [start // share_rows]
            row += [(p + t) % parts * piece_rows for t in range(parts)]
            row += [
                g * slice_width,
                p * piece_rows // chunk_rows,
                p * piece_rows % chunk_rows,
                2 * p,
            ]
            rows.append(row)
    return np.asarray(rows, np.int32).reshape(groups.size, parts, -1)


def after(x, *others):
    return lax.optimization_barrier((x, others))[0]


def body(hidden, norm_gain, head_weight, target_logits, valid_rows, parents, features):
    groups = Groups(lax.axis_size("dp"))
    parts = lax.axis_size("vocab")
    ring = Ring(parts, groups.chips)
    group_rows, block_width = hidden.shape
    chunk_rows = group_rows // CHUNKS
    step_rows = groups.size * chunk_rows
    piece_rows = step_rows // parts
    model_width = block_width * parts
    slots = parts // groups.size
    slice_width = block_width * slots
    vocab_width = target_logits.shape[1]

    table = device_table(
        groups, ring, slots, (group_rows, chunk_rows, piece_rows, slice_width)
    )
    table = lax.dynamic_slice(
        jnp.asarray(table),
        (lax.axis_index("dp"), lax.axis_index("vocab"), 0),
        (1, 1, table.shape[2]),
    ).reshape(-1)
    place_index = table[: 2 * parts + 1]
    piece_index = table[2 * parts + 1 : 3 * parts + 2]
    starts = table[3 * parts + 2 :].astype(jnp.uint32)
    gain_start, own_entry, own_first, own_lane = [starts[parts + k] for k in range(4)]

    def chunk(x, h):
        return x[h * chunk_rows : (h + 1) * chunk_rows]

    def column_owner(g, v):
        far = g % CORES * groups.chips + g // CORES
        return v // slots * parts + far * slots + v % slots

    turn = [
        (g * parts + v, column_owner(g, v)) for g in range(groups.size) for v in range(parts)
    ]
    turned = [lax.ppermute(chunk(hidden, h), ("dp", "vocab"), turn) for h in range(CHUNKS)]

    live_rows = (valid_rows == 1).astype(F32)
    targets = target_logits.astype(F32)
    target_top = jnp.max(targets, axis=1)
    target_total = jnp.sum(jnp.exp(targets - target_top[:, None]), axis=1)
    square_part = jnp.sum(jnp.square(hidden.astype(F32)), axis=1)

    def merge_totals(a, b):
        top = jnp.maximum(a[-2], b[-2])
        total = a[-1] * jnp.exp(a[-2] - top) + b[-1] * jnp.exp(b[-2] - top)
        return jnp.concatenate([a[:-2] + b[:-2], jnp.stack([top, total])])

    met = ring.meet(jnp.stack([square_part, target_top, target_total]), merge_totals)
    target_scale = jnp.exp(target_top - met[1]) / met[2]
    both = groups.gather(jnp.stack([met[0], live_rows]))
    valid_count = jnp.sum(both[:, 1])
    row_factor = lax.rsqrt(both[:, 0] / model_width + 1e-05)

    tree_rows = jnp.arange(group_rows, dtype=jnp.int32) // TREE * TREE + parents
    own_chosen = features.at[tree_rows].get(mode="promise_in_bounds")

    gain = lax.dynamic_slice(norm_gain, (gain_start,), (slice_width,)).reshape(1, slice_width)
    row_weight = 1048576.0 * live_rows / valid_count
    lane = lax.broadcasted_iota(jnp.uint32, (chunk_rows, LANES), 1)

    def group_logits(h, blocks):
        factor = row_factor[:, h * chunk_rows : (h + 1) * chunk_rows]
        normed, piece = normalise(place_index, blocks, factor[:, :, None], gain, piece_rows)
        pieces.append(piece)
        own = lax.dot_general(
            normed, head_weight, (((1,), (1,)), ((), ())), preferred_element_type=F32
        )
        yield own
        half = step_rows // CORES
        summed = own[:half] + groups.swap(own[half:])
        yield summed
        summed = summed.reshape(groups.chips, chunk_rows, vocab_width)
        logits = summed[0]
        for d in range(1, groups.chips):
            logits = logits + groups.shift(summed[d], d)
        yield logits

    gathered, logits_of, pieces = [], [], []
    for h in range(CHUNKS):
        waits = None
        if h > 0:
            stages = group_logits(h - 1, gathered[-1])
            waits = {
                0: lambda: (gathered[-1],),
                1: lambda: (next(stages),),
                2: lambda: (next(stages),),
            }
        gathered.append(ring.gather(turned[h], waits))
        if h > 0:
            logits_of.append(list(stages)[-1])
    logits_of.append(list(group_logits(CHUNKS - 1, gathered[-1]))[-1])

    grads = []
    for h in range(CHUNKS):
        logits = logits_of[h]
        factor = row_factor[:, h * chunk_rows : (h + 1) * chunk_rows]
        top = jnp.max(logits, axis=1)
        total = jnp.sum(jnp.exp(logits - top[:, None]), axis=1)
        met = ring.meet(jnp.stack([top, total]), merge_totals)
        scale = jnp.exp(top - met[0]) / met[1]
        draft_probs = jnp.exp(logits - top[:, None]) * scale[:, None]
        target_probs = (
            jnp.exp(chunk(targets, h) - chunk(target_top, h)[:, None])
            * chunk(target_scale, h)[:, None]
        )
        logit_grad = chunk(row_weight, h)[:, None] * (draft_probs - target_probs)
        logit_grad = lax.reduce_precision(logit_grad, 8, 7)
        dot_part = jnp.sum(logit_grad * logits, axis=1)
        dot_high = lax.reduce_precision(dot_part, 8, 7)
        dot_low = dot_part - dot_high
        lanes = jnp.where(lane == own_lane, dot_high[:, None], 0.0) + jnp.where(
            lane == own_lane + 1, dot_low[:, None], 0.0
        )
        message = jnp.concatenate([logit_grad.astype(BF16), lanes.astype(BF16)], axis=1)
        everyone = groups.gather(message).reshape(step_rows, vocab_width + LANES)
        if h == CHUNKS - 1:
            chosen = groups.gather(after(own_chosen, everyone).reshape(CHUNKS, chunk_rows, -1))
            chosen = chosen.transpose(1, 0, 2, 3).reshape(CHUNKS * step_rows, -1)
        normed_grad = jnp.dot(
            everyone[:, :vocab_width], head_weight, preferred_element_type=F32
        )
        dots = everyone[:, vocab_width:]

        def part(t):
            start = (starts[t % parts], jnp.uint32(0))
            return jnp.concatenate(
                [
                    lax.dynamic_slice(normed_grad, start, (piece_rows, slice_width)),
                    lax.dynamic_slice(dots, start, (piece_rows, LANES)).astype(F32),
                ],
                axis=1,
            )

        summed = ring.scatter_sum(part)
        own_factor = lax.dynamic_slice(factor, (own_entry, own_first), (1, piece_rows))[0]
        row_dot = jnp.sum(summed[:, slice_width:], axis=1) / own_factor
        grad_piece = (
            own_factor[:, None] * gain * summed[:, :slice_width]
            - pieces[h].astype(F32) * (own_factor**3 * row_dot / model_width)[:, None]
        ).astype(BF16)
        grads.append(ring.gather(grad_piece))

    grad_joining, grad_share = outer(piece_index, chosen, grads, group_rows // slots)
    return (grad_share, grad_joining)


def solution(mesh):
    placed = (
        P("dp", "vocab"),
        P(),
        P("vocab", "dp"),
        P("dp", "vocab"),
        P("dp"),
        P("dp"),
        P("dp", "vocab"),
    )
    return jax.shard_map(
        body,
        mesh=mesh,
        in_specs=placed,
        out_specs=(P("vocab", "dp"), P("dp", "vocab")),
        check_vma=False,
    )
```

```python
import functools

import jax
import jax.numpy as jnp
import numpy as np
from jax import lax
from jax.experimental import pallas as pl
from jax.experimental.pallas import tpu as pltpu
from jax.sharding import PartitionSpec as P

TREE = 64
CORES = 2
LANES = 128
CHUNKS = 2
F32 = jnp.float32
BF16 = jnp.bfloat16


def ring_order(rows, columns):
    if columns == 1 or rows == 1:
        return list(range(rows * columns))
    order = [r * columns for r in range(rows)]
    for step in range(rows):
        r = rows - 1 - step
        line = [r * columns + c for c in range(1, columns)]
        order += line if step % 2 == 0 else line[::-1]
    return order


class Ring:
    def __init__(self, size, columns):
        self.size = size
        self.half = size // 2
        self.order = ring_order(size // columns, columns)
        self.place = [0] * size
        for position, index in enumerate(self.order):
            self.place[index] = position

    def shift(self, x, step):
        size, order = self.size, self.order
        return lax.ppermute(
            x, "vocab", [(order[p], order[(p + step) % size]) for p in range(size)]
        )

    def partner(self, x, bit):
        return lax.ppermute(x, "vocab", [(v, v ^ bit) for v in range(self.size)])

    def meet(self, x, merge, waits=None):
        bit = 1
        while bit < self.size:
            if waits and bit in waits:
                x = after(x, waits[bit]())
            x = merge(x, self.partner(x, bit))
            bit *= 2
        return x

    def reach(self, h):
        return (self.half, self.half - 1) if h % 2 == 0 else (self.half - 1, self.half)

    def gather(self, block, h, waits=None):
        far_ahead, far_behind = self.reach(h)
        ahead, behind = [block], [block]
        for step in range(self.half):
            if waits and step in waits:
                others = waits[step]()
                ahead[-1], behind[-1] = after(ahead[-1], others), after(behind[-1], others)
            if step < far_ahead:
                ahead.append(self.shift(ahead[-1], 1))
            if step < far_behind:
                behind.append(self.shift(behind[-1], -1))
        return ahead[1:][::-1] + [block] + behind[1:]

    def sources(self, vocab, h):
        p, far_ahead = self.place[vocab], self.reach(h)[0]
        return [(p + k - far_ahead) % self.size for k in range(self.size)]

    def scatter_sum(self, part, h):
        far_ahead, far_behind = self.reach(h)
        got_ahead = got_behind = None
        for step in range(self.half, 0, -1):
            if step <= far_ahead:
                ahead = part(step) if got_ahead is None else part(step) + got_ahead
                got_ahead = self.shift(ahead.astype(BF16), 1).astype(F32)
            if step <= far_behind:
                behind = part(-step) if got_behind is None else part(-step) + got_behind
                got_behind = self.shift(behind.astype(BF16), -1).astype(F32)
        return part(0) + got_ahead + got_behind


class Groups:
    def __init__(self, size):
        self.size = size
        self.chips = size // CORES

    def entry(self, index, group):
        chip = (group // CORES - index // CORES) % self.chips
        return (group % CORES ^ index % CORES) * self.chips + chip

    def swap(self, x):
        return lax.ppermute(x, "dp", [(i, i ^ 1) for i in range(self.size)])

    def shift(self, x, step):
        size = self.size
        return lax.ppermute(x, "dp", [(i, (i + CORES * step) % size) for i in range(size)])

    def gather_halves(self, block):
        mine = jnp.stack([block] + [self.shift(block, -d) for d in range(1, self.chips)])
        return mine, self.swap(mine)

    def gather(self, block):
        return jnp.concatenate(self.gather_halves(block), axis=0)


VMEM = pl.BlockSpec(memory_space=pltpu.VMEM)
SMEM = pl.BlockSpec(memory_space=pltpu.SMEM)


def transpose_into(out_ref, ref):
    tile = min(ref.shape[1], 256)
    for start in range(0, ref.shape[1], tile):
        block = ref[:, pl.ds(start, tile)].astype(F32)
        out_ref[pl.ds(start, tile), :] = block.T.astype(BF16)


def project_kernel(count, index_ref, factor_ref, gain_ref, weight_ref, *refs):
    blocks = refs[:count]
    keep_ref, send_ref, piece_ref, raw_ref, normed_ref, turned_ref = refs[count:]
    rows, width = blocks[0].shape
    piece = piece_ref.shape[0]
    half = keep_ref.shape[0]

    @pl.when(pl.program_id(0) == 0)
    def _():
        for k, ref in enumerate(blocks):
            start = pl.multiple_of(index_ref[k] * rows, rows)
            column = pl.multiple_of(index_ref[count + k] * width, width)
            raw_ref[pl.ds(start, rows), pl.ds(column, width)] = ref[...]
        for g in range(factor_ref.shape[0]):
            group = pl.ds(g * rows, rows)
            normed_ref[group, :] = (
                raw_ref[group, :].astype(F32) * factor_ref[g] * gain_ref[...]
            ).astype(BF16)
        transpose_into(turned_ref, normed_ref)
        start = pl.multiple_of(index_ref[2 * count] * piece, piece)
        piece_ref[...] = raw_ref[pl.ds(start, piece), :]

    logits = jnp.dot(weight_ref[...], turned_ref[...], preferred_element_type=F32).T
    keep_ref[...] = logits[:half]
    send_ref[...] = logits[half:]


def project(index, blocks, factor, gain, weight, piece_rows):
    rows = blocks[0].shape[0]
    vocab, depth = weight.shape
    all_rows = factor.shape[0] * rows
    half = all_rows // CORES
    tile = min(vocab, 512)
    out = jax.ShapeDtypeStruct((half, vocab), F32)
    return pl.pallas_call(
        functools.partial(project_kernel, len(blocks)),
        grid=(vocab // tile,),
        in_specs=[SMEM, VMEM, VMEM, pl.BlockSpec((tile, depth), lambda n: (n, 0))]
        + [VMEM] * len(blocks),
        out_specs=[pl.BlockSpec((half, tile), lambda n: (0, n))] * 2
        + [pl.BlockSpec((piece_rows, depth), lambda n: (0, 0))],
        out_shape=[out, out, jax.ShapeDtypeStruct((piece_rows, depth), BF16)],
        scratch_shapes=[
            pltpu.VMEM((all_rows, depth), BF16),
            pltpu.VMEM((all_rows, depth), BF16),
            pltpu.VMEM((depth, all_rows), BF16),
        ],
        compiler_params=pltpu.CompilerParams(vmem_limit_bytes=24 * 2**20),
        cost_estimate=pl.CostEstimate(
            flops=2 * all_rows * depth * vocab,
            bytes_accessed=2 * vocab * depth + all_rows * (2 * depth + 4 * vocab),
            transcendentals=0,
        ),
    )(index, factor, gain, weight, *blocks)


def back_kernel(piece, index_ref, mine_ref, other_ref, weight_ref, out_ref, grad_ref):
    vocab = weight_ref.shape[0]
    tile = weight_ref.shape[1]
    half = mine_ref.shape[0]
    depth = out_ref.shape[1] - LANES
    step = pl.program_id(0)

    @pl.when(step == 0)
    def _():
        for k in range(2 * half // piece):
            ref, first = (mine_ref, k * piece) if k * piece < half else (other_ref, k * piece - half)
            rows = pl.ds(pl.multiple_of(index_ref[k] * piece, piece), piece)
            grad_ref[rows, :] = ref[pl.ds(first, piece), :vocab]
            out_ref[rows, pl.ds(depth, LANES)] = ref[pl.ds(first, piece), vocab:].astype(F32)

    columns = pl.ds(pl.multiple_of(step * tile, tile), tile)
    out_ref[:, columns] = jnp.dot(grad_ref[...], weight_ref[...], preferred_element_type=F32)


def back(index, mine, other, weight, piece_rows):
    vocab, depth = weight.shape
    all_rows = mine.shape[0] + other.shape[0]
    tile = min(depth, 512)
    return pl.pallas_call(
        functools.partial(back_kernel, piece_rows),
        grid=(depth // tile,),
        in_specs=[SMEM, VMEM, VMEM, pl.BlockSpec((vocab, tile), lambda n: (0, n))],
        out_specs=pl.BlockSpec((all_rows, depth + LANES), lambda n: (0, 0)),
        out_shape=jax.ShapeDtypeStruct((all_rows, depth + LANES), F32),
        scratch_shapes=[pltpu.VMEM((all_rows, vocab), BF16)],
        compiler_params=pltpu.CompilerParams(vmem_limit_bytes=24 * 2**20),
        cost_estimate=pl.CostEstimate(
            flops=2 * all_rows * depth * vocab,
            bytes_accessed=2 * vocab * depth + all_rows * (2 * vocab + 4 * depth),
            transcendentals=0,
        ),
    )(index, mine, other, weight)


def outer_kernel(count, index_ref, chosen_ref, *refs):
    pieces, (out_ref, share_ref, grad_ref, turned_ref) = refs[:-4], refs[-4:]
    rows = pieces[0].shape[0]
    share = share_ref.shape[0]

    @pl.when(pl.program_id(0) == 0)
    def _():
        for k, ref in enumerate(pieces):
            start = pl.multiple_of((k // count * count + index_ref[k]) * rows, rows)
            grad_ref[pl.ds(start, rows), :] = ref[...]
        transpose_into(turned_ref, grad_ref)
        start = pl.multiple_of(index_ref[len(pieces)] * share, share)
        share_ref[...] = grad_ref[pl.ds(start, share), :]

    out_ref[...] = jnp.dot(turned_ref[...], chosen_ref[...], preferred_element_type=F32)


def outer(index, chosen, chunks, share_rows):
    depth = chunks[0][0].shape[1]
    all_rows, joined = chosen.shape
    tile = min(joined, 256)
    pieces = [x for chunk in chunks for x in chunk]
    return pl.pallas_call(
        functools.partial(outer_kernel, len(chunks[0])),
        grid=(joined // tile,),
        in_specs=[SMEM, pl.BlockSpec((all_rows, tile), lambda n: (0, n))] + [VMEM] * len(pieces),
        out_specs=[
            pl.BlockSpec((depth, tile), lambda n: (0, n)),
            pl.BlockSpec((share_rows, depth), lambda n: (0, 0)),
        ],
        out_shape=[
            jax.ShapeDtypeStruct((depth, joined), F32),
            jax.ShapeDtypeStruct((share_rows, depth), BF16),
        ],
        scratch_shapes=[
            pltpu.VMEM((all_rows, depth), BF16),
            pltpu.VMEM((depth, all_rows), BF16),
        ],
        compiler_params=pltpu.CompilerParams(vmem_limit_bytes=32 * 2**20),
        cost_estimate=pl.CostEstimate(
            flops=2 * all_rows * depth * joined,
            bytes_accessed=4 * depth * joined + 2 * all_rows * (depth + joined),
            transcendentals=0,
        ),
    )(index, chosen, *pieces)


def device_table(groups, ring, slots, widths):
    group_rows, chunk_rows, piece_rows, slice_width = widths
    parts = ring.size
    step_rows = piece_rows * parts
    share_rows = group_rows // slots
    table = {}

    def add(name, values):
        table.setdefault(name, []).append(values)

    for g in range(groups.size):
        for v in range(parts):
            p = ring.place[v]
            for h in range(CHUNKS):
                held = [ring.order[q] for q in ring.sources(v, h)]
                group = [
                    i // slots % groups.chips * CORES + i // slots // groups.chips for i in held
                ]
                add(f"place{h}", [groups.entry(g, i) for i in group] + [i % slots for i in held] + [p])
            entry = groups.entry(g, v * share_rows // group_rows)
            first = v * share_rows % group_rows
            start = first // chunk_rows * step_rows + entry * chunk_rows + first % chunk_rows
            pieces = [q for h in range(CHUNKS) for q in ring.sources(v, h)]
            add("pieces", pieces + [start // share_rows])
            add("turn", [(k - p) % parts for k in range(parts)])
            start = p * piece_rows
            add("starts", [g * slice_width, start // chunk_rows, start % chunk_rows, 2 * p])
    return {
        name: np.asarray(rows, np.int32).reshape(groups.size, parts, -1)
        for name, rows in table.items()
    }


def after(x, *others):
    return lax.optimization_barrier((x, others))[0]


def body(hidden, norm_gain, head_weight, target_logits, valid_rows, parents, features):
    groups = Groups(lax.axis_size("dp"))
    parts = lax.axis_size("vocab")
    ring = Ring(parts, groups.chips)
    group_rows, block_width = hidden.shape
    chunk_rows = group_rows // CHUNKS
    step_rows = groups.size * chunk_rows
    piece_rows = step_rows // parts
    model_width = block_width * parts
    slots = parts // groups.size
    slice_width = block_width * slots
    vocab_width = target_logits.shape[1]

    table = device_table(
        groups, ring, slots, (group_rows, chunk_rows, piece_rows, slice_width)
    )
    own = lax.dynamic_slice(
        jnp.asarray(np.concatenate(list(table.values()), axis=2)),
        (lax.axis_index("dp"), lax.axis_index("vocab"), 0),
        (1, 1, sum(rows.shape[2] for rows in table.values())),
    ).reshape(-1)
    index, first = {}, 0
    for name, rows in table.items():
        index[name] = own[first : first + rows.shape[2]]
        first += rows.shape[2]
    gain_start, own_entry, own_first, own_lane = [
        index["starts"].astype(jnp.uint32)[k] for k in range(4)
    ]

    def chunk(x, h):
        return x[h * chunk_rows : (h + 1) * chunk_rows]

    def column_owner(g, v):
        far = g % CORES * groups.chips + g // CORES
        return v // slots * parts + far * slots + v % slots

    turn = [
        (g * parts + v, column_owner(g, v)) for g in range(groups.size) for v in range(parts)
    ]
    turned = [lax.ppermute(chunk(hidden, h), ("dp", "vocab"), turn) for h in range(CHUNKS)]

    live_rows = (valid_rows == 1).astype(F32)
    squares = jnp.sum(jnp.square(hidden.astype(F32)), axis=1)[None]
    squares = ring.meet(squares, lambda a, b: a + b, {2: lambda: (turned[0],)})
    both = groups.gather(jnp.concatenate([squares, live_rows[None]]))
    valid_count = jnp.sum(both[:, 1])
    row_factor = lax.rsqrt(both[:, 0] / model_width + 1e-05)

    targets = target_logits.astype(F32)
    target_top = jnp.max(targets, axis=1)
    target_total = jnp.sum(jnp.exp(targets - target_top[:, None]), axis=1)

    def merge_totals(a, b):
        top = jnp.maximum(a[0], b[0])
        total = a[1] * jnp.exp(a[0] - top) + b[1] * jnp.exp(b[0] - top)
        return jnp.stack([top, total])

    tree_rows = jnp.arange(group_rows, dtype=jnp.int32) // TREE * TREE + parents
    own_chosen = features.at[tree_rows].get(mode="promise_in_bounds")

    gain = lax.dynamic_slice(norm_gain, (gain_start,), (slice_width,)).reshape(1, slice_width)
    row_weight = 1048576.0 * live_rows / valid_count
    lane = lax.broadcasted_iota(jnp.uint32, (chunk_rows, LANES), 1)

    def group_logits(h, blocks):
        factor = row_factor[:, h * chunk_rows : (h + 1) * chunk_rows]
        keep, send, piece = project(
            index[f"place{h}"], blocks, factor[:, :, None], gain, head_weight, piece_rows
        )
        pieces.append(piece)
        yield keep
        summed = keep + groups.swap(send)
        yield summed
        summed = summed.reshape(groups.chips, chunk_rows, vocab_width)
        logits = summed[0]
        for d in range(1, groups.chips):
            logits = logits + groups.shift(summed[d], d)
        yield logits

    gathered, logits_of, pieces = [], [], []
    for h in range(CHUNKS):
        waits = {1: lambda: tuple(turned[1:])}
        if h > 0:
            stages = group_logits(h - 1, gathered[-1])
            waits = {
                0: lambda: (gathered[-1],),
                1: lambda: (next(stages),),
                2: lambda: (next(stages),),
                3: lambda: (logits_of.append(next(stages)), logits_of[-1])[1:],
            }
        gathered.append(ring.gather(turned[h], h, waits))
    logits_of.append(list(group_logits(CHUNKS - 1, gathered[-1]))[-1])

    grads = []
    for h in range(CHUNKS):
        logits = logits_of[h]
        factor = row_factor[:, h * chunk_rows : (h + 1) * chunk_rows]
        top = jnp.max(logits, axis=1)
        total = jnp.sum(jnp.exp(logits - top[:, None]), axis=1)
        mine = jnp.stack([top, total])
        if h == 0:
            mine = jnp.concatenate([mine, jnp.stack([target_top, target_total])], axis=1)
        met = ring.meet(mine, merge_totals)
        scale = jnp.exp(top - met[0, :chunk_rows]) / met[1, :chunk_rows]
        if h == 0:
            target_scale = jnp.exp(target_top - met[0, chunk_rows:]) / met[1, chunk_rows:]
        draft_probs = jnp.exp(logits - top[:, None]) * scale[:, None]
        target_probs = (
            jnp.exp(chunk(targets, h) - chunk(target_top, h)[:, None])
            * chunk(target_scale, h)[:, None]
        )
        logit_grad = chunk(row_weight, h)[:, None] * (draft_probs - target_probs)
        logit_grad = lax.reduce_precision(logit_grad, 8, 7)
        dot_part = jnp.sum(logit_grad * logits, axis=1)
        dot_high = lax.reduce_precision(dot_part, 8, 7)
        dot_low = dot_part - dot_high
        lanes = jnp.where(lane == own_lane, dot_high[:, None], 0.0) + jnp.where(
            lane == own_lane + 1, dot_low[:, None], 0.0
        )
        message = jnp.concatenate([logit_grad.astype(BF16), lanes.astype(BF16)], axis=1)
        everyone = groups.gather_halves(message)
        if h == CHUNKS - 1:
            chosen = groups.gather(after(own_chosen, everyone).reshape(CHUNKS, chunk_rows, -1))
            chosen = chosen.transpose(1, 0, 2, 3).reshape(CHUNKS * step_rows, -1)
        mine, other = [x.reshape(step_rows // CORES, -1) for x in everyone]
        normed_grad = back(index["turn"], mine, other, head_weight, piece_rows)

        def part(t):
            first = t % parts * piece_rows
            return normed_grad[first : first + piece_rows]

        summed = ring.scatter_sum(part, h)
        own_factor = lax.dynamic_slice(factor, (own_entry, own_first), (1, piece_rows))[0]
        row_dot = jnp.sum(summed[:, slice_width:], axis=1) / own_factor
        grad_piece = (
            own_factor[:, None] * gain * summed[:, :slice_width]
            - pieces[h].astype(F32) * (own_factor**3 * row_dot / model_width)[:, None]
        ).astype(BF16)
        grads.append(ring.gather(grad_piece, h))

    grad_joining, grad_share = outer(index["pieces"], chosen, grads, group_rows // slots)
    return (grad_share, grad_joining)


def solution(mesh):
    placed = (
        P("dp", "vocab"),
        P(),
        P("vocab", "dp"),
        P("dp", "vocab"),
        P("dp"),
        P("dp"),
        P("dp", "vocab"),
    )
    return jax.shard_map(
        body,
        mesh=mesh,
        in_specs=placed,
        out_specs=(P("vocab", "dp"), P("dp", "vocab")),
        check_vma=False,
    )
```

```python
import functools

import jax
import jax.numpy as jnp
import numpy as np
from jax import lax
from jax.experimental import pallas as pl
from jax.experimental.pallas import tpu as pltpu
from jax.sharding import PartitionSpec as P

TREE = 64
CORES = 2
LANES = 128
CHUNKS = 2
F32 = jnp.float32
BF16 = jnp.bfloat16


def ring_order(rows, columns):
    if columns == 1 or rows == 1:
        return list(range(rows * columns))
    order = [r * columns for r in range(rows)]
    for step in range(rows):
        r = rows - 1 - step
        line = [r * columns + c for c in range(1, columns)]
        order += line if step % 2 == 0 else line[::-1]
    return order


class Ring:
    def __init__(self, size, columns):
        self.size = size
        self.columns = columns
        self.half = size // 2
        self.order = ring_order(size // columns, columns)
        self.place = [0] * size
        for position, index in enumerate(self.order):
            self.place[index] = position

    def shift(self, x, step):
        size, order = self.size, self.order
        return lax.ppermute(
            x, "vocab", [(order[p], order[(p + step) % size]) for p in range(size)]
        )

    def partner(self, x, bit):
        return lax.ppermute(x, "vocab", [(v, v ^ bit) for v in range(self.size)])

    def meetings(self, merge):
        near = [bit for bit in range(1, self.columns)]
        far = [bit for bit in range(self.columns, self.size, self.columns)]
        return [
            lambda x, bits=bits: merge([x] + [self.partner(x, bit) for bit in bits])
            for bits in (near, far)
        ]

    def meet(self, x, merge):
        for round in self.meetings(merge):
            x = round(x)
        return x

    def reach(self, h):
        return (self.half, self.half - 1) if h % 2 == 0 else (self.half - 1, self.half)

    def gather(self, block, h, seen=None):
        far_ahead, far_behind = self.reach(h)
        ahead, behind = [block], [block]
        for step in range(self.half):
            if step < far_ahead:
                ahead.append(self.shift(ahead[-1], 1))
            if step < far_behind:
                behind.append(self.shift(behind[-1], -1))
            if seen:
                seen(step, (ahead[-1], behind[-1]))
        return ahead[1:][::-1] + [block] + behind[1:]

    def sources(self, vocab, h):
        p, far_ahead = self.place[vocab], self.reach(h)[0]
        return [(p + k - far_ahead) % self.size for k in range(self.size)]

    def scatter_sum(self, part, h, seen=None):
        far_ahead, far_behind = self.reach(h)
        got_ahead = got_behind = None
        for step in range(self.half, 0, -1):
            if step <= far_ahead:
                ahead = part(step) if got_ahead is None else part(step) + got_ahead
                got_ahead = self.shift(ahead.astype(BF16), 1).astype(F32)
            if step <= far_behind:
                behind = part(-step) if got_behind is None else part(-step) + got_behind
                got_behind = self.shift(behind.astype(BF16), -1).astype(F32)
            if seen:
                seen(self.half - step, (got_ahead, got_behind))
        return part(0) + got_ahead + got_behind


class Groups:
    def __init__(self, size):
        self.size = size
        self.chips = size // CORES

    def entry(self, index, group):
        chip = (group // CORES - index // CORES) % self.chips
        return (group % CORES ^ index % CORES) * self.chips + chip

    def swap(self, x):
        return lax.ppermute(x, "dp", [(i, i ^ 1) for i in range(self.size)])

    def shift(self, x, step):
        size = self.size
        return lax.ppermute(x, "dp", [(i, (i + CORES * step) % size) for i in range(size)])

    def gather_chips(self, block):
        return jnp.stack([block] + [self.shift(block, -d) for d in range(1, self.chips)])

    def gather_halves(self, block):
        mine = self.gather_chips(block)
        return mine, self.swap(mine)

    def gather(self, block):
        return jnp.concatenate(self.gather_halves(block), axis=0)


VMEM = pl.BlockSpec(memory_space=pltpu.VMEM)
SMEM = pl.BlockSpec(memory_space=pltpu.SMEM)


def transpose_into(out_ref, ref):
    tile = min(ref.shape[1], 256)
    for start in range(0, ref.shape[1], tile):
        block = ref[:, pl.ds(start, tile)].astype(F32)
        out_ref[pl.ds(start, tile), :] = block.T.astype(BF16)


def project_kernel(count, index_ref, factor_ref, gain_ref, weight_ref, *refs):
    blocks, refs = refs[:count], refs[count:]
    logits_refs, piece_refs = refs[:CORES], refs[CORES:-5]
    raw_ref, normed_ref, turned_ref, held_ref, sems = refs[-5:]
    rows, width = blocks[0].shape
    step = pl.program_id(0)
    tiles, tile = held_ref.shape[:2]
    piece = piece_refs[0].shape[0]
    half = logits_refs[0].shape[0]

    def fetch(n):
        return pltpu.make_async_copy(
            weight_ref.at[pl.ds(n * tile, tile), :], held_ref.at[n], sems.at[n]
        )

    @pl.when(step == 0)
    def _():
        for n in range(tiles):
            fetch(n).start()
        for k, ref in enumerate(blocks):
            start = pl.multiple_of(index_ref[k] * rows, rows)
            column = pl.multiple_of(index_ref[count + k] * width, width)
            raw_ref[pl.ds(start, rows), pl.ds(column, width)] = ref[...]
        for g in range(factor_ref.shape[0]):
            group = pl.ds(g * rows, rows)
            normed_ref[group, :] = (
                raw_ref[group, :].astype(F32) * factor_ref[g] * gain_ref[...]
            ).astype(BF16)
        for h, ref in enumerate(piece_refs):
            start = pl.multiple_of(index_ref[2 * count + h] * piece, piece)
            ref[...] = raw_ref[pl.ds(start, piece), :]
        transpose_into(turned_ref, normed_ref)

    fetch(step).wait()
    logits = jnp.dot(held_ref[step], turned_ref[...], preferred_element_type=F32).T
    for k, ref in enumerate(logits_refs):
        ref[...] = logits[k * half : (k + 1) * half]


def project(index, blocks, factor, gain, weight, piece_rows):
    vocab, depth = weight.shape
    all_rows = factor.shape[0] * blocks[0].shape[0]
    half = all_rows // CORES
    tile = min(vocab, 512)
    out = jax.ShapeDtypeStruct((half, vocab), F32)
    piece = jax.ShapeDtypeStruct((piece_rows, depth), BF16)
    return pl.pallas_call(
        functools.partial(project_kernel, len(blocks)),
        grid=(vocab // tile,),
        in_specs=[SMEM, VMEM, VMEM, pl.BlockSpec(memory_space=pltpu.HBM)]
        + [VMEM] * len(blocks),
        out_specs=[pl.BlockSpec((half, tile), lambda n: (0, n))] * CORES
        + [pl.BlockSpec((piece_rows, depth), lambda n: (0, 0))] * CHUNKS,
        out_shape=[out] * CORES + [piece] * CHUNKS,
        scratch_shapes=[
            pltpu.VMEM((all_rows, depth), BF16),
            pltpu.VMEM((all_rows, depth), BF16),
            pltpu.VMEM((depth, all_rows), BF16),
            pltpu.VMEM((vocab // tile, tile, depth), BF16),
            pltpu.SemaphoreType.DMA((vocab // tile,)),
        ],
        compiler_params=pltpu.CompilerParams(vmem_limit_bytes=48 * 2**20),
        cost_estimate=pl.CostEstimate(
            flops=2 * all_rows * depth * vocab,
            bytes_accessed=2 * vocab * depth + all_rows * (2 * depth + 4 * vocab),
            transcendentals=0,
        ),
    )(index, factor, gain, weight, *blocks)


def back_kernel(piece, index_ref, mine_ref, other_ref, weight_ref, out_ref, grad_ref):
    vocab = weight_ref.shape[0]
    tile = weight_ref.shape[1]
    half = mine_ref.shape[0]
    depth = out_ref.shape[1] - LANES
    step = pl.program_id(0)

    @pl.when(step == 0)
    def _():
        for k in range(2 * half // piece):
            ref, first = (mine_ref, k * piece) if k * piece < half else (other_ref, k * piece - half)
            rows = pl.ds(pl.multiple_of(index_ref[k] * piece, piece), piece)
            grad_ref[rows, :] = ref[pl.ds(first, piece), :vocab]
            out_ref[rows, pl.ds(depth, LANES)] = ref[pl.ds(first, piece), vocab:].astype(F32)

    columns = pl.ds(pl.multiple_of(step * tile, tile), tile)
    out_ref[:, columns] = jnp.dot(grad_ref[...], weight_ref[...], preferred_element_type=F32)


def back(index, mine, other, weight, piece_rows):
    vocab, depth = weight.shape
    all_rows = mine.shape[0] + other.shape[0]
    tile = min(depth, 512)
    return pl.pallas_call(
        functools.partial(back_kernel, piece_rows),
        grid=(depth // tile,),
        in_specs=[SMEM, VMEM, VMEM, pl.BlockSpec((vocab, tile), lambda n: (0, n))],
        out_specs=pl.BlockSpec((all_rows, depth + LANES), lambda n: (0, 0)),
        out_shape=jax.ShapeDtypeStruct((all_rows, depth + LANES), F32),
        scratch_shapes=[pltpu.VMEM((all_rows, vocab), BF16)],
        compiler_params=pltpu.CompilerParams(vmem_limit_bytes=24 * 2**20),
        cost_estimate=pl.CostEstimate(
            flops=2 * all_rows * depth * vocab,
            bytes_accessed=2 * vocab * depth + all_rows * (2 * vocab + 4 * depth),
            transcendentals=0,
        ),
    )(index, mine, other, weight)


def outer_kernel(count, tile, index_ref, chosen_ref, *refs):
    pieces, (out_ref, share_ref, grad_ref) = refs[:-3], refs[-3:]
    rows = pieces[0].shape[0]
    share = share_ref.shape[0]
    step = pl.program_id(0)

    @pl.when(step == 0)
    def _():
        for k, ref in enumerate(pieces):
            start = pl.multiple_of((k // count * count + index_ref[k]) * rows, rows)
            grad_ref[pl.ds(start, rows), :] = ref[...]
        start = pl.multiple_of(index_ref[len(pieces)] * share, share)
        share_ref[...] = grad_ref[pl.ds(start, share), :]

    columns = pl.ds(pl.multiple_of(step * tile, tile), tile)
    out_ref[...] = lax.dot_general(
        grad_ref[:, columns], chosen_ref[...], (((0,), (0,)), ((), ())), preferred_element_type=F32
    )


def outer(index, chosen, chunks, share_rows):
    depth = chunks[0][0].shape[1]
    all_rows, joined = chosen.shape
    tile = min(depth, 256)
    pieces = [x for chunk in chunks for x in chunk]
    return pl.pallas_call(
        functools.partial(outer_kernel, len(chunks[0]), tile),
        grid=(depth // tile,),
        in_specs=[SMEM, VMEM] + [VMEM] * len(pieces),
        out_specs=[
            pl.BlockSpec((tile, joined), lambda n: (n, 0)),
            pl.BlockSpec((share_rows, depth), lambda n: (0, 0)),
        ],
        out_shape=[
            jax.ShapeDtypeStruct((depth, joined), F32),
            jax.ShapeDtypeStruct((share_rows, depth), BF16),
        ],
        scratch_shapes=[pltpu.VMEM((all_rows, depth), BF16)],
        compiler_params=pltpu.CompilerParams(vmem_limit_bytes=40 * 2**20),
        cost_estimate=pl.CostEstimate(
            flops=2 * all_rows * depth * joined,
            bytes_accessed=4 * depth * joined + 2 * all_rows * (depth + joined),
            transcendentals=0,
        ),
    )(index, chosen, *pieces)


def device_table(groups, ring, slots, widths):
    group_rows, chunk_rows, piece_rows, slice_width = widths
    parts = ring.size
    step_rows = piece_rows * parts
    share_rows = group_rows // slots
    table = {}

    def add(name, values):
        table.setdefault(name, []).append(values)

    for g in range(groups.size):
        for v in range(parts):
            p = ring.place[v]
            held = [ring.order[q] for q in ring.sources(v, 0)]
            group = [i // slots % groups.chips * CORES + i // slots // groups.chips for i in held]
            add("place", [groups.entry(g, i) for i in group] + [i % slots for i in held])
            for h in range(CHUNKS):
                start = p * piece_rows
                start = start // chunk_rows * group_rows + h * chunk_rows + start % chunk_rows
                table["place"][-1].append(start // piece_rows)
            entry = groups.entry(g, v * share_rows // group_rows)
            first = v * share_rows % group_rows
            start = first // chunk_rows * step_rows + entry * chunk_rows + first % chunk_rows
            pieces = [q for h in range(CHUNKS) for q in ring.sources(v, h)]
            add("pieces", pieces + [start // share_rows])
            add("turn", [(k - p) % parts for k in range(parts)])
            start = p * piece_rows
            add("starts", [g * slice_width, start // chunk_rows, start % chunk_rows, 2 * p])
    return {
        name: np.asarray(rows, np.int32).reshape(groups.size, parts, -1)
        for name, rows in table.items()
    }


def after(x, *others):
    return lax.optimization_barrier((x, others))[0]


def body(hidden, norm_gain, head_weight, target_logits, valid_rows, parents, features):
    groups = Groups(lax.axis_size("dp"))
    parts = lax.axis_size("vocab")
    ring = Ring(parts, groups.chips)
    group_rows, block_width = hidden.shape
    chunk_rows = group_rows // CHUNKS
    step_rows = groups.size * chunk_rows
    piece_rows = step_rows // parts
    model_width = block_width * parts
    slots = parts // groups.size
    slice_width = block_width * slots
    vocab_width = target_logits.shape[1]

    table = device_table(
        groups, ring, slots, (group_rows, chunk_rows, piece_rows, slice_width)
    )
    own = lax.dynamic_slice(
        jnp.asarray(np.concatenate(list(table.values()), axis=2)),
        (lax.axis_index("dp"), lax.axis_index("vocab"), 0),
        (1, 1, sum(rows.shape[2] for rows in table.values())),
    ).reshape(-1)
    index, first = {}, 0
    for name, rows in table.items():
        index[name] = own[first : first + rows.shape[2]]
        first += rows.shape[2]
    gain_start, own_entry, own_first, own_lane = [
        index["starts"].astype(jnp.uint32)[k] for k in range(4)
    ]

    def chunk(x, h):
        return x[h * chunk_rows : (h + 1) * chunk_rows]

    def column_owner(g, v):
        far = g % CORES * groups.chips + g // CORES
        return v // slots * parts + far * slots + v % slots

    turn = [
        (g * parts + v, column_owner(g, v)) for g in range(groups.size) for v in range(parts)
    ]
    turned = lax.ppermute(hidden, ("dp", "vocab"), turn)

    live_rows = (valid_rows == 1).astype(F32)
    squares = jnp.sum(jnp.square(hidden.astype(F32)), axis=1)[None]
    rounds = ring.meetings(lambda terms: sum(terms[1:], terms[0]))
    rounds.append(lambda x: groups.gather_chips(jnp.concatenate([x, live_rows[None]])))
    rounds.append(lambda x: jnp.concatenate([x, groups.swap(x)], axis=0))
    exchanged = [rounds[0](squares)]
    late = rounds[1:]

    def seen(step, arrivals):
        if step < len(late):
            exchanged.append(late[step](after(exchanged[-1], arrivals)))

    blocks = ring.gather(turned, 0, seen)
    both = exchanged[-1]
    valid_count = jnp.sum(both[:, 1])
    row_factor = lax.rsqrt(both[:, 0] / model_width + 1e-05)

    targets = target_logits.astype(F32)
    target_top = jnp.max(targets, axis=1)
    target_total = jnp.sum(jnp.exp(targets - target_top[:, None]), axis=1)

    def merge_totals(terms):
        top = functools.reduce(jnp.maximum, [x[0] for x in terms])
        return jnp.stack([top, sum(x[1] * jnp.exp(x[0] - top) for x in terms)])

    tree_rows = jnp.arange(group_rows, dtype=jnp.int32) // TREE * TREE + parents
    own_chosen = features.at[tree_rows].get(mode="promise_in_bounds")

    gain = lax.dynamic_slice(norm_gain, (gain_start,), (slice_width,)).reshape(1, slice_width)
    row_weight = 1048576.0 * live_rows / valid_count
    lane = lax.broadcasted_iota(jnp.uint32, (chunk_rows, LANES), 1)

    keep, send, *pieces = project(
        index["place"], blocks, row_factor[:, :, None], gain, head_weight, piece_rows
    )
    summed = (keep + groups.swap(send)).reshape(groups.chips, group_rows, vocab_width)
    logits = summed[0]
    for d in range(1, groups.chips):
        logits = logits + groups.shift(summed[d], d)

    top = jnp.max(logits, axis=1)
    total = jnp.sum(jnp.exp(logits - top[:, None]), axis=1)
    mine = jnp.stack([jnp.concatenate([top, target_top]), jnp.concatenate([total, target_total])])
    met = ring.meet(mine, merge_totals)
    scale = jnp.exp(mine[0] - met[0]) / met[1]
    draft_scale, target_scale = scale[:group_rows], scale[group_rows:]

    grads = []
    for h in range(CHUNKS):
        factor = row_factor[:, h * chunk_rows : (h + 1) * chunk_rows]
        own = chunk(logits, h)
        draft_probs = jnp.exp(own - chunk(top, h)[:, None]) * chunk(draft_scale, h)[:, None]
        target_probs = (
            jnp.exp(chunk(targets, h) - chunk(target_top, h)[:, None])
            * chunk(target_scale, h)[:, None]
        )
        logit_grad = chunk(row_weight, h)[:, None] * (draft_probs - target_probs)
        logit_grad = lax.reduce_precision(logit_grad, 8, 7)
        dot_part = jnp.sum(logit_grad * own, axis=1)
        dot_high = lax.reduce_precision(dot_part, 8, 7)
        dot_low = dot_part - dot_high
        lanes = jnp.where(lane == own_lane, dot_high[:, None], 0.0) + jnp.where(
            lane == own_lane + 1, dot_low[:, None], 0.0
        )
        message = jnp.concatenate([logit_grad.astype(BF16), lanes.astype(BF16)], axis=1)
        everyone = groups.gather_halves(message)
        if h == CHUNKS - 1:
            chosen = groups.gather(after(own_chosen, everyone).reshape(CHUNKS, chunk_rows, -1))
            chosen = chosen.transpose(1, 0, 2, 3).reshape(CHUNKS * step_rows, -1)
        mine, other = [x.reshape(step_rows // CORES, -1) for x in everyone]
        normed_grad = back(index["turn"], mine, other, head_weight, piece_rows)

        def part(t):
            first = t % parts * piece_rows
            return normed_grad[first : first + piece_rows]

        summed = ring.scatter_sum(part, h)
        own_factor = lax.dynamic_slice(factor, (own_entry, own_first), (1, piece_rows))[0]
        row_dot = jnp.sum(summed[:, slice_width:], axis=1) / own_factor
        grad_piece = (
            own_factor[:, None] * gain * summed[:, :slice_width]
            - pieces[h].astype(F32) * (own_factor**3 * row_dot / model_width)[:, None]
        ).astype(BF16)
        grads.append(ring.gather(grad_piece, h))

    grad_joining, grad_share = outer(index["pieces"], chosen, grads, group_rows // slots)
    return (grad_share, grad_joining)


def solution(mesh):
    placed = (
        P("dp", "vocab"),
        P(),
        P("vocab", "dp"),
        P("dp", "vocab"),
        P("dp"),
        P("dp"),
        P("dp", "vocab"),
    )
    return jax.shard_map(
        body,
        mesh=mesh,
        in_specs=placed,
        out_specs=(P("vocab", "dp"), P("dp", "vocab")),
        check_vma=False,
    )
```

```python
import functools

import jax
import jax.numpy as jnp
import numpy as np
from jax import lax
from jax.experimental import pallas as pl
from jax.experimental.pallas import tpu as pltpu
from jax.sharding import PartitionSpec as P

TREE = 64
CORES = 2
LANES = 128
CHUNKS = 2
F32 = jnp.float32
BF16 = jnp.bfloat16


def ring_order(rows, columns):
    if columns == 1 or rows == 1:
        return list(range(rows * columns))
    order = [r * columns for r in range(rows)]
    for step in range(rows):
        r = rows - 1 - step
        line = [r * columns + c for c in range(1, columns)]
        order += line if step % 2 == 0 else line[::-1]
    return order


class Ring:
    def __init__(self, size, columns):
        self.size = size
        self.columns = columns
        self.half = size // 2
        self.order = ring_order(size // columns, columns)
        self.place = [0] * size
        for position, index in enumerate(self.order):
            self.place[index] = position

    def shift(self, x, step):
        size, order = self.size, self.order
        return lax.ppermute(
            x, "vocab", [(order[p], order[(p + step) % size]) for p in range(size)]
        )

    def partner(self, x, bit):
        return lax.ppermute(x, "vocab", [(v, v ^ bit) for v in range(self.size)])

    def meetings(self, merge):
        near = [bit for bit in range(1, self.columns)]
        far = [bit for bit in range(self.columns, self.size, self.columns)]
        return [
            lambda x, bits=bits: merge([x] + [self.partner(x, bit) for bit in bits])
            for bits in (near, far)
        ]

    def meet(self, x, merge):
        for round in self.meetings(merge):
            x = round(x)
        return x

    def reach(self, h):
        return (self.half, self.half - 1) if h % 2 == 0 else (self.half - 1, self.half)

    def gather(self, block, h, seen=None):
        far_ahead, far_behind = self.reach(h)
        ahead, behind = [block], [block]
        for step in range(self.half):
            if step < far_ahead:
                ahead.append(self.shift(ahead[-1], 1))
            if step < far_behind:
                behind.append(self.shift(behind[-1], -1))
            if seen:
                seen(step, (ahead[-1], behind[-1]))
        return ahead[1:][::-1] + [block] + behind[1:]

    def sources(self, vocab, h):
        p, far_ahead = self.place[vocab], self.reach(h)[0]
        return [(p + k - far_ahead) % self.size for k in range(self.size)]

    def scatter_sum(self, part, h, seen=None):
        far_ahead, far_behind = self.reach(h)
        got_ahead = got_behind = None
        for step in range(self.half, 0, -1):
            if step <= far_ahead:
                ahead = part(step) if got_ahead is None else part(step) + got_ahead
                got_ahead = self.shift(ahead.astype(BF16), 1).astype(F32)
            if step <= far_behind:
                behind = part(-step) if got_behind is None else part(-step) + got_behind
                got_behind = self.shift(behind.astype(BF16), -1).astype(F32)
            if seen:
                seen(self.half - step, (got_ahead, got_behind))
        return part(0) + got_ahead + got_behind


class Groups:
    def __init__(self, size):
        self.size = size
        self.chips = size // CORES

    def entry(self, index, group):
        chip = (group // CORES - index // CORES) % self.chips
        return (group % CORES ^ index % CORES) * self.chips + chip

    def swap(self, x):
        return lax.ppermute(x, "dp", [(i, i ^ 1) for i in range(self.size)])

    def shift(self, x, step):
        size = self.size
        return lax.ppermute(x, "dp", [(i, (i + CORES * step) % size) for i in range(size)])

    def gather_chips(self, block):
        return jnp.stack([block] + [self.shift(block, -d) for d in range(1, self.chips)])

    def gather_halves(self, block):
        mine = self.gather_chips(block)
        return mine, self.swap(mine)

    def gather(self, block):
        return jnp.concatenate(self.gather_halves(block), axis=0)


VMEM = pl.BlockSpec(memory_space=pltpu.VMEM)
SMEM = pl.BlockSpec(memory_space=pltpu.SMEM)


def transpose_into(out_ref, ref):
    tile = min(ref.shape[1], 256)
    for start in range(0, ref.shape[1], tile):
        block = ref[:, pl.ds(start, tile)].astype(F32)
        out_ref[pl.ds(start, tile), :] = block.T.astype(BF16)


def fetch_tiles(weight_ref, first, held_ref, sems):
    tile = held_ref.shape[1]
    return lambda n: pltpu.make_async_copy(
        weight_ref.at[pl.ds(first + n * tile, tile), :], held_ref.at[n], sems.at[n]
    )


def tile_logits(fetch, held_ref, turned_ref, keep_ref, send_ref):
    step = pl.program_id(0)
    half = keep_ref.shape[0]
    fetch(step).wait()
    logits = jnp.dot(held_ref[step], turned_ref[...], preferred_element_type=F32).T
    keep_ref[...] = logits[:half]
    send_ref[...] = logits[half:]


def project_kernel(count, index_ref, factor_ref, gain_ref, weight_ref, *refs):
    blocks, refs = refs[: CHUNKS * count], refs[CHUNKS * count :]
    keep_ref, send_ref, turned_ref = refs[:3]
    piece_refs = refs[3 : 3 + CHUNKS]
    raw_ref, normed_ref, held_ref, sems = refs[3 + CHUNKS :]
    rows, width = blocks[0].shape
    group_rows = CHUNKS * rows
    piece = piece_refs[0].shape[0]
    fetch = fetch_tiles(weight_ref, 0, held_ref, sems)

    @pl.when(pl.program_id(0) == 0)
    def _():
        for n in range(held_ref.shape[0]):
            fetch(n).start()
        for k, ref in enumerate(blocks):
            h, at = k // count, k + k // count * count
            start = pl.multiple_of(index_ref[at] * group_rows + h * rows, rows)
            column = pl.multiple_of(index_ref[at + count] * width, width)
            raw_ref[pl.ds(start, rows), pl.ds(column, width)] = ref[...]
        for g in range(factor_ref.shape[0]):
            group = pl.ds(g * group_rows, group_rows)
            normed_ref[group, :] = (
                raw_ref[group, :].astype(F32) * factor_ref[g] * gain_ref[...]
            ).astype(BF16)
        transpose_into(turned_ref, normed_ref)
        for h, ref in enumerate(piece_refs):
            start = pl.multiple_of(index_ref[2 * CHUNKS * count + h] * piece, piece)
            ref[...] = raw_ref[pl.ds(start, piece), :]

    tile_logits(fetch, held_ref, turned_ref, keep_ref, send_ref)


def project_rest_kernel(weight_ref, turned_ref, keep_ref, send_ref, held_ref, sems):
    fetch = fetch_tiles(weight_ref, weight_ref.shape[0] // 2, held_ref, sems)

    @pl.when(pl.program_id(0) == 0)
    def _():
        for n in range(held_ref.shape[0]):
            fetch(n).start()

    tile_logits(fetch, held_ref, turned_ref, keep_ref, send_ref)


def project(index, blocks, factor, gain, weight, piece_rows):
    vocab, depth = weight.shape
    all_rows = factor.shape[0] * factor.shape[1]
    half = all_rows // CORES
    tile = min(vocab // 2, 512)
    tiles = vocab // 2 // tile
    out = [jax.ShapeDtypeStruct((half, vocab // 2), F32)] * CORES
    out_specs = [pl.BlockSpec((half, tile), lambda n: (0, n))] * CORES
    whole = lambda rows, columns: pl.BlockSpec((rows, columns), lambda n: (0, 0))
    held = [pltpu.VMEM((tiles, tile, depth), BF16), pltpu.SemaphoreType.DMA((tiles,))]
    hbm = pl.BlockSpec(memory_space=pltpu.HBM)
    params = pltpu.CompilerParams(vmem_limit_bytes=48 * 2**20)
    cost = pl.CostEstimate(
        flops=all_rows * depth * vocab,
        bytes_accessed=vocab * depth + all_rows * (2 * depth + 2 * vocab),
        transcendentals=0,
    )
    keep, send, turned, *pieces = pl.pallas_call(
        functools.partial(project_kernel, len(blocks[0])),
        grid=(tiles,),
        in_specs=[SMEM, VMEM, VMEM, hbm] + [VMEM] * (CHUNKS * len(blocks[0])),
        out_specs=out_specs + [whole(depth, all_rows)] + [whole(piece_rows, depth)] * CHUNKS,
        out_shape=out
        + [jax.ShapeDtypeStruct((depth, all_rows), BF16)]
        + [jax.ShapeDtypeStruct((piece_rows, depth), BF16)] * CHUNKS,
        scratch_shapes=[pltpu.VMEM((all_rows, depth), BF16)] * 2 + held,
        compiler_params=params,
        cost_estimate=cost,
    )(index, factor, gain, weight, *[x for chunk in blocks for x in chunk])
    rest = pl.pallas_call(
        project_rest_kernel,
        grid=(tiles,),
        in_specs=[hbm, VMEM],
        out_specs=out_specs,
        out_shape=out,
        scratch_shapes=held,
        compiler_params=params,
        cost_estimate=cost,
    )(weight, turned)
    return [(keep, send), rest], pieces


def back_kernel(piece, index_ref, mine_ref, other_ref, weight_ref, out_ref, grad_ref):
    vocab = weight_ref.shape[0]
    tile = weight_ref.shape[1]
    half = mine_ref.shape[0]
    depth = out_ref.shape[1] - LANES
    step = pl.program_id(0)

    @pl.when(step == 0)
    def _():
        for k in range(2 * half // piece):
            ref, first = (mine_ref, k * piece) if k * piece < half else (other_ref, k * piece - half)
            rows = pl.ds(pl.multiple_of(index_ref[k] * piece, piece), piece)
            grad_ref[rows, :] = ref[pl.ds(first, piece), :vocab]
            out_ref[rows, pl.ds(depth, LANES)] = ref[pl.ds(first, piece), vocab:].astype(F32)

    columns = pl.ds(pl.multiple_of(step * tile, tile), tile)
    out_ref[:, columns] = jnp.dot(grad_ref[...], weight_ref[...], preferred_element_type=F32)


def back(index, mine, other, weight, piece_rows):
    vocab, depth = weight.shape
    all_rows = mine.shape[0] + other.shape[0]
    tile = min(depth, 512)
    return pl.pallas_call(
        functools.partial(back_kernel, piece_rows),
        grid=(depth // tile,),
        in_specs=[SMEM, VMEM, VMEM, pl.BlockSpec((vocab, tile), lambda n: (0, n))],
        out_specs=pl.BlockSpec((all_rows, depth + LANES), lambda n: (0, 0)),
        out_shape=jax.ShapeDtypeStruct((all_rows, depth + LANES), F32),
        scratch_shapes=[pltpu.VMEM((all_rows, vocab), BF16)],
        compiler_params=pltpu.CompilerParams(vmem_limit_bytes=24 * 2**20),
        cost_estimate=pl.CostEstimate(
            flops=2 * all_rows * depth * vocab,
            bytes_accessed=2 * vocab * depth + all_rows * (2 * vocab + 4 * depth),
            transcendentals=0,
        ),
    )(index, mine, other, weight)


def outer_kernel(count, tile, index_ref, chosen_ref, *refs):
    pieces, (out_ref, share_ref, grad_ref) = refs[:-3], refs[-3:]
    rows = pieces[0].shape[0]
    share = share_ref.shape[0]
    step = pl.program_id(0)

    @pl.when(step == 0)
    def _():
        for k, ref in enumerate(pieces):
            start = pl.multiple_of((k // count * count + index_ref[k]) * rows, rows)
            grad_ref[pl.ds(start, rows), :] = ref[...]
        start = pl.multiple_of(index_ref[len(pieces)] * share, share)
        share_ref[...] = grad_ref[pl.ds(start, share), :]

    columns = pl.ds(pl.multiple_of(step * tile, tile), tile)
    out_ref[...] = lax.dot_general(
        grad_ref[:, columns], chosen_ref[...], (((0,), (0,)), ((), ())), preferred_element_type=F32
    )


def outer(index, chosen, chunks, share_rows):
    depth = chunks[0][0].shape[1]
    all_rows, joined = chosen.shape
    tile = min(depth, 256)
    pieces = [x for chunk in chunks for x in chunk]
    return pl.pallas_call(
        functools.partial(outer_kernel, len(chunks[0]), tile),
        grid=(depth // tile,),
        in_specs=[SMEM, VMEM] + [VMEM] * len(pieces),
        out_specs=[
            pl.BlockSpec((tile, joined), lambda n: (n, 0)),
            pl.BlockSpec((share_rows, depth), lambda n: (0, 0)),
        ],
        out_shape=[
            jax.ShapeDtypeStruct((depth, joined), F32),
            jax.ShapeDtypeStruct((share_rows, depth), BF16),
        ],
        scratch_shapes=[pltpu.VMEM((all_rows, depth), BF16)],
        compiler_params=pltpu.CompilerParams(vmem_limit_bytes=40 * 2**20),
        cost_estimate=pl.CostEstimate(
            flops=2 * all_rows * depth * joined,
            bytes_accessed=4 * depth * joined + 2 * all_rows * (depth + joined),
            transcendentals=0,
        ),
    )(index, chosen, *pieces)


def device_table(groups, ring, slots, widths):
    group_rows, chunk_rows, piece_rows, slice_width = widths
    parts = ring.size
    step_rows = piece_rows * parts
    share_rows = group_rows // slots
    table = {}

    def add(name, values):
        table.setdefault(name, []).append(values)

    for g in range(groups.size):
        for v in range(parts):
            p = ring.place[v]
            place = []
            for h in range(CHUNKS):
                held = [ring.order[q] for q in ring.sources(v, h)]
                for i in held:
                    group = i // slots % groups.chips * CORES + i // slots // groups.chips
                    place.append(groups.entry(g, group))
                place += [i % slots for i in held]
            for h in range(CHUNKS):
                start = p * piece_rows
                start = start // chunk_rows * group_rows + h * chunk_rows + start % chunk_rows
                place.append(start // piece_rows)
            add("place", place)
            entry = groups.entry(g, v * share_rows // group_rows)
            first = v * share_rows % group_rows
            start = first // chunk_rows * step_rows + entry * chunk_rows + first % chunk_rows
            pieces = [q for h in range(CHUNKS) for q in ring.sources(v, h)]
            add("pieces", pieces + [start // share_rows])
            add("turn", [(k - p) % parts for k in range(parts)])
            start = p * piece_rows
            add("starts", [g * slice_width, start // chunk_rows, start % chunk_rows, 2 * p])
    return {
        name: np.asarray(rows, np.int32).reshape(groups.size, parts, -1)
        for name, rows in table.items()
    }


def after(x, *others):
    return lax.optimization_barrier((x, others))[0]


def body(hidden, norm_gain, head_weight, target_logits, valid_rows, parents, features):
    groups = Groups(lax.axis_size("dp"))
    parts = lax.axis_size("vocab")
    ring = Ring(parts, groups.chips)
    group_rows, block_width = hidden.shape
    chunk_rows = group_rows // CHUNKS
    step_rows = groups.size * chunk_rows
    piece_rows = step_rows // parts
    model_width = block_width * parts
    slots = parts // groups.size
    slice_width = block_width * slots
    vocab_width = target_logits.shape[1]

    table = device_table(
        groups, ring, slots, (group_rows, chunk_rows, piece_rows, slice_width)
    )
    own = lax.dynamic_slice(
        jnp.asarray(np.concatenate(list(table.values()), axis=2)),
        (lax.axis_index("dp"), lax.axis_index("vocab"), 0),
        (1, 1, sum(rows.shape[2] for rows in table.values())),
    ).reshape(-1)
    index, first = {}, 0
    for name, rows in table.items():
        index[name] = own[first : first + rows.shape[2]]
        first += rows.shape[2]
    gain_start, own_entry, own_first, own_lane = [
        index["starts"].astype(jnp.uint32)[k] for k in range(4)
    ]

    def chunk(x, h):
        return x[h * chunk_rows : (h + 1) * chunk_rows]

    def column_owner(g, v):
        far = g % CORES * groups.chips + g // CORES
        return v // slots * parts + far * slots + v % slots

    turn = [
        (g * parts + v, column_owner(g, v)) for g in range(groups.size) for v in range(parts)
    ]
    turned = lax.ppermute(hidden, ("dp", "vocab"), turn)

    live_rows = (valid_rows == 1).astype(F32)
    squares = jnp.sum(jnp.square(hidden.astype(F32)), axis=1)[None]
    rounds = ring.meetings(lambda terms: sum(terms[1:], terms[0]))
    rounds.append(lambda x: groups.gather_chips(jnp.concatenate([x, live_rows[None]])))
    rounds.append(lambda x: jnp.concatenate([x, groups.swap(x)], axis=0))
    for round in rounds[:2]:
        squares = round(squares)
    turned = after(turned, squares)
    late = rounds[2:]
    exchanged = [squares]

    def seen(step, arrivals):
        if step < len(late):
            exchanged.append(late[step](after(exchanged[-1], arrivals)))

    blocks = [ring.gather(chunk(turned, h), h, seen if h == 0 else None) for h in range(CHUNKS)]
    both = exchanged[-1]
    valid_count = jnp.sum(both[:, 1])
    row_factor = lax.rsqrt(both[:, 0] / model_width + 1e-05)

    targets = target_logits.astype(F32)
    target_top = jnp.max(targets, axis=1)
    target_total = jnp.sum(jnp.exp(targets - target_top[:, None]), axis=1)

    def merge_totals(terms):
        top = functools.reduce(jnp.maximum, [x[0] for x in terms])
        return jnp.stack([top, sum(x[1] * jnp.exp(x[0] - top) for x in terms)])

    tree_rows = jnp.arange(group_rows, dtype=jnp.int32) // TREE * TREE + parents
    own_chosen = features.at[tree_rows].get(mode="promise_in_bounds")

    gain = lax.dynamic_slice(norm_gain, (gain_start,), (slice_width,)).reshape(1, slice_width)
    row_weight = 1048576.0 * live_rows / valid_count
    lane = lax.broadcasted_iota(jnp.uint32, (chunk_rows, LANES), 1)

    halves, pieces = project(
        index["place"], blocks, row_factor[:, :, None], gain, head_weight, piece_rows
    )
    logits, totals = [], []
    for keep, send in halves:
        summed = (keep + groups.swap(send)).reshape(groups.chips, group_rows, -1)
        half = summed[0]
        for d in range(1, groups.chips):
            half = half + groups.shift(summed[d], d)
        top = jnp.max(half, axis=1)
        logits.append(half)
        totals.append(jnp.stack([top, jnp.sum(jnp.exp(half - top[:, None]), axis=1)]))

    mine = jnp.concatenate([merge_totals(totals), jnp.stack([target_top, target_total])], axis=1)
    met = ring.meet(mine, merge_totals)
    scale = jnp.exp(mine[0] - met[0]) / met[1]
    top, draft_scale, target_scale = mine[0], scale[:group_rows], scale[group_rows:]

    grads = []
    for h in range(CHUNKS):
        factor = row_factor[:, h * chunk_rows : (h + 1) * chunk_rows]
        parts_of, dot_part = [], 0.0
        for k, half in enumerate(logits):
            own = chunk(half, h)
            columns = slice(k * own.shape[1], (k + 1) * own.shape[1])
            draft_probs = jnp.exp(own - chunk(top, h)[:, None]) * chunk(draft_scale, h)[:, None]
            target_probs = (
                jnp.exp(chunk(targets, h)[:, columns] - chunk(target_top, h)[:, None])
                * chunk(target_scale, h)[:, None]
            )
            logit_grad = chunk(row_weight, h)[:, None] * (draft_probs - target_probs)
            logit_grad = lax.reduce_precision(logit_grad, 8, 7)
            dot_part = dot_part + jnp.sum(logit_grad * own, axis=1)
            parts_of.append(logit_grad.astype(BF16))
        dot_high = lax.reduce_precision(dot_part, 8, 7)
        dot_low = dot_part - dot_high
        lanes = jnp.where(lane == own_lane, dot_high[:, None], 0.0) + jnp.where(
            lane == own_lane + 1, dot_low[:, None], 0.0
        )
        message = jnp.concatenate(parts_of + [lanes.astype(BF16)], axis=1)
        if h > 0:
            message = after(message, mine)
        mine = groups.gather_chips(message)
        mine, other = [x.reshape(step_rows // CORES, -1) for x in (mine, groups.swap(mine))]
        normed_grad = back(index["turn"], mine, other, head_weight, piece_rows)
        if h == CHUNKS - 1:
            chosen = after(own_chosen, normed_grad).reshape(CHUNKS, chunk_rows, -1)
            chosen = groups.gather(chosen).transpose(1, 0, 2, 3).reshape(CHUNKS * step_rows, -1)

        def part(t):
            first = t % parts * piece_rows
            return normed_grad[first : first + piece_rows]

        summed = ring.scatter_sum(part, h)
        own_factor = lax.dynamic_slice(factor, (own_entry, own_first), (1, piece_rows))[0]
        row_dot = jnp.sum(summed[:, slice_width:], axis=1) / own_factor
        grad_piece = (
            own_factor[:, None] * gain * summed[:, :slice_width]
            - pieces[h].astype(F32) * (own_factor**3 * row_dot / model_width)[:, None]
        ).astype(BF16)
        grads.append(ring.gather(grad_piece, h))

    grad_joining, grad_share = outer(index["pieces"], chosen, grads, group_rows // slots)
    return (grad_share, grad_joining)


def solution(mesh):
    placed = (
        P("dp", "vocab"),
        P(),
        P("vocab", "dp"),
        P("dp", "vocab"),
        P("dp"),
        P("dp"),
        P("dp", "vocab"),
    )
    return jax.shard_map(
        body,
        mesh=mesh,
        in_specs=placed,
        out_specs=(P("vocab", "dp"), P("dp", "vocab")),
        check_vma=False,
    )
```

```python
import functools

import jax
import jax.numpy as jnp
import numpy as np
from jax import lax
from jax.experimental import pallas as pl
from jax.experimental.pallas import tpu as pltpu
from jax.sharding import PartitionSpec as P

TREE = 64
CORES = 2
LANES = 128
CHUNKS = 2
F32 = jnp.float32
BF16 = jnp.bfloat16


def ring_order(rows, columns):
    if columns == 1 or rows == 1:
        return list(range(rows * columns))
    order = [r * columns for r in range(rows)]
    for step in range(rows):
        r = rows - 1 - step
        line = [r * columns + c for c in range(1, columns)]
        order += line if step % 2 == 0 else line[::-1]
    return order


class Ring:
    def __init__(self, size, columns):
        self.size = size
        self.columns = columns
        self.half = size // 2
        self.order = ring_order(size // columns, columns)
        self.place = [0] * size
        for position, index in enumerate(self.order):
            self.place[index] = position

    def shift(self, x, step):
        size, order = self.size, self.order
        return lax.ppermute(
            x, "vocab", [(order[p], order[(p + step) % size]) for p in range(size)]
        )

    def partner(self, x, bit):
        return lax.ppermute(x, "vocab", [(v, v ^ bit) for v in range(self.size)])

    def meetings(self, merge):
        near = [bit for bit in range(1, self.columns)]
        far = [bit for bit in range(self.columns, self.size, self.columns)]
        return [
            lambda x, bits=bits: merge([x] + [self.partner(x, bit) for bit in bits])
            for bits in (near, far)
        ]

    def meet(self, x, merge):
        for round in self.meetings(merge):
            x = round(x)
        return x

    def reach(self, h):
        return (self.half, self.half - 1) if h % 2 == 0 else (self.half - 1, self.half)

    def gather(self, block, h, seen=None):
        far_ahead, far_behind = self.reach(h)
        ahead, behind = [block], [block]
        for step in range(self.half):
            if step < far_ahead:
                ahead.append(self.shift(ahead[-1], 1))
            if step < far_behind:
                behind.append(self.shift(behind[-1], -1))
            if seen:
                seen(step, (ahead[-1], behind[-1]))
        return ahead[1:][::-1] + [block] + behind[1:]

    def sources(self, vocab, h):
        p, far_ahead = self.place[vocab], self.reach(h)[0]
        return [(p + k - far_ahead) % self.size for k in range(self.size)]

    def scatter_sum(self, part, h, seen=None):
        far_ahead, far_behind = self.reach(h)
        got_ahead = got_behind = None
        for step in range(self.half, 0, -1):
            if step <= far_ahead:
                ahead = part(step) if got_ahead is None else part(step) + got_ahead
                got_ahead = self.shift(ahead.astype(BF16), 1).astype(F32)
            if step <= far_behind:
                behind = part(-step) if got_behind is None else part(-step) + got_behind
                got_behind = self.shift(behind.astype(BF16), -1).astype(F32)
            if seen:
                seen(self.half - step, (got_ahead, got_behind))
        return part(0) + got_ahead + got_behind


class Groups:
    def __init__(self, size):
        self.size = size
        self.chips = size // CORES

    def entry(self, index, group):
        chip = (group // CORES - index // CORES) % self.chips
        return (group % CORES ^ index % CORES) * self.chips + chip

    def swap(self, x):
        return lax.ppermute(x, "dp", [(i, i ^ 1) for i in range(self.size)])

    def shift(self, x, step):
        size = self.size
        return lax.ppermute(x, "dp", [(i, (i + CORES * step) % size) for i in range(size)])

    def gather_chips(self, block):
        return jnp.stack([block] + [self.shift(block, -d) for d in range(1, self.chips)])

    def gather_halves(self, block):
        mine = self.gather_chips(block)
        return mine, self.swap(mine)

    def gather(self, block):
        return jnp.concatenate(self.gather_halves(block), axis=0)


VMEM = pl.BlockSpec(memory_space=pltpu.VMEM)
SMEM = pl.BlockSpec(memory_space=pltpu.SMEM)


def transpose_into(out_ref, ref):
    tile = min(ref.shape[1], 256)
    for start in range(0, ref.shape[1], tile):
        block = ref[:, pl.ds(start, tile)].astype(F32)
        out_ref[pl.ds(start, tile), :] = block.T.astype(BF16)


def hold_kernel(weight_ref, held_ref, sems):
    tile = weight_ref.shape[0] // sems.shape[0]
    copies = [
        pltpu.make_async_copy(
            weight_ref.at[pl.ds(n * tile, tile), :], held_ref.at[pl.ds(n * tile, tile), :], sems.at[n]
        )
        for n in range(sems.shape[0])
    ]
    for copy in copies:
        copy.start()
    for copy in copies:
        copy.wait()


def hold(weight):
    return pl.pallas_call(
        hold_kernel,
        in_specs=[pl.BlockSpec(memory_space=pltpu.HBM)],
        out_specs=VMEM,
        out_shape=jax.ShapeDtypeStruct(weight.shape, weight.dtype),
        scratch_shapes=[pltpu.SemaphoreType.DMA((4,))],
        compiler_params=pltpu.CompilerParams(vmem_limit_bytes=12 * 2**20),
        cost_estimate=pl.CostEstimate(flops=0, bytes_accessed=2 * weight.size, transcendentals=0),
    )(weight)


def project_kernel(count, tile, index_ref, factor_ref, gain_ref, weight_ref, *refs):
    blocks, refs = refs[: CHUNKS * count], refs[CHUNKS * count :]
    keep_ref, send_ref = refs[:CORES]
    piece_refs = refs[CORES : CORES + CHUNKS]
    raw_ref, normed_ref, turned_ref = refs[CORES + CHUNKS :]
    rows, width = blocks[0].shape
    group_rows = CHUNKS * rows
    piece = piece_refs[0].shape[0]
    half = keep_ref.shape[0]
    step = pl.program_id(0)

    @pl.when(step == 0)
    def _():
        for k, ref in enumerate(blocks):
            h, at = k // count, k + k // count * count
            start = pl.multiple_of(index_ref[at] * group_rows + h * rows, rows)
            column = pl.multiple_of(index_ref[at + count] * width, width)
            raw_ref[pl.ds(start, rows), pl.ds(column, width)] = ref[...]
        for g in range(factor_ref.shape[0]):
            group = pl.ds(g * group_rows, group_rows)
            normed_ref[group, :] = (
                raw_ref[group, :].astype(F32) * factor_ref[g] * gain_ref[...]
            ).astype(BF16)
        transpose_into(turned_ref, normed_ref)
        for h, ref in enumerate(piece_refs):
            start = pl.multiple_of(index_ref[2 * CHUNKS * count + h] * piece, piece)
            ref[...] = raw_ref[pl.ds(start, piece), :]

    rows = pl.ds(pl.multiple_of(step * tile, tile), tile)
    logits = jnp.dot(weight_ref[rows, :], turned_ref[...], preferred_element_type=F32).T
    keep_ref[...] = logits[:half]
    send_ref[...] = logits[half:]


def project(index, blocks, factor, gain, weight, piece_rows):
    vocab, depth = weight.shape
    all_rows = factor.shape[0] * factor.shape[1]
    half = all_rows // CORES
    tile = min(vocab, 512)
    out = jax.ShapeDtypeStruct((half, vocab), F32)
    piece = jax.ShapeDtypeStruct((piece_rows, depth), BF16)
    return pl.pallas_call(
        functools.partial(project_kernel, len(blocks[0]), tile),
        grid=(vocab // tile,),
        in_specs=[SMEM] + [VMEM] * (3 + CHUNKS * len(blocks[0])),
        out_specs=[pl.BlockSpec((half, tile), lambda n: (0, n))] * CORES
        + [pl.BlockSpec((piece_rows, depth), lambda n: (0, 0))] * CHUNKS,
        out_shape=[out] * CORES + [piece] * CHUNKS,
        scratch_shapes=[pltpu.VMEM((all_rows, depth), BF16)] * 2
        + [pltpu.VMEM((depth, all_rows), BF16)],
        compiler_params=pltpu.CompilerParams(vmem_limit_bytes=28 * 2**20),
        cost_estimate=pl.CostEstimate(
            flops=2 * all_rows * depth * vocab,
            bytes_accessed=2 * vocab * depth + all_rows * (2 * depth + 4 * vocab),
            transcendentals=0,
        ),
    )(index, factor, gain, weight, *[x for chunk in blocks for x in chunk])


def back_kernel(piece, tile, index_ref, mine_ref, other_ref, weight_ref, out_ref, grad_ref):
    vocab = weight_ref.shape[0]
    half = mine_ref.shape[0]
    depth = out_ref.shape[1] - LANES
    step = pl.program_id(0)

    @pl.when(step == 0)
    def _():
        for k in range(2 * half // piece):
            ref, first = (mine_ref, k * piece) if k * piece < half else (other_ref, k * piece - half)
            rows = pl.ds(pl.multiple_of(index_ref[k] * piece, piece), piece)
            grad_ref[rows, :] = ref[pl.ds(first, piece), :vocab]
            out_ref[rows, pl.ds(depth, LANES)] = ref[pl.ds(first, piece), vocab:].astype(F32)

    columns = pl.ds(pl.multiple_of(step * tile, tile), tile)
    out_ref[:, columns] = jnp.dot(
        grad_ref[...], weight_ref[:, columns], preferred_element_type=F32
    )


def back(index, mine, other, weight, piece_rows):
    vocab, depth = weight.shape
    all_rows = mine.shape[0] + other.shape[0]
    tile = min(depth, 512)
    return pl.pallas_call(
        functools.partial(back_kernel, piece_rows, tile),
        grid=(depth // tile,),
        in_specs=[SMEM, VMEM, VMEM, VMEM],
        out_specs=pl.BlockSpec((all_rows, depth + LANES), lambda n: (0, 0)),
        out_shape=jax.ShapeDtypeStruct((all_rows, depth + LANES), F32),
        scratch_shapes=[pltpu.VMEM((all_rows, vocab), BF16)],
        compiler_params=pltpu.CompilerParams(vmem_limit_bytes=24 * 2**20),
        cost_estimate=pl.CostEstimate(
            flops=2 * all_rows * depth * vocab,
            bytes_accessed=2 * vocab * depth + all_rows * (2 * vocab + 4 * depth),
            transcendentals=0,
        ),
    )(index, mine, other, weight)


def outer_kernel(count, tile, index_ref, chosen_ref, *refs):
    pieces, (out_ref, share_ref, grad_ref) = refs[:-3], refs[-3:]
    rows = pieces[0].shape[0]
    share = share_ref.shape[0]
    step = pl.program_id(0)

    @pl.when(step == 0)
    def _():
        for k, ref in enumerate(pieces):
            start = pl.multiple_of((k // count * count + index_ref[k]) * rows, rows)
            grad_ref[pl.ds(start, rows), :] = ref[...]
        start = pl.multiple_of(index_ref[len(pieces)] * share, share)
        share_ref[...] = grad_ref[pl.ds(start, share), :]

    columns = pl.ds(pl.multiple_of(step * tile, tile), tile)
    out_ref[...] = lax.dot_general(
        grad_ref[:, columns], chosen_ref[...], (((0,), (0,)), ((), ())), preferred_element_type=F32
    )


def outer(index, chosen, chunks, share_rows):
    depth = chunks[0][0].shape[1]
    all_rows, joined = chosen.shape
    tile = min(depth, 256)
    pieces = [x for chunk in chunks for x in chunk]
    return pl.pallas_call(
        functools.partial(outer_kernel, len(chunks[0]), tile),
        grid=(depth // tile,),
        in_specs=[SMEM, VMEM] + [VMEM] * len(pieces),
        out_specs=[
            pl.BlockSpec((tile, joined), lambda n: (n, 0)),
            pl.BlockSpec((share_rows, depth), lambda n: (0, 0)),
        ],
        out_shape=[
            jax.ShapeDtypeStruct((depth, joined), F32),
            jax.ShapeDtypeStruct((share_rows, depth), BF16),
        ],
        scratch_shapes=[pltpu.VMEM((all_rows, depth), BF16)],
        compiler_params=pltpu.CompilerParams(vmem_limit_bytes=40 * 2**20),
        cost_estimate=pl.CostEstimate(
            flops=2 * all_rows * depth * joined,
            bytes_accessed=4 * depth * joined + 2 * all_rows * (depth + joined),
            transcendentals=0,
        ),
    )(index, chosen, *pieces)


def device_table(groups, ring, slots, widths):
    group_rows, chunk_rows, piece_rows, slice_width = widths
    parts = ring.size
    step_rows = piece_rows * parts
    share_rows = group_rows // slots
    table = {}

    def add(name, values):
        table.setdefault(name, []).append(values)

    for g in range(groups.size):
        for v in range(parts):
            p = ring.place[v]
            place = []
            for h in range(CHUNKS):
                held = [ring.order[q] for q in ring.sources(v, h)]
                for i in held:
                    group = i // slots % groups.chips * CORES + i // slots // groups.chips
                    place.append(groups.entry(g, group))
                place += [i % slots for i in held]
            for h in range(CHUNKS):
                start = p * piece_rows
                start = start // chunk_rows * group_rows + h * chunk_rows + start % chunk_rows
                place.append(start // piece_rows)
            add("place", place)
            entry = groups.entry(g, v * share_rows // group_rows)
            first = v * share_rows % group_rows
            start = first // chunk_rows * step_rows + entry * chunk_rows + first % chunk_rows
            pieces = [q for h in range(CHUNKS) for q in ring.sources(v, h)]
            add("pieces", pieces + [start // share_rows])
            add("turn", [(k - p) % parts for k in range(parts)])
            start = p * piece_rows
            add("starts", [g * slice_width, start // chunk_rows, start % chunk_rows, 2 * p])
    return {
        name: np.asarray(rows, np.int32).reshape(groups.size, parts, -1)
        for name, rows in table.items()
    }


def after(x, *others):
    return lax.optimization_barrier((x, others))[0]


def body(hidden, norm_gain, head_weight, target_logits, valid_rows, parents, features):
    groups = Groups(lax.axis_size("dp"))
    parts = lax.axis_size("vocab")
    ring = Ring(parts, groups.chips)
    group_rows, block_width = hidden.shape
    chunk_rows = group_rows // CHUNKS
    step_rows = groups.size * chunk_rows
    piece_rows = step_rows // parts
    model_width = block_width * parts
    slots = parts // groups.size
    slice_width = block_width * slots
    vocab_width = target_logits.shape[1]

    table = device_table(
        groups, ring, slots, (group_rows, chunk_rows, piece_rows, slice_width)
    )
    own = lax.dynamic_slice(
        jnp.asarray(np.concatenate(list(table.values()), axis=2)),
        (lax.axis_index("dp"), lax.axis_index("vocab"), 0),
        (1, 1, sum(rows.shape[2] for rows in table.values())),
    ).reshape(-1)
    index, first = {}, 0
    for name, rows in table.items():
        index[name] = own[first : first + rows.shape[2]]
        first += rows.shape[2]
    gain_start, own_entry, own_first, own_lane = [
        index["starts"].astype(jnp.uint32)[k] for k in range(4)
    ]

    def chunk(x, h):
        return x[h * chunk_rows : (h + 1) * chunk_rows]

    def column_owner(g, v):
        far = g % CORES * groups.chips + g // CORES
        return v // slots * parts + far * slots + v % slots

    turn = [
        (g * parts + v, column_owner(g, v)) for g in range(groups.size) for v in range(parts)
    ]
    turned = lax.ppermute(hidden, ("dp", "vocab"), turn)

    weight = hold(head_weight)

    live_rows = (valid_rows == 1).astype(F32)
    squares = jnp.sum(jnp.square(hidden.astype(F32)), axis=1)[None]
    rounds = ring.meetings(lambda terms: sum(terms[1:], terms[0]))
    rounds.append(lambda x: groups.gather_chips(jnp.concatenate([x, live_rows[None]])))
    rounds.append(lambda x: jnp.concatenate([x, groups.swap(x)], axis=0))
    for round in rounds[:2]:
        squares = round(squares)
    turned = after(turned, squares, weight)
    late = rounds[2:]
    exchanged = [squares]

    def seen(step, arrivals):
        if step < len(late):
            exchanged.append(late[step](after(exchanged[-1], arrivals)))

    blocks = [ring.gather(chunk(turned, h), h, seen if h == 0 else None) for h in range(CHUNKS)]
    both = exchanged[-1]
    valid_count = jnp.sum(both[:, 1])
    row_factor = lax.rsqrt(both[:, 0] / model_width + 1e-05)

    targets = target_logits.astype(F32)
    target_top = jnp.max(targets, axis=1)
    target_total = jnp.sum(jnp.exp(targets - target_top[:, None]), axis=1)

    def merge_totals(terms):
        top = functools.reduce(jnp.maximum, [x[0] for x in terms])
        return jnp.stack([top, sum(x[1] * jnp.exp(x[0] - top) for x in terms)])

    tree_rows = jnp.arange(group_rows, dtype=jnp.int32) // TREE * TREE + parents
    own_chosen = features.at[tree_rows].get(mode="promise_in_bounds")

    gain = lax.dynamic_slice(norm_gain, (gain_start,), (slice_width,)).reshape(1, slice_width)
    row_weight = 1048576.0 * live_rows / valid_count
    lane = lax.broadcasted_iota(jnp.uint32, (chunk_rows, LANES), 1)

    keep, send, *pieces = project(
        index["place"], blocks, row_factor[:, :, None], gain, weight, piece_rows
    )
    other = groups.swap(send)

    def chip_sum(d):
        rows = slice(d * group_rows, (d + 1) * group_rows)
        return keep[rows] + other[rows]

    came = [groups.shift(chip_sum(d), d) for d in range(1, groups.chips)]
    logits = sum(came, chip_sum(0))
    top = jnp.max(logits, axis=1)
    total = jnp.sum(jnp.exp(logits - top[:, None]), axis=1)
    mine = jnp.stack([jnp.concatenate([top, target_top]), jnp.concatenate([total, target_total])])
    met = ring.meet(mine, merge_totals)
    scale = jnp.exp(mine[0] - met[0]) / met[1]
    draft_scale, target_scale = scale[:group_rows], scale[group_rows:]

    grads = []
    for h in range(CHUNKS):
        factor = row_factor[:, h * chunk_rows : (h + 1) * chunk_rows]
        own = chunk(logits, h)
        draft_probs = jnp.exp(own - chunk(top, h)[:, None]) * chunk(draft_scale, h)[:, None]
        target_probs = (
            jnp.exp(chunk(targets, h) - chunk(target_top, h)[:, None])
            * chunk(target_scale, h)[:, None]
        )
        logit_grad = chunk(row_weight, h)[:, None] * (draft_probs - target_probs)
        logit_grad = lax.reduce_precision(logit_grad, 8, 7)
        dot_part = jnp.sum(logit_grad * own, axis=1)
        dot_high = lax.reduce_precision(dot_part, 8, 7)
        dot_low = dot_part - dot_high
        lanes = jnp.where(lane == own_lane, dot_high[:, None], 0.0) + jnp.where(
            lane == own_lane + 1, dot_low[:, None], 0.0
        )
        message = jnp.concatenate([logit_grad.astype(BF16), lanes.astype(BF16)], axis=1)
        if h > 0:
            message = after(message, mine)
        mine = groups.gather_chips(message)
        mine, other = [x.reshape(step_rows // CORES, -1) for x in (mine, groups.swap(mine))]
        normed_grad = back(index["turn"], mine, other, weight, piece_rows)
        if h == CHUNKS - 1:
            chosen = after(own_chosen, normed_grad).reshape(CHUNKS, chunk_rows, -1)
            chosen = groups.gather(chosen).transpose(1, 0, 2, 3).reshape(CHUNKS * step_rows, -1)

        def part(t):
            first = t % parts * piece_rows
            return normed_grad[first : first + piece_rows]

        summed = ring.scatter_sum(part, h)
        own_factor = lax.dynamic_slice(factor, (own_entry, own_first), (1, piece_rows))[0]
        row_dot = jnp.sum(summed[:, slice_width:], axis=1) / own_factor
        grad_piece = (
            own_factor[:, None] * gain * summed[:, :slice_width]
            - pieces[h].astype(F32) * (own_factor**3 * row_dot / model_width)[:, None]
        ).astype(BF16)
        grads.append(ring.gather(grad_piece, h))

    grad_joining, grad_share = outer(index["pieces"], chosen, grads, group_rows // slots)
    return (grad_share, grad_joining)


def solution(mesh):
    placed = (
        P("dp", "vocab"),
        P(),
        P("vocab", "dp"),
        P("dp", "vocab"),
        P("dp"),
        P("dp"),
        P("dp", "vocab"),
    )
    return jax.shard_map(
        body,
        mesh=mesh,
        in_specs=placed,
        out_specs=(P("vocab", "dp"), P("dp", "vocab")),
        check_vma=False,
    )
```

```python
import functools

import jax
import jax.numpy as jnp
import numpy as np
from jax import lax
from jax.experimental import pallas as pl
from jax.experimental.pallas import tpu as pltpu
from jax.sharding import PartitionSpec as P

TREE = 64
CORES = 2
LANES = 128
CHUNKS = 2
F32 = jnp.float32
BF16 = jnp.bfloat16


def ring_order(rows, columns):
    if columns == 1 or rows == 1:
        return list(range(rows * columns))
    order = [r * columns for r in range(rows)]
    for step in range(rows):
        r = rows - 1 - step
        line = [r * columns + c for c in range(1, columns)]
        order += line if step % 2 == 0 else line[::-1]
    return order


class Ring:
    def __init__(self, size, columns):
        self.size = size
        self.columns = columns
        self.half = size // 2
        self.order = ring_order(size // columns, columns)
        self.place = [0] * size
        for position, index in enumerate(self.order):
            self.place[index] = position

    def shift(self, x, step):
        size, order = self.size, self.order
        return lax.ppermute(
            x, "vocab", [(order[p], order[(p + step) % size]) for p in range(size)]
        )

    def partner(self, x, bit):
        return lax.ppermute(x, "vocab", [(v, v ^ bit) for v in range(self.size)])

    def meetings(self, merge):
        near = [bit for bit in range(1, self.columns)]
        far = [bit for bit in range(self.columns, self.size, self.columns)]
        return [
            lambda x, bits=bits: merge([x] + [self.partner(x, bit) for bit in bits])
            for bits in (near, far)
        ]

    def meet(self, x, merge):
        for round in self.meetings(merge):
            x = round(x)
        return x

    def reach(self, h):
        return (self.half, self.half - 1) if h % 2 == 0 else (self.half - 1, self.half)

    def gather(self, block, h, seen=None):
        far_ahead, far_behind = self.reach(h)
        ahead, behind = [block], [block]
        for step in range(self.half):
            if step < far_ahead:
                ahead.append(self.shift(ahead[-1], 1))
            if step < far_behind:
                behind.append(self.shift(behind[-1], -1))
            if seen:
                seen(step, (ahead[-1], behind[-1]))
        return ahead[1:][::-1] + [block] + behind[1:]

    def sources(self, vocab, h):
        p, far_ahead = self.place[vocab], self.reach(h)[0]
        return [(p + k - far_ahead) % self.size for k in range(self.size)]

    def scatter_sum(self, part, h, wait):
        far_ahead, far_behind = self.reach(h)
        got_ahead = got_behind = None
        for step in range(self.half, 0, -1):
            if step <= far_ahead:
                ahead = part(step) if got_ahead is None else part(step) + got_ahead
                got_ahead = self.shift(ahead.astype(BF16), 1).astype(F32)
            if step <= far_behind:
                behind = part(-step) if got_behind is None else part(-step) + got_behind
                got_behind = self.shift(behind.astype(BF16), -1).astype(F32)
            if step == self.half:
                got_ahead, got_behind = [
                    x if x is None else after(x, wait) for x in (got_ahead, got_behind)
                ]
        return part(0) + got_ahead + got_behind


class Groups:
    def __init__(self, size):
        self.size = size
        self.chips = size // CORES

    def entry(self, index, group):
        chip = (group // CORES - index // CORES) % self.chips
        return (group % CORES ^ index % CORES) * self.chips + chip

    def swap(self, x):
        return lax.ppermute(x, "dp", [(i, i ^ 1) for i in range(self.size)])

    def shift(self, x, step):
        size = self.size
        return lax.ppermute(x, "dp", [(i, (i + CORES * step) % size) for i in range(size)])

    def gather_chips(self, block):
        return jnp.stack([block] + [self.shift(block, -d) for d in range(1, self.chips)])

    def gather_halves(self, block):
        mine = self.gather_chips(block)
        return mine, self.swap(mine)

    def gather(self, block):
        return jnp.concatenate(self.gather_halves(block), axis=0)


VMEM = pl.BlockSpec(memory_space=pltpu.VMEM)
SMEM = pl.BlockSpec(memory_space=pltpu.SMEM)


def choose_kernel(parents_ref, features_ref, out_ref):
    rows = features_ref.shape[0]
    from_row = lax.broadcasted_iota(jnp.int32, (rows, rows), 0)
    row = lax.broadcasted_iota(jnp.int32, (rows, rows), 1)
    chosen = from_row == row // TREE * TREE + parents_ref[...]
    out_ref[...] = lax.dot_general(
        chosen.astype(BF16),
        features_ref[...],
        (((0,), (0,)), ((), ())),
        preferred_element_type=F32,
    ).astype(BF16)


def choose(parents, features):
    return pl.pallas_call(
        choose_kernel,
        in_specs=[VMEM, VMEM],
        out_specs=VMEM,
        out_shape=jax.ShapeDtypeStruct(features.shape, BF16),
        compiler_params=pltpu.CompilerParams(vmem_limit_bytes=12 * 2**20),
        cost_estimate=pl.CostEstimate(
            flops=2 * features.shape[0] * features.size,
            bytes_accessed=4 * features.size,
            transcendentals=0,
        ),
    )(parents.reshape(1, -1), features)


def hold_kernel(weight_ref, held_ref, sems):
    tile = weight_ref.shape[0] // sems.shape[0]
    copies = [
        pltpu.make_async_copy(
            weight_ref.at[pl.ds(n * tile, tile), :], held_ref.at[pl.ds(n * tile, tile), :], sems.at[n]
        )
        for n in range(sems.shape[0])
    ]
    for copy in copies:
        copy.start()
    for copy in copies:
        copy.wait()


def hold(weight):
    return pl.pallas_call(
        hold_kernel,
        in_specs=[pl.BlockSpec(memory_space=pltpu.HBM)],
        out_specs=VMEM,
        out_shape=jax.ShapeDtypeStruct(weight.shape, weight.dtype),
        scratch_shapes=[pltpu.SemaphoreType.DMA((4,))],
        compiler_params=pltpu.CompilerParams(vmem_limit_bytes=12 * 2**20),
        cost_estimate=pl.CostEstimate(flops=0, bytes_accessed=2 * weight.size, transcendentals=0),
    )(weight)


def project_kernel(count, tile, index_ref, factor_ref, gain_ref, weight_ref, *refs):
    blocks, refs = refs[: CHUNKS * count], refs[CHUNKS * count :]
    keep_ref, send_ref = refs[:CORES]
    piece_refs = refs[CORES : CORES + CHUNKS]
    raw_ref, turned_ref = refs[CORES + CHUNKS :]
    rows, width = blocks[0].shape
    group_rows = CHUNKS * rows
    piece = piece_refs[0].shape[0]
    half = keep_ref.shape[0]
    step = pl.program_id(0)

    @pl.when(step == 0)
    def _():
        for k, ref in enumerate(blocks):
            h, at = k // count, k + k // count * count
            start = pl.multiple_of(index_ref[at] * group_rows + h * rows, rows)
            column = pl.multiple_of(index_ref[at + count] * width, width)
            raw_ref[pl.ds(start, rows), pl.ds(column, width)] = ref[...]
        slab = min(raw_ref.shape[1], 256)
        for g in range(factor_ref.shape[0]):
            group = pl.ds(g * group_rows, group_rows)
            for first in range(0, raw_ref.shape[1], slab):
                columns = pl.ds(first, slab)
                values = raw_ref[group, columns].astype(F32) * gain_ref[:, columns]
                turned_ref[columns, group] = (values.T * factor_ref[g : g + 1, :]).astype(BF16)
        for h, ref in enumerate(piece_refs):
            start = pl.multiple_of(index_ref[2 * CHUNKS * count + h] * piece, piece)
            ref[...] = raw_ref[pl.ds(start, piece), :]

    rows = pl.ds(pl.multiple_of(step * tile, tile), tile)
    logits = jnp.dot(weight_ref[rows, :], turned_ref[...], preferred_element_type=F32).T
    keep_ref[...] = logits[:half]
    send_ref[...] = logits[half:]


def project(index, blocks, factor, gain, weight, piece_rows):
    vocab, depth = weight.shape
    all_rows = factor.shape[0] * factor.shape[1]
    half = all_rows // CORES
    tile = min(vocab, 512)
    out = jax.ShapeDtypeStruct((half, vocab), F32)
    piece = jax.ShapeDtypeStruct((piece_rows, depth), BF16)
    return pl.pallas_call(
        functools.partial(project_kernel, len(blocks[0]), tile),
        grid=(vocab // tile,),
        in_specs=[SMEM] + [VMEM] * (3 + CHUNKS * len(blocks[0])),
        out_specs=[pl.BlockSpec((half, tile), lambda n: (0, n))] * CORES
        + [pl.BlockSpec((piece_rows, depth), lambda n: (0, 0))] * CHUNKS,
        out_shape=[out] * CORES + [piece] * CHUNKS,
        scratch_shapes=[
            pltpu.VMEM((all_rows, depth), BF16),
            pltpu.VMEM((depth, all_rows), BF16),
        ],
        compiler_params=pltpu.CompilerParams(vmem_limit_bytes=28 * 2**20),
        cost_estimate=pl.CostEstimate(
            flops=2 * all_rows * depth * vocab,
            bytes_accessed=2 * vocab * depth + all_rows * (2 * depth + 4 * vocab),
            transcendentals=0,
        ),
    )(index, factor, gain, weight, *[x for chunk in blocks for x in chunk])


def back_kernel(piece, tile, index_ref, mine_ref, other_ref, weight_ref, out_ref, grad_ref):
    vocab = weight_ref.shape[0]
    half = mine_ref.shape[0]
    depth = out_ref.shape[1] - LANES
    step = pl.program_id(0)

    @pl.when(step == 0)
    def _():
        for k in range(2 * half // piece):
            ref, first = (mine_ref, k * piece) if k * piece < half else (other_ref, k * piece - half)
            rows = pl.ds(pl.multiple_of(index_ref[k] * piece, piece), piece)
            grad_ref[rows, :] = ref[pl.ds(first, piece), :vocab]
            out_ref[rows, pl.ds(depth, LANES)] = ref[pl.ds(first, piece), vocab:].astype(F32)

    columns = pl.ds(pl.multiple_of(step * tile, tile), tile)
    out_ref[:, columns] = jnp.dot(
        grad_ref[...], weight_ref[:, columns], preferred_element_type=F32
    )


def back(index, mine, other, weight, piece_rows):
    vocab, depth = weight.shape
    all_rows = mine.shape[0] + other.shape[0]
    tile = min(depth, 512)
    return pl.pallas_call(
        functools.partial(back_kernel, piece_rows, tile),
        grid=(depth // tile,),
        in_specs=[SMEM, VMEM, VMEM, VMEM],
        out_specs=pl.BlockSpec((all_rows, depth + LANES), lambda n: (0, 0)),
        out_shape=jax.ShapeDtypeStruct((all_rows, depth + LANES), F32),
        scratch_shapes=[pltpu.VMEM((all_rows, vocab), BF16)],
        compiler_params=pltpu.CompilerParams(vmem_limit_bytes=24 * 2**20),
        cost_estimate=pl.CostEstimate(
            flops=2 * all_rows * depth * vocab,
            bytes_accessed=2 * vocab * depth + all_rows * (2 * vocab + 4 * depth),
            transcendentals=0,
        ),
    )(index, mine, other, weight)


def outer_kernel(count, tile, index_ref, chosen_ref, *refs):
    pieces, (out_ref, share_ref, grad_ref) = refs[:-3], refs[-3:]
    rows = pieces[0].shape[0]
    share = share_ref.shape[0]
    step = pl.program_id(0)

    @pl.when(step == 0)
    def _():
        for k, ref in enumerate(pieces):
            start = pl.multiple_of((k // count * count + index_ref[k]) * rows, rows)
            grad_ref[pl.ds(start, rows), :] = ref[...]
        start = pl.multiple_of(index_ref[len(pieces)] * share, share)
        share_ref[...] = grad_ref[pl.ds(start, share), :]

    columns = pl.ds(pl.multiple_of(step * tile, tile), tile)
    out_ref[...] = lax.dot_general(
        grad_ref[:, columns], chosen_ref[...], (((0,), (0,)), ((), ())), preferred_element_type=F32
    )


def outer(index, chosen, chunks, share_rows):
    depth = chunks[0][0].shape[1]
    all_rows, joined = chosen.shape
    tile = min(depth, 256)
    pieces = [x for chunk in chunks for x in chunk]
    return pl.pallas_call(
        functools.partial(outer_kernel, len(chunks[0]), tile),
        grid=(depth // tile,),
        in_specs=[SMEM, VMEM] + [VMEM] * len(pieces),
        out_specs=[
            pl.BlockSpec((tile, joined), lambda n: (n, 0)),
            pl.BlockSpec((share_rows, depth), lambda n: (0, 0)),
        ],
        out_shape=[
            jax.ShapeDtypeStruct((depth, joined), F32),
            jax.ShapeDtypeStruct((share_rows, depth), BF16),
        ],
        scratch_shapes=[pltpu.VMEM((all_rows, depth), BF16)],
        compiler_params=pltpu.CompilerParams(vmem_limit_bytes=40 * 2**20),
        cost_estimate=pl.CostEstimate(
            flops=2 * all_rows * depth * joined,
            bytes_accessed=4 * depth * joined + 2 * all_rows * (depth + joined),
            transcendentals=0,
        ),
    )(index, chosen, *pieces)


def device_table(groups, ring, slots, widths):
    group_rows, chunk_rows, piece_rows, slice_width = widths
    parts = ring.size
    step_rows = piece_rows * parts
    share_rows = group_rows // slots
    table = {}

    def add(name, values):
        table.setdefault(name, []).append(values)

    for g in range(groups.size):
        for v in range(parts):
            p = ring.place[v]
            place = []
            for h in range(CHUNKS):
                held = [ring.order[q] for q in ring.sources(v, h)]
                for i in held:
                    group = i // slots % groups.chips * CORES + i // slots // groups.chips
                    place.append(groups.entry(g, group))
                place += [i % slots for i in held]
            for h in range(CHUNKS):
                start = p * piece_rows
                start = start // chunk_rows * group_rows + h * chunk_rows + start % chunk_rows
                place.append(start // piece_rows)
            add("place", place)
            entry = groups.entry(g, v * share_rows // group_rows)
            first = v * share_rows % group_rows
            start = first // chunk_rows * step_rows + entry * chunk_rows + first % chunk_rows
            pieces = [q for h in range(CHUNKS) for q in ring.sources(v, h)]
            add("pieces", pieces + [start // share_rows])
            add("turn", [(k - p) % parts for k in range(parts)])
            start = p * piece_rows
            add("starts", [g * slice_width, start // chunk_rows, start % chunk_rows, 2 * p, 2 * p + 1])
    return {
        name: np.asarray(rows, np.int32).reshape(groups.size, parts, -1)
        for name, rows in table.items()
    }


def after(x, *others):
    return lax.optimization_barrier((x, others))[0]


def body(hidden, norm_gain, head_weight, target_logits, valid_rows, parents, features):
    groups = Groups(lax.axis_size("dp"))
    parts = lax.axis_size("vocab")
    ring = Ring(parts, groups.chips)
    group_rows, block_width = hidden.shape
    chunk_rows = group_rows // CHUNKS
    step_rows = groups.size * chunk_rows
    piece_rows = step_rows // parts
    model_width = block_width * parts
    slots = parts // groups.size
    slice_width = block_width * slots
    vocab_width = target_logits.shape[1]

    table = device_table(
        groups, ring, slots, (group_rows, chunk_rows, piece_rows, slice_width)
    )
    own = lax.dynamic_slice(
        jnp.asarray(np.concatenate(list(table.values()), axis=2)),
        (lax.axis_index("dp"), lax.axis_index("vocab"), 0),
        (1, 1, sum(rows.shape[2] for rows in table.values())),
    ).reshape(-1)
    index, first = {}, 0
    for name, rows in table.items():
        index[name] = own[first : first + rows.shape[2]]
        first += rows.shape[2]
    gain_start, own_entry, own_first, high_lane, low_lane = [
        index["starts"].astype(jnp.uint32)[k] for k in range(5)
    ]

    def chunk(x, h):
        return x[h * chunk_rows : (h + 1) * chunk_rows]

    def column_owner(g, v):
        far = g % CORES * groups.chips + g // CORES
        return v // slots * parts + far * slots + v % slots

    turn = [
        (g * parts + v, column_owner(g, v)) for g in range(groups.size) for v in range(parts)
    ]
    turned = lax.ppermute(hidden, ("dp", "vocab"), turn)

    weight = hold(head_weight)

    live_rows = (valid_rows == 1).astype(F32)
    squares = jnp.sum(jnp.square(hidden.astype(F32)), axis=1)[None]
    rounds = ring.meetings(lambda terms: sum(terms[1:], terms[0]))
    rounds.append(lambda x: groups.gather_chips(jnp.concatenate([x, live_rows[None]])))
    rounds.append(lambda x: jnp.concatenate([x, groups.swap(x)], axis=0))
    for round in rounds[:2]:
        squares = round(squares)
    turned = after(turned, squares, weight)
    late = rounds[2:]
    exchanged = [squares]

    def seen(step, arrivals):
        if step < len(late):
            exchanged.append(late[step](after(exchanged[-1], arrivals)))

    blocks = [ring.gather(chunk(turned, h), h, seen if h == 0 else None) for h in range(CHUNKS)]
    both = exchanged[-1]
    valid_count = jnp.sum(both[:, 1])
    row_factor = lax.rsqrt(both[:, 0] / model_width + 1e-05)

    targets = target_logits.astype(F32)
    target_top = jnp.max(targets, axis=1)
    target_total = jnp.sum(jnp.exp(targets - target_top[:, None]), axis=1)

    def merge_totals(terms):
        top = functools.reduce(jnp.maximum, [x[0] for x in terms])
        return jnp.stack([top, sum(x[1] * jnp.exp(x[0] - top) for x in terms)])

    own_chosen = choose(parents, features)

    gain = lax.dynamic_slice(norm_gain, (gain_start,), (slice_width,)).reshape(1, slice_width)
    row_weight = 1048576.0 * live_rows / valid_count
    lane = lax.broadcasted_iota(jnp.uint32, (chunk_rows, LANES), 1)

    keep, send, *pieces = project(
        index["place"], blocks, row_factor, gain, weight, piece_rows
    )
    other = groups.swap(send)

    def chip_sum(d):
        rows = slice(d * group_rows, (d + 1) * group_rows)
        return keep[rows] + other[rows]

    came = [groups.shift(chip_sum(d), d) for d in range(1, groups.chips)]
    logits = sum(came, chip_sum(0))
    top = jnp.max(logits, axis=1)
    total = jnp.sum(jnp.exp(logits - top[:, None]), axis=1)
    mine = jnp.stack([jnp.concatenate([top, target_top]), jnp.concatenate([total, target_total])])
    met = ring.meet(mine, merge_totals)
    scale = jnp.exp(mine[0] - met[0]) / met[1]
    draft_scale, target_scale = scale[:group_rows], scale[group_rows:]

    products = []
    for h in range(CHUNKS):
        own = chunk(logits, h)
        draft_probs = jnp.exp(own - chunk(top, h)[:, None]) * chunk(draft_scale, h)[:, None]
        target_probs = (
            jnp.exp(chunk(targets, h) - chunk(target_top, h)[:, None])
            * chunk(target_scale, h)[:, None]
        )
        logit_grad = chunk(row_weight, h)[:, None] * (draft_probs - target_probs)
        logit_grad = lax.reduce_precision(logit_grad, 8, 7)
        dot_part = jnp.sum(logit_grad * own, axis=1)
        dot_high = lax.reduce_precision(dot_part, 8, 7)
        dot_low = dot_part - dot_high
        lanes = jnp.where(lane == high_lane, dot_high[:, None], 0.0) + jnp.where(
            lane == low_lane, dot_low[:, None], 0.0
        )
        message = jnp.concatenate([logit_grad.astype(BF16), lanes.astype(BF16)], axis=1)
        if h > 0:
            message = after(message, mine)
        mine = groups.gather_chips(message)
        mine, other = [x.reshape(step_rows // CORES, -1) for x in (mine, groups.swap(mine))]
        products.append(back(index["turn"], mine, other, weight, piece_rows))
    chosen = after(own_chosen, products[-1]).reshape(CHUNKS, chunk_rows, -1)
    chosen = groups.gather(chosen).transpose(1, 0, 2, 3).reshape(CHUNKS * step_rows, -1)

    grads = []
    for h, normed_grad in enumerate(products):

        def part(t):
            first = t % parts * piece_rows
            return normed_grad[first : first + piece_rows]

        summed = ring.scatter_sum(part, h, products)
        factor = row_factor[:, h * chunk_rows : (h + 1) * chunk_rows]
        own_factor = lax.dynamic_slice(factor, (own_entry, own_first), (1, piece_rows))[0]
        row_dot = jnp.sum(summed[:, slice_width:], axis=1) / own_factor
        grad_piece = (
            own_factor[:, None] * gain * summed[:, :slice_width]
            - pieces[h].astype(F32) * (own_factor**3 * row_dot / model_width)[:, None]
        ).astype(BF16)
        grads.append(ring.gather(grad_piece, h))

    grad_joining, grad_share = outer(index["pieces"], chosen, grads, group_rows // slots)
    return (grad_share, grad_joining)


def solution(mesh):
    placed = (
        P("dp", "vocab"),
        P(),
        P("vocab", "dp"),
        P("dp", "vocab"),
        P("dp"),
        P("dp"),
        P("dp", "vocab"),
    )
    return jax.shard_map(
        body,
        mesh=mesh,
        in_specs=placed,
        out_specs=(P("vocab", "dp"), P("dp", "vocab")),
        check_vma=False,
    )
```

```python
import functools

import jax
import jax.numpy as jnp
import numpy as np
from jax import lax
from jax.experimental import pallas as pl
from jax.experimental.pallas import tpu as pltpu
from jax.sharding import PartitionSpec as P

TREE = 64
CORES = 2
LANES = 128
CHUNKS = 2
F32 = jnp.float32
BF16 = jnp.bfloat16


def ring_order(rows, columns):
    if columns == 1 or rows == 1:
        return list(range(rows * columns))
    order = [r * columns for r in range(rows)]
    for step in range(rows):
        r = rows - 1 - step
        line = [r * columns + c for c in range(1, columns)]
        order += line if step % 2 == 0 else line[::-1]
    return order


class Ring:
    def __init__(self, size, columns):
        self.size = size
        self.columns = columns
        self.half = size // 2
        self.order = ring_order(size // columns, columns)
        self.place = [0] * size
        for position, index in enumerate(self.order):
            self.place[index] = position

    def shift(self, x, step):
        size, order = self.size, self.order
        return lax.ppermute(
            x, "vocab", [(order[p], order[(p + step) % size]) for p in range(size)]
        )

    def partner(self, x, bit):
        return lax.ppermute(x, "vocab", [(v, v ^ bit) for v in range(self.size)])

    def meetings(self, merge):
        near = [bit for bit in range(1, self.columns)]
        far = [bit for bit in range(self.columns, self.size, self.columns)]
        return [
            lambda x, bits=bits: merge([x] + [self.partner(x, bit) for bit in bits])
            for bits in (near, far)
        ]

    def meet(self, x, merge):
        for round in self.meetings(merge):
            x = round(x)
        return x

    def reach(self, h):
        return (self.half, self.half - 1) if h % 2 == 0 else (self.half - 1, self.half)

    def gather(self, block, h, seen=None):
        far_ahead, far_behind = self.reach(h)
        ahead, behind = [block], [block]
        for step in range(self.half):
            if step < far_ahead:
                ahead.append(self.shift(ahead[-1], 1))
            if step < far_behind:
                behind.append(self.shift(behind[-1], -1))
            if seen:
                seen(step, (ahead[-1], behind[-1]))
        return ahead[1:][::-1] + [block] + behind[1:]

    def sources(self, vocab, h):
        p, far_ahead = self.place[vocab], self.reach(h)[0]
        return [(p + k - far_ahead) % self.size for k in range(self.size)]

    def scatter_sum(self, part, h):
        far_ahead, far_behind = self.reach(h)
        got_ahead = got_behind = None
        for step in range(self.half, 0, -1):
            if step <= far_ahead:
                ahead = part(step) if got_ahead is None else part(step) + got_ahead
                got_ahead = self.shift(ahead.astype(BF16), 1).astype(F32)
            if step <= far_behind:
                behind = part(-step) if got_behind is None else part(-step) + got_behind
                got_behind = self.shift(behind.astype(BF16), -1).astype(F32)
        return part(0) + got_ahead + got_behind


class Groups:
    def __init__(self, size):
        self.size = size
        self.chips = size // CORES

    def entry(self, index, group):
        chip = (group // CORES - index // CORES) % self.chips
        return (group % CORES ^ index % CORES) * self.chips + chip

    def swap(self, x):
        return lax.ppermute(x, "dp", [(i, i ^ 1) for i in range(self.size)])

    def shift(self, x, step):
        size = self.size
        return lax.ppermute(x, "dp", [(i, (i + CORES * step) % size) for i in range(size)])

    def gather_chips(self, block):
        return jnp.stack([block] + [self.shift(block, -d) for d in range(1, self.chips)])

    def gather_halves(self, block):
        mine = self.gather_chips(block)
        return mine, self.swap(mine)

    def gather(self, block):
        return jnp.concatenate(self.gather_halves(block), axis=0)


VMEM = pl.BlockSpec(memory_space=pltpu.VMEM)
SMEM = pl.BlockSpec(memory_space=pltpu.SMEM)


def choose_kernel(parents_ref, features_ref, out_ref):
    rows = features_ref.shape[0]
    from_row = lax.broadcasted_iota(jnp.int32, (rows, rows), 0)
    row = lax.broadcasted_iota(jnp.int32, (rows, rows), 1)
    chosen = from_row == row // TREE * TREE + parents_ref[...]
    out_ref[...] = lax.dot_general(
        chosen.astype(BF16),
        features_ref[...],
        (((0,), (0,)), ((), ())),
        preferred_element_type=F32,
    ).astype(BF16)


def choose(parents, features):
    return pl.pallas_call(
        choose_kernel,
        in_specs=[VMEM, VMEM],
        out_specs=VMEM,
        out_shape=jax.ShapeDtypeStruct(features.shape, BF16),
        compiler_params=pltpu.CompilerParams(vmem_limit_bytes=12 * 2**20),
        cost_estimate=pl.CostEstimate(
            flops=2 * features.shape[0] * features.size,
            bytes_accessed=4 * features.size,
            transcendentals=0,
        ),
    )(parents.reshape(1, -1), features)


def hold_kernel(weight_ref, held_ref, sems):
    tile = weight_ref.shape[0] // sems.shape[0]
    copies = [
        pltpu.make_async_copy(
            weight_ref.at[pl.ds(n * tile, tile), :], held_ref.at[pl.ds(n * tile, tile), :], sems.at[n]
        )
        for n in range(sems.shape[0])
    ]
    for copy in copies:
        copy.start()
    for copy in copies:
        copy.wait()


def hold(weight):
    return pl.pallas_call(
        hold_kernel,
        in_specs=[pl.BlockSpec(memory_space=pltpu.HBM)],
        out_specs=VMEM,
        out_shape=jax.ShapeDtypeStruct(weight.shape, weight.dtype),
        scratch_shapes=[pltpu.SemaphoreType.DMA((4,))],
        compiler_params=pltpu.CompilerParams(vmem_limit_bytes=12 * 2**20),
        cost_estimate=pl.CostEstimate(flops=0, bytes_accessed=2 * weight.size, transcendentals=0),
    )(weight)


def project_kernel(count, tile, index_ref, factor_ref, gain_ref, weight_ref, *refs):
    blocks, refs = refs[: CHUNKS * count], refs[CHUNKS * count :]
    keep_ref, send_ref = refs[:CORES]
    piece_refs = refs[CORES : CORES + CHUNKS]
    raw_ref, turned_ref = refs[CORES + CHUNKS :]
    rows, width = blocks[0].shape
    group_rows = CHUNKS * rows
    piece = piece_refs[0].shape[0]
    half = keep_ref.shape[0]
    step = pl.program_id(0)

    @pl.when(step == 0)
    def _():
        for k, ref in enumerate(blocks):
            h, at = k // count, k + k // count * count
            start = pl.multiple_of(index_ref[at] * group_rows + h * rows, rows)
            column = pl.multiple_of(index_ref[at + count] * width, width)
            raw_ref[pl.ds(start, rows), pl.ds(column, width)] = ref[...]
        slab = min(raw_ref.shape[1], 256)
        for g in range(factor_ref.shape[0]):
            group = pl.ds(g * group_rows, group_rows)
            for first in range(0, raw_ref.shape[1], slab):
                columns = pl.ds(first, slab)
                values = raw_ref[group, columns].astype(F32) * gain_ref[:, columns]
                turned_ref[columns, group] = (values.T * factor_ref[g : g + 1, :]).astype(BF16)
        for h, ref in enumerate(piece_refs):
            start = pl.multiple_of(index_ref[2 * CHUNKS * count + h] * piece, piece)
            ref[...] = raw_ref[pl.ds(start, piece), :]

    rows = pl.ds(pl.multiple_of(step * tile, tile), tile)
    logits = jnp.dot(weight_ref[rows, :], turned_ref[...], preferred_element_type=F32).T
    keep_ref[...] = logits[:half]
    send_ref[...] = logits[half:]


def project(index, blocks, factor, gain, weight, piece_rows):
    vocab, depth = weight.shape
    all_rows = factor.shape[0] * factor.shape[1]
    half = all_rows // CORES
    tile = min(vocab, 512)
    out = jax.ShapeDtypeStruct((half, vocab), F32)
    piece = jax.ShapeDtypeStruct((piece_rows, depth), BF16)
    return pl.pallas_call(
        functools.partial(project_kernel, len(blocks[0]), tile),
        grid=(vocab // tile,),
        in_specs=[SMEM] + [VMEM] * (3 + CHUNKS * len(blocks[0])),
        out_specs=[pl.BlockSpec((half, tile), lambda n: (0, n))] * CORES
        + [pl.BlockSpec((piece_rows, depth), lambda n: (0, 0))] * CHUNKS,
        out_shape=[out] * CORES + [piece] * CHUNKS,
        scratch_shapes=[
            pltpu.VMEM((all_rows, depth), BF16),
            pltpu.VMEM((depth, all_rows), BF16),
        ],
        compiler_params=pltpu.CompilerParams(vmem_limit_bytes=28 * 2**20),
        cost_estimate=pl.CostEstimate(
            flops=2 * all_rows * depth * vocab,
            bytes_accessed=2 * vocab * depth + all_rows * (2 * depth + 4 * vocab),
            transcendentals=0,
        ),
    )(index, factor, gain, weight, *[x for chunk in blocks for x in chunk])


def back_kernel(piece, tile, index_ref, mine_ref, other_ref, weight_ref, *refs):
    out_refs, grad_ref = refs[:-1], refs[-1]
    vocab = weight_ref.shape[0]
    rows, depth = out_refs[0].shape[0], out_refs[0].shape[1] - LANES
    step = pl.program_id(0)
    groups, group_rows = mine_ref.shape[:2]
    chunk_rows = group_rows // CHUNKS

    @pl.when(step == 0)
    def _():
        for h, out_ref in enumerate(out_refs):
            for k in range(rows // piece):
                entry, first = k * piece // chunk_rows, k * piece % chunk_rows
                ref = mine_ref if entry < groups else other_ref
                source = (entry % groups, pl.ds(h * chunk_rows + first, piece))
                start = pl.multiple_of(index_ref[k] * piece, piece)
                grad_ref[pl.ds(h * rows + start, piece), :] = ref[source + (slice(0, vocab),)]
                lanes = ref[source + (slice(vocab, vocab + LANES),)]
                out_ref[pl.ds(start, piece), pl.ds(depth, LANES)] = lanes.astype(F32)

    columns = pl.ds(pl.multiple_of(step * tile, tile), tile)
    product = jnp.dot(grad_ref[...], weight_ref[:, columns], preferred_element_type=F32)
    for h, out_ref in enumerate(out_refs):
        out_ref[:, columns] = product[h * rows : (h + 1) * rows]


def back(index, mine, other, weight, piece_rows):
    vocab, depth = weight.shape
    all_rows = 2 * mine.shape[0] * mine.shape[1]
    tile = min(depth, 512)
    shape = (all_rows // CHUNKS, depth + LANES)
    return pl.pallas_call(
        functools.partial(back_kernel, piece_rows, tile),
        grid=(depth // tile,),
        in_specs=[SMEM, VMEM, VMEM, VMEM],
        out_specs=[pl.BlockSpec(shape, lambda n: (0, 0))] * CHUNKS,
        out_shape=[jax.ShapeDtypeStruct(shape, F32)] * CHUNKS,
        scratch_shapes=[pltpu.VMEM((all_rows, vocab), BF16)],
        compiler_params=pltpu.CompilerParams(vmem_limit_bytes=28 * 2**20),
        cost_estimate=pl.CostEstimate(
            flops=2 * all_rows * depth * vocab,
            bytes_accessed=2 * vocab * depth + all_rows * (2 * vocab + 4 * depth),
            transcendentals=0,
        ),
    )(index, mine, other, weight)


def outer_kernel(count, copies, index_ref, chosen_ref, *refs):
    pieces, (out_ref, share_ref, grad_ref, held_ref, sems) = refs[:-5], refs[-5:]
    rows = pieces[0].shape[0]
    share = share_ref.shape[0]
    step = pl.program_id(0)
    steps = pl.num_programs(0)
    slots, tile = held_ref.shape[:2]
    part = tile // copies

    def copy(step, k):
        slot = lax.rem(step, slots)
        start = pl.multiple_of(step * tile + k * part, part)
        return pltpu.make_async_copy(
            held_ref.at[slot, pl.ds(k * part, part), :],
            out_ref.at[pl.ds(start, part), :],
            sems.at[slot, k],
        )

    @pl.when(step == 0)
    def _():
        for k, ref in enumerate(pieces):
            start = pl.multiple_of((k // count * count + index_ref[k]) * rows, rows)
            grad_ref[pl.ds(start, rows), :] = ref[...]
        start = pl.multiple_of(index_ref[len(pieces)] * share, share)
        share_ref[...] = grad_ref[pl.ds(start, share), :]

    @pl.when(step >= slots)
    def _():
        for k in range(copies):
            copy(step - slots, k).wait()

    columns = pl.ds(pl.multiple_of(step * tile, tile), tile)
    held_ref[lax.rem(step, slots)] = lax.dot_general(
        grad_ref[:, columns], chosen_ref[...], (((0,), (0,)), ((), ())), preferred_element_type=F32
    )
    for k in range(copies):
        copy(step, k).start()

    @pl.when(step == steps - 1)
    def _():
        for back in range(slots - 1, -1, -1):
            for k in range(copies):
                copy(step - back, k).wait()


def outer(index, chosen, chunks, share_rows):
    depth = chunks[0][0].shape[1]
    all_rows, joined = chosen.shape
    tile = min(depth // 4, 256)
    slots, copies = 3, 4
    pieces = [x for chunk in chunks for x in chunk]
    return pl.pallas_call(
        functools.partial(outer_kernel, len(chunks[0]), copies),
        grid=(depth // tile,),
        in_specs=[SMEM, VMEM] + [VMEM] * len(pieces),
        out_specs=[
            pl.BlockSpec(memory_space=pl.ANY),
            pl.BlockSpec((share_rows, depth), lambda n: (0, 0)),
        ],
        out_shape=[
            jax.ShapeDtypeStruct((depth, joined), F32),
            jax.ShapeDtypeStruct((share_rows, depth), BF16),
        ],
        scratch_shapes=[
            pltpu.VMEM((all_rows, depth), BF16),
            pltpu.VMEM((slots, tile, joined), F32),
            pltpu.SemaphoreType.DMA((slots, copies)),
        ],
        compiler_params=pltpu.CompilerParams(vmem_limit_bytes=32 * 2**20),
        cost_estimate=pl.CostEstimate(
            flops=2 * all_rows * depth * joined,
            bytes_accessed=4 * depth * joined + 2 * all_rows * (depth + joined),
            transcendentals=0,
        ),
    )(index, chosen, *pieces)


def device_table(groups, ring, slots, widths):
    group_rows, chunk_rows, piece_rows, slice_width = widths
    parts = ring.size
    step_rows = piece_rows * parts
    share_rows = group_rows // slots
    table = {}

    def add(name, values):
        table.setdefault(name, []).append(values)

    for g in range(groups.size):
        for v in range(parts):
            p = ring.place[v]
            place = []
            for h in range(CHUNKS):
                held = [ring.order[q] for q in ring.sources(v, h)]
                for i in held:
                    group = i // slots % groups.chips * CORES + i // slots // groups.chips
                    place.append(groups.entry(g, group))
                place += [i % slots for i in held]
            for h in range(CHUNKS):
                start = p * piece_rows
                start = start // chunk_rows * group_rows + h * chunk_rows + start % chunk_rows
                place.append(start // piece_rows)
            add("place", place)
            entry = groups.entry(g, v * share_rows // group_rows)
            first = v * share_rows % group_rows
            start = first // chunk_rows * step_rows + entry * chunk_rows + first % chunk_rows
            pieces = [q for h in range(CHUNKS) for q in ring.sources(v, h)]
            add("pieces", pieces + [start // share_rows])
            add("turn", [(k - p) % parts for k in range(parts)])
            start = p * piece_rows
            add("starts", [g * slice_width, start // chunk_rows, start % chunk_rows, 2 * p, 2 * p + 1])
    return {
        name: np.asarray(rows, np.int32).reshape(groups.size, parts, -1)
        for name, rows in table.items()
    }


def after(x, *others):
    return lax.optimization_barrier((x, others))[0]


def body(hidden, norm_gain, head_weight, target_logits, valid_rows, parents, features):
    groups = Groups(lax.axis_size("dp"))
    parts = lax.axis_size("vocab")
    ring = Ring(parts, groups.chips)
    group_rows, block_width = hidden.shape
    chunk_rows = group_rows // CHUNKS
    step_rows = groups.size * chunk_rows
    piece_rows = step_rows // parts
    model_width = block_width * parts
    slots = parts // groups.size
    slice_width = block_width * slots
    vocab_width = target_logits.shape[1]

    table = device_table(
        groups, ring, slots, (group_rows, chunk_rows, piece_rows, slice_width)
    )
    own = lax.dynamic_slice(
        jnp.asarray(np.concatenate(list(table.values()), axis=2)),
        (lax.axis_index("dp"), lax.axis_index("vocab"), 0),
        (1, 1, sum(rows.shape[2] for rows in table.values())),
    ).reshape(-1)
    index, first = {}, 0
    for name, rows in table.items():
        index[name] = own[first : first + rows.shape[2]]
        first += rows.shape[2]
    gain_start, own_entry, own_first, high_lane, low_lane = [
        index["starts"].astype(jnp.uint32)[k] for k in range(5)
    ]

    def chunk(x, h):
        return x[h * chunk_rows : (h + 1) * chunk_rows]

    def column_owner(g, v):
        far = g % CORES * groups.chips + g // CORES
        return v // slots * parts + far * slots + v % slots

    turn = [
        (g * parts + v, column_owner(g, v)) for g in range(groups.size) for v in range(parts)
    ]
    turned = lax.ppermute(hidden, ("dp", "vocab"), turn)

    weight = hold(head_weight)

    live_rows = (valid_rows == 1).astype(F32)
    squares = jnp.sum(jnp.square(hidden.astype(F32)), axis=1)[None]
    rounds = ring.meetings(lambda terms: sum(terms[1:], terms[0]))
    rounds.append(lambda x: groups.gather_chips(jnp.concatenate([x, live_rows[None]])))
    rounds.append(lambda x: jnp.concatenate([x, groups.swap(x)], axis=0))
    for round in rounds[:2]:
        squares = round(squares)
    turned = after(turned, squares, weight)
    late = rounds[2:]
    exchanged = [squares]

    def seen(step, arrivals):
        if step < len(late):
            exchanged.append(late[step](after(exchanged[-1], arrivals)))

    blocks = [ring.gather(chunk(turned, h), h, seen if h == 0 else None) for h in range(CHUNKS)]
    both = exchanged[-1]
    valid_count = jnp.sum(both[:, 1])
    row_factor = lax.rsqrt(both[:, 0] / model_width + 1e-05)

    targets = lax.optimization_barrier(target_logits.astype(F32))
    target_top = jnp.max(targets, axis=1)
    target_total = jnp.sum(jnp.exp(targets - target_top[:, None]), axis=1)

    def merge_totals(terms):
        top = functools.reduce(jnp.maximum, [x[0] for x in terms])
        return jnp.stack([top, sum(x[1] * jnp.exp(x[0] - top) for x in terms)])

    own_chosen = choose(parents, features)

    gain = lax.dynamic_slice(norm_gain, (gain_start,), (slice_width,)).reshape(1, slice_width)
    row_weight = 1048576.0 * live_rows / valid_count
    lane = lax.broadcasted_iota(jnp.uint32, (group_rows, LANES), 1)

    keep, send, *pieces = project(
        index["place"], blocks, row_factor, gain, weight, piece_rows
    )
    other = groups.swap(send)

    def chip_sum(d):
        rows = slice(d * group_rows, (d + 1) * group_rows)
        return keep[rows] + other[rows]

    came = [groups.shift(chip_sum(d), d) for d in range(1, groups.chips)]
    logits = sum(came, chip_sum(0))
    top = jnp.max(logits, axis=1)
    total = jnp.sum(jnp.exp(logits - top[:, None]), axis=1)
    mine = jnp.stack([jnp.concatenate([top, target_top]), jnp.concatenate([total, target_total])])
    met = ring.meet(mine, merge_totals)
    scale = jnp.exp(mine[0] - met[0]) / met[1]
    draft_scale, target_scale = scale[:group_rows], scale[group_rows:]

    draft_probs = jnp.exp(logits - top[:, None]) * draft_scale[:, None]
    target_probs = jnp.exp(targets - target_top[:, None]) * target_scale[:, None]
    logit_grad = row_weight[:, None] * (draft_probs - target_probs)
    logit_grad = lax.reduce_precision(logit_grad, 8, 7)
    dot_part = jnp.sum(logit_grad * logits, axis=1)
    dot_high = lax.reduce_precision(dot_part, 8, 7)
    dot_low = dot_part - dot_high
    lanes = jnp.where(lane == high_lane, dot_high[:, None], 0.0) + jnp.where(
        lane == low_lane, dot_low[:, None], 0.0
    )
    mine, other = groups.gather_halves(
        jnp.concatenate([logit_grad.astype(BF16), lanes.astype(BF16)], axis=1)
    )
    products = back(index["turn"], mine, other, weight, piece_rows)
    chosen = after(own_chosen, products).reshape(CHUNKS, chunk_rows, -1)
    chosen = groups.gather(chosen).transpose(1, 0, 2, 3).reshape(CHUNKS * step_rows, -1)

    grads = []
    for h, normed_grad in enumerate(products):

        def part(t):
            first = t % parts * piece_rows
            return normed_grad[first : first + piece_rows]

        summed = ring.scatter_sum(part, h)
        factor = row_factor[:, h * chunk_rows : (h + 1) * chunk_rows]
        own_factor = lax.dynamic_slice(factor, (own_entry, own_first), (1, piece_rows))[0]
        row_dot = jnp.sum(summed[:, slice_width:], axis=1) / own_factor
        grad_piece = (
            own_factor[:, None] * gain * summed[:, :slice_width]
            - pieces[h].astype(F32) * (own_factor**3 * row_dot / model_width)[:, None]
        ).astype(BF16)
        grads.append(ring.gather(grad_piece, h))

    grad_joining, grad_share = outer(index["pieces"], chosen, grads, group_rows // slots)
    return (grad_share, grad_joining)


def solution(mesh):
    placed = (
        P("dp", "vocab"),
        P(),
        P("vocab", "dp"),
        P("dp", "vocab"),
        P("dp"),
        P("dp"),
        P("dp", "vocab"),
    )
    return jax.shard_map(
        body,
        mesh=mesh,
        in_specs=placed,
        out_specs=(P("vocab", "dp"), P("dp", "vocab")),
        check_vma=False,
    )
```

```python
import functools

import jax
import jax.numpy as jnp
import numpy as np
from jax import lax
from jax.experimental import pallas as pl
from jax.experimental.pallas import tpu as pltpu
from jax.sharding import PartitionSpec as P

TREE = 64
CORES = 2
LANES = 128
CHUNKS = 2
F32 = jnp.float32
BF16 = jnp.bfloat16


def ring_order(rows, columns):
    if columns == 1 or rows == 1:
        return list(range(rows * columns))
    order = [r * columns for r in range(rows)]
    for step in range(rows):
        r = rows - 1 - step
        line = [r * columns + c for c in range(1, columns)]
        order += line if step % 2 == 0 else line[::-1]
    return order


class Ring:
    def __init__(self, size, columns):
        self.size = size
        self.columns = columns
        self.half = size // 2
        self.order = ring_order(size // columns, columns)
        self.place = [0] * size
        for position, index in enumerate(self.order):
            self.place[index] = position

    def shift(self, x, step):
        size, order = self.size, self.order
        return lax.ppermute(
            x, "vocab", [(order[p], order[(p + step) % size]) for p in range(size)]
        )

    def partner(self, x, bit):
        return lax.ppermute(x, "vocab", [(v, v ^ bit) for v in range(self.size)])

    def meetings(self, merge):
        near = [bit for bit in range(1, self.columns)]
        far = [bit for bit in range(self.columns, self.size, self.columns)]
        return [
            lambda x, bits=bits: merge([x] + [self.partner(x, bit) for bit in bits])
            for bits in (near, far)
        ]

    def meet(self, x, merge):
        for round in self.meetings(merge):
            x = round(x)
        return x

    def reach(self, h):
        return (self.half, self.half - 1) if h % 2 == 0 else (self.half - 1, self.half)

    def gather(self, block, h, seen=None):
        far_ahead, far_behind = self.reach(h)
        ahead, behind = [block], [block]
        for step in range(self.half):
            if step < far_ahead:
                ahead.append(self.shift(ahead[-1], 1))
            if step < far_behind:
                behind.append(self.shift(behind[-1], -1))
            if seen:
                seen(step, (ahead[-1], behind[-1]))
        return ahead[1:][::-1] + [block] + behind[1:]

    def sources(self, vocab, h):
        p, far_ahead = self.place[vocab], self.reach(h)[0]
        return [(p + k - far_ahead) % self.size for k in range(self.size)]

    def scatter_sums(self, parts):
        got = [[None, None] for _ in parts]
        sent = []
        for step in range(self.half, 0, -1):
            for h, part in enumerate(parts):
                for way, reach in enumerate(self.reach(h)):
                    if step > reach:
                        continue
                    share = part(step if way == 0 else -step)
                    if got[h][way] is not None:
                        share = share + got[h][way].astype(F32)
                    share = share.astype(BF16)
                    if len(sent) >= len(parts):
                        share = after(share, sent[-len(parts)])
                    got[h][way] = self.shift(share, 1 if way == 0 else -1)
                sent.append([x for x in got[h] if x is not None])
        return [
            part(0) + got[h][0].astype(F32) + got[h][1].astype(F32) for h, part in enumerate(parts)
        ]


class Groups:
    def __init__(self, size):
        self.size = size
        self.chips = size // CORES

    def entry(self, index, group):
        chip = (group // CORES - index // CORES) % self.chips
        return (group % CORES ^ index % CORES) * self.chips + chip

    def swap(self, x):
        return lax.ppermute(x, "dp", [(i, i ^ 1) for i in range(self.size)])

    def shift(self, x, step):
        size = self.size
        return lax.ppermute(x, "dp", [(i, (i + CORES * step) % size) for i in range(size)])

    def gather_chips(self, block):
        return jnp.stack([block] + [self.shift(block, -d) for d in range(1, self.chips)])

    def gather_halves(self, block):
        mine = self.gather_chips(block)
        return mine, self.swap(mine)

    def gather(self, block):
        return jnp.concatenate(self.gather_halves(block), axis=0)


VMEM = pl.BlockSpec(memory_space=pltpu.VMEM)
SMEM = pl.BlockSpec(memory_space=pltpu.SMEM)


def choose_kernel(parents_ref, features_ref, out_ref):
    rows = features_ref.shape[0]
    from_row = lax.broadcasted_iota(jnp.int32, (rows, rows), 0)
    row = lax.broadcasted_iota(jnp.int32, (rows, rows), 1)
    chosen = from_row == row // TREE * TREE + parents_ref[...]
    out_ref[...] = lax.dot_general(
        chosen.astype(BF16),
        features_ref[...],
        (((0,), (0,)), ((), ())),
        preferred_element_type=F32,
    ).astype(BF16)


def choose(parents, features):
    return pl.pallas_call(
        choose_kernel,
        in_specs=[VMEM, VMEM],
        out_specs=VMEM,
        out_shape=jax.ShapeDtypeStruct(features.shape, BF16),
        compiler_params=pltpu.CompilerParams(vmem_limit_bytes=12 * 2**20),
        cost_estimate=pl.CostEstimate(
            flops=2 * features.shape[0] * features.size,
            bytes_accessed=4 * features.size,
            transcendentals=0,
        ),
    )(parents.reshape(1, -1), features)


def hold_kernel(weight_ref, held_ref, sems):
    tile = weight_ref.shape[0] // sems.shape[0]
    copies = [
        pltpu.make_async_copy(
            weight_ref.at[pl.ds(n * tile, tile), :], held_ref.at[pl.ds(n * tile, tile), :], sems.at[n]
        )
        for n in range(sems.shape[0])
    ]
    for copy in copies:
        copy.start()
    for copy in copies:
        copy.wait()


def hold(weight):
    return pl.pallas_call(
        hold_kernel,
        in_specs=[pl.BlockSpec(memory_space=pltpu.HBM)],
        out_specs=VMEM,
        out_shape=jax.ShapeDtypeStruct(weight.shape, weight.dtype),
        scratch_shapes=[pltpu.SemaphoreType.DMA((4,))],
        compiler_params=pltpu.CompilerParams(vmem_limit_bytes=12 * 2**20),
        cost_estimate=pl.CostEstimate(flops=0, bytes_accessed=2 * weight.size, transcendentals=0),
    )(weight)


def project_kernel(count, tile, index_ref, factor_ref, gain_ref, weight_ref, *refs):
    blocks, refs = refs[: CHUNKS * count], refs[CHUNKS * count :]
    keep_ref, send_ref = refs[:CORES]
    piece_refs = refs[CORES : CORES + CHUNKS]
    raw_ref, turned_ref = refs[CORES + CHUNKS :]
    rows, width = blocks[0].shape
    group_rows = CHUNKS * rows
    piece = piece_refs[0].shape[0]
    half = keep_ref.shape[0]
    step = pl.program_id(0)

    @pl.when(step == 0)
    def _():
        for k, ref in enumerate(blocks):
            h, at = k // count, k + k // count * count
            start = pl.multiple_of(index_ref[at] * group_rows + h * rows, rows)
            column = pl.multiple_of(index_ref[at + count] * width, width)
            raw_ref[pl.ds(start, rows), pl.ds(column, width)] = ref[...]
        slab = min(raw_ref.shape[1], 256)
        for g in range(factor_ref.shape[0]):
            group = pl.ds(g * group_rows, group_rows)
            for first in range(0, raw_ref.shape[1], slab):
                columns = pl.ds(first, slab)
                values = raw_ref[group, columns].astype(F32) * gain_ref[:, columns]
                turned_ref[columns, group] = (values.T * factor_ref[g : g + 1, :]).astype(BF16)
        for h, ref in enumerate(piece_refs):
            start = pl.multiple_of(index_ref[2 * CHUNKS * count + h] * piece, piece)
            ref[...] = raw_ref[pl.ds(start, piece), :]

    rows = pl.ds(pl.multiple_of(step * tile, tile), tile)
    logits = jnp.dot(weight_ref[rows, :], turned_ref[...], preferred_element_type=F32).T
    keep_ref[...] = logits[:half]
    send_ref[...] = logits[half:]


def project(index, blocks, factor, gain, weight, piece_rows):
    vocab, depth = weight.shape
    all_rows = factor.shape[0] * factor.shape[1]
    half = all_rows // CORES
    tile = min(vocab, 512)
    out = jax.ShapeDtypeStruct((half, vocab), F32)
    piece = jax.ShapeDtypeStruct((piece_rows, depth), BF16)
    return pl.pallas_call(
        functools.partial(project_kernel, len(blocks[0]), tile),
        grid=(vocab // tile,),
        in_specs=[SMEM] + [VMEM] * (3 + CHUNKS * len(blocks[0])),
        out_specs=[pl.BlockSpec((half, tile), lambda n: (0, n))] * CORES
        + [pl.BlockSpec((piece_rows, depth), lambda n: (0, 0))] * CHUNKS,
        out_shape=[out] * CORES + [piece] * CHUNKS,
        scratch_shapes=[
            pltpu.VMEM((all_rows, depth), BF16),
            pltpu.VMEM((depth, all_rows), BF16),
        ],
        compiler_params=pltpu.CompilerParams(vmem_limit_bytes=28 * 2**20),
        cost_estimate=pl.CostEstimate(
            flops=2 * all_rows * depth * vocab,
            bytes_accessed=2 * vocab * depth + all_rows * (2 * depth + 4 * vocab),
            transcendentals=0,
        ),
    )(index, factor, gain, weight, *[x for chunk in blocks for x in chunk])


def back_kernel(piece, tile, index_ref, mine_ref, other_ref, weight_ref, *refs):
    out_refs, grad_ref = refs[:-1], refs[-1]
    vocab = weight_ref.shape[0]
    rows, depth = out_refs[0].shape[0], out_refs[0].shape[1] - LANES
    step = pl.program_id(0)
    groups, group_rows = mine_ref.shape[:2]
    chunk_rows = group_rows // CHUNKS

    @pl.when(step == 0)
    def _():
        for h, out_ref in enumerate(out_refs):
            for k in range(rows // piece):
                entry, first = k * piece // chunk_rows, k * piece % chunk_rows
                ref = mine_ref if entry < groups else other_ref
                source = (entry % groups, pl.ds(h * chunk_rows + first, piece))
                start = pl.multiple_of(index_ref[k] * piece, piece)
                grad_ref[pl.ds(h * rows + start, piece), :] = ref[source + (slice(0, vocab),)]
                lanes = ref[source + (slice(vocab, vocab + LANES),)]
                out_ref[pl.ds(start, piece), pl.ds(depth, LANES)] = lanes.astype(F32)

    columns = pl.ds(pl.multiple_of(step * tile, tile), tile)
    product = jnp.dot(grad_ref[...], weight_ref[:, columns], preferred_element_type=F32)
    for h, out_ref in enumerate(out_refs):
        out_ref[:, columns] = product[h * rows : (h + 1) * rows]


def back(index, mine, other, weight, piece_rows):
    vocab, depth = weight.shape
    all_rows = 2 * mine.shape[0] * mine.shape[1]
    tile = min(depth, 512)
    shape = (all_rows // CHUNKS, depth + LANES)
    return pl.pallas_call(
        functools.partial(back_kernel, piece_rows, tile),
        grid=(depth // tile,),
        in_specs=[SMEM, VMEM, VMEM, VMEM],
        out_specs=[pl.BlockSpec(shape, lambda n: (0, 0))] * CHUNKS,
        out_shape=[jax.ShapeDtypeStruct(shape, F32)] * CHUNKS,
        scratch_shapes=[pltpu.VMEM((all_rows, vocab), BF16)],
        compiler_params=pltpu.CompilerParams(vmem_limit_bytes=28 * 2**20),
        cost_estimate=pl.CostEstimate(
            flops=2 * all_rows * depth * vocab,
            bytes_accessed=2 * vocab * depth + all_rows * (2 * vocab + 4 * depth),
            transcendentals=0,
        ),
    )(index, mine, other, weight)


def outer_kernel(count, copies, index_ref, chosen_ref, *refs):
    pieces, (out_ref, share_ref, grad_ref, held_ref, sems) = refs[:-5], refs[-5:]
    rows = pieces[0].shape[0]
    share = share_ref.shape[0]
    step = pl.program_id(0)
    steps = pl.num_programs(0)
    slots, tile = held_ref.shape[:2]
    part = tile // copies

    def copy(step, k):
        slot = lax.rem(step, slots)
        start = pl.multiple_of(step * tile + k * part, part)
        return pltpu.make_async_copy(
            held_ref.at[slot, pl.ds(k * part, part), :],
            out_ref.at[pl.ds(start, part), :],
            sems.at[slot, k],
        )

    @pl.when(step == 0)
    def _():
        for k, ref in enumerate(pieces):
            start = pl.multiple_of((k // count * count + index_ref[k]) * rows, rows)
            grad_ref[pl.ds(start, rows), :] = ref[...]
        start = pl.multiple_of(index_ref[len(pieces)] * share, share)
        share_ref[...] = grad_ref[pl.ds(start, share), :]

    @pl.when(step >= slots)
    def _():
        for k in range(copies):
            copy(step - slots, k).wait()

    columns = pl.ds(pl.multiple_of(step * tile, tile), tile)
    held_ref[lax.rem(step, slots)] = lax.dot_general(
        grad_ref[:, columns], chosen_ref[...], (((0,), (0,)), ((), ())), preferred_element_type=F32
    )
    for k in range(copies):
        copy(step, k).start()

    @pl.when(step == steps - 1)
    def _():
        for back in range(slots - 1, -1, -1):
            for k in range(copies):
                copy(step - back, k).wait()


def outer(index, chosen, chunks, share_rows):
    depth = chunks[0][0].shape[1]
    all_rows, joined = chosen.shape
    tile = min(depth // 4, 256)
    slots, copies = 3, 4
    pieces = [x for chunk in chunks for x in chunk]
    return pl.pallas_call(
        functools.partial(outer_kernel, len(chunks[0]), copies),
        grid=(depth // tile,),
        in_specs=[SMEM, VMEM] + [VMEM] * len(pieces),
        out_specs=[
            pl.BlockSpec(memory_space=pl.ANY),
            pl.BlockSpec((share_rows, depth), lambda n: (0, 0)),
        ],
        out_shape=[
            jax.ShapeDtypeStruct((depth, joined), F32),
            jax.ShapeDtypeStruct((share_rows, depth), BF16),
        ],
        scratch_shapes=[
            pltpu.VMEM((all_rows, depth), BF16),
            pltpu.VMEM((slots, tile, joined), F32),
            pltpu.SemaphoreType.DMA((slots, copies)),
        ],
        compiler_params=pltpu.CompilerParams(vmem_limit_bytes=32 * 2**20),
        cost_estimate=pl.CostEstimate(
            flops=2 * all_rows * depth * joined,
            bytes_accessed=4 * depth * joined + 2 * all_rows * (depth + joined),
            transcendentals=0,
        ),
    )(index, chosen, *pieces)


def device_table(groups, ring, slots, widths):
    group_rows, chunk_rows, piece_rows, slice_width = widths
    parts = ring.size
    step_rows = piece_rows * parts
    share_rows = group_rows // slots
    table = {}

    def add(name, values):
        table.setdefault(name, []).append(values)

    for g in range(groups.size):
        for v in range(parts):
            p = ring.place[v]
            place = []
            for h in range(CHUNKS):
                held = [ring.order[q] for q in ring.sources(v, h)]
                for i in held:
                    group = i // slots % groups.chips * CORES + i // slots // groups.chips
                    place.append(groups.entry(g, group))
                place += [i % slots for i in held]
            for h in range(CHUNKS):
                start = p * piece_rows
                start = start // chunk_rows * group_rows + h * chunk_rows + start % chunk_rows
                place.append(start // piece_rows)
            add("place", place)
            entry = groups.entry(g, v * share_rows // group_rows)
            first = v * share_rows % group_rows
            start = first // chunk_rows * step_rows + entry * chunk_rows + first % chunk_rows
            pieces = [q for h in range(CHUNKS) for q in ring.sources(v, h)]
            add("pieces", pieces + [start // share_rows])
            add("turn", [(k - p) % parts for k in range(parts)])
            start = p * piece_rows
            add("starts", [g * slice_width, start // chunk_rows, start % chunk_rows, 2 * p, 2 * p + 1])
    return {
        name: np.asarray(rows, np.int32).reshape(groups.size, parts, -1)
        for name, rows in table.items()
    }


def after(x, *others):
    return lax.optimization_barrier((x, others))[0]


def body(hidden, norm_gain, head_weight, target_logits, valid_rows, parents, features):
    groups = Groups(lax.axis_size("dp"))
    parts = lax.axis_size("vocab")
    ring = Ring(parts, groups.chips)
    group_rows, block_width = hidden.shape
    chunk_rows = group_rows // CHUNKS
    step_rows = groups.size * chunk_rows
    piece_rows = step_rows // parts
    model_width = block_width * parts
    slots = parts // groups.size
    slice_width = block_width * slots
    vocab_width = target_logits.shape[1]

    table = device_table(
        groups, ring, slots, (group_rows, chunk_rows, piece_rows, slice_width)
    )
    own = lax.dynamic_slice(
        jnp.asarray(np.concatenate(list(table.values()), axis=2)),
        (lax.axis_index("dp"), lax.axis_index("vocab"), 0),
        (1, 1, sum(rows.shape[2] for rows in table.values())),
    ).reshape(-1)
    index, first = {}, 0
    for name, rows in table.items():
        index[name] = own[first : first + rows.shape[2]]
        first += rows.shape[2]
    gain_start, own_entry, own_first, high_lane, low_lane = [
        index["starts"].astype(jnp.uint32)[k] for k in range(5)
    ]

    def chunk(x, h):
        return x[h * chunk_rows : (h + 1) * chunk_rows]

    def column_owner(g, v):
        far = g % CORES * groups.chips + g // CORES
        return v // slots * parts + far * slots + v % slots

    turn = [
        (g * parts + v, column_owner(g, v)) for g in range(groups.size) for v in range(parts)
    ]
    turned = lax.ppermute(hidden, ("dp", "vocab"), turn)

    weight = hold(head_weight)

    live_rows = (valid_rows == 1).astype(F32)
    squares = jnp.sum(jnp.square(hidden.astype(F32)), axis=1)[None]
    rounds = ring.meetings(lambda terms: sum(terms[1:], terms[0]))
    rounds.append(lambda x: groups.gather_chips(jnp.concatenate([x, live_rows[None]])))
    rounds.append(lambda x: jnp.concatenate([x, groups.swap(x)], axis=0))
    for round in rounds[:2]:
        squares = round(squares)
    turned = after(turned, squares, weight)
    late = rounds[2:]
    exchanged = [squares]

    def seen(step, arrivals):
        if step < len(late):
            exchanged.append(late[step](after(exchanged[-1], arrivals)))

    blocks = [ring.gather(chunk(turned, h), h, seen if h == 0 else None) for h in range(CHUNKS)]
    both = exchanged[-1]
    valid_count = jnp.sum(both[:, 1])
    row_factor = lax.rsqrt(both[:, 0] / model_width + 1e-05)

    targets = target_logits.astype(F32)
    target_top = jnp.max(targets, axis=1)
    target_total = jnp.sum(jnp.exp(targets - target_top[:, None]), axis=1)

    def merge_totals(terms):
        top = functools.reduce(jnp.maximum, [x[0] for x in terms])
        return jnp.stack([top, sum(x[1] * jnp.exp(x[0] - top) for x in terms)])

    own_chosen = choose(parents, features)

    gain = lax.dynamic_slice(norm_gain, (gain_start,), (slice_width,)).reshape(1, slice_width)
    row_weight = 1048576.0 * live_rows / valid_count
    lane = lax.broadcasted_iota(jnp.uint32, (group_rows, LANES), 1)

    keep, send, *pieces = project(
        index["place"], blocks, row_factor, gain, weight, piece_rows
    )
    other = groups.swap(send)

    def chip_sum(d):
        rows = slice(d * group_rows, (d + 1) * group_rows)
        return keep[rows] + other[rows]

    def cross(x, d):
        largest = jnp.maximum(jnp.max(jnp.abs(x), axis=1), 1e-30)
        code = jnp.round(x * (32767.0 / largest)[:, None]).astype(jnp.int16)
        scale = groups.shift(largest, d) / 32767.0
        return groups.shift(code, d).astype(F32) * scale[:, None]

    logits = sum([cross(chip_sum(d), d) for d in range(1, groups.chips)], chip_sum(0))
    top = jnp.max(logits, axis=1)
    total = jnp.sum(jnp.exp(logits - top[:, None]), axis=1)
    mine = jnp.stack([jnp.concatenate([top, target_top]), jnp.concatenate([total, target_total])])
    met = ring.meet(mine, merge_totals)
    scale = jnp.exp(mine[0] - met[0]) / met[1]
    draft_scale, target_scale = scale[:group_rows], scale[group_rows:]

    draft_probs = jnp.exp(logits - top[:, None]) * draft_scale[:, None]
    target_probs = jnp.exp(targets - target_top[:, None]) * target_scale[:, None]
    logit_grad = row_weight[:, None] * (draft_probs - target_probs)
    logit_grad = lax.reduce_precision(logit_grad, 8, 7)
    dot_part = jnp.sum(logit_grad * logits, axis=1)
    dot_high = lax.reduce_precision(dot_part, 8, 7)
    dot_low = dot_part - dot_high
    lanes = jnp.where(lane == high_lane, dot_high[:, None], 0.0) + jnp.where(
        lane == low_lane, dot_low[:, None], 0.0
    )
    mine, other = groups.gather_halves(
        jnp.concatenate([logit_grad.astype(BF16), lanes.astype(BF16)], axis=1)
    )
    products = back(index["turn"], mine, other, weight, piece_rows)
    chosen = after(own_chosen, products).reshape(CHUNKS, chunk_rows, -1)
    chosen = groups.gather(chosen).transpose(1, 0, 2, 3).reshape(CHUNKS * step_rows, -1)

    def shares(product):
        return lambda t: product[t % parts * piece_rows :][:piece_rows]

    grads = []
    for h, summed in enumerate(ring.scatter_sums([shares(x) for x in products])):
        factor = row_factor[:, h * chunk_rows : (h + 1) * chunk_rows]
        own_factor = lax.dynamic_slice(factor, (own_entry, own_first), (1, piece_rows))[0]
        row_dot = jnp.sum(summed[:, slice_width:], axis=1) / own_factor
        grad_piece = (
            own_factor[:, None] * gain * summed[:, :slice_width]
            - pieces[h].astype(F32) * (own_factor**3 * row_dot / model_width)[:, None]
        ).astype(BF16)
        grads.append(ring.gather(grad_piece, h))

    grad_joining, grad_share = outer(index["pieces"], chosen, grads, group_rows // slots)
    return (grad_share, grad_joining)


def solution(mesh):
    placed = (
        P("dp", "vocab"),
        P(),
        P("vocab", "dp"),
        P("dp", "vocab"),
        P("dp"),
        P("dp"),
        P("dp", "vocab"),
    )
    return jax.shard_map(
        body,
        mesh=mesh,
        in_specs=placed,
        out_specs=(P("vocab", "dp"), P("dp", "vocab")),
        check_vma=False,
    )
```

```python
import functools

import jax
import jax.numpy as jnp
import numpy as np
from jax import lax
from jax.experimental import pallas as pl
from jax.experimental.pallas import tpu as pltpu
from jax.sharding import PartitionSpec as P

TREE = 64
CORES = 2
LANES = 128
CHUNKS = 2
F32 = jnp.float32
BF16 = jnp.bfloat16


def ring_order(rows, columns):
    if columns == 1 or rows == 1:
        return list(range(rows * columns))
    order = [r * columns for r in range(rows)]
    for step in range(rows):
        r = rows - 1 - step
        line = [r * columns + c for c in range(1, columns)]
        order += line if step % 2 == 0 else line[::-1]
    return order


class Ring:
    def __init__(self, size, columns):
        self.size = size
        self.columns = columns
        self.half = size // 2
        self.order = ring_order(size // columns, columns)
        self.place = [0] * size
        for position, index in enumerate(self.order):
            self.place[index] = position

    def shift(self, x, step):
        size, order = self.size, self.order
        return lax.ppermute(
            x, "vocab", [(order[p], order[(p + step) % size]) for p in range(size)]
        )

    def partner(self, x, bit):
        return lax.ppermute(x, "vocab", [(v, v ^ bit) for v in range(self.size)])

    def meetings(self, merge):
        near = [bit for bit in range(1, self.columns)]
        far = [bit for bit in range(self.columns, self.size, self.columns)]
        return [
            lambda x, bits=bits: merge([x] + [self.partner(x, bit) for bit in bits])
            for bits in (near, far)
        ]

    def meet(self, x, merge):
        for round in self.meetings(merge):
            x = round(x)
        return x

    def reach(self, h):
        return (self.half, self.half - 1) if h % 2 == 0 else (self.half - 1, self.half)

    def gather(self, block, h, seen=None):
        far_ahead, far_behind = self.reach(h)
        ahead, behind = [block], [block]
        for step in range(self.half):
            if step < far_ahead:
                ahead.append(self.shift(ahead[-1], 1))
            if step < far_behind:
                behind.append(self.shift(behind[-1], -1))
            if seen:
                seen(step, (ahead[-1], behind[-1]))
        return ahead[1:][::-1] + [block] + behind[1:]

    def sources(self, vocab, h):
        p, far_ahead = self.place[vocab], self.reach(h)[0]
        return [(p + k - far_ahead) % self.size for k in range(self.size)]

    def scatter_sums(self, parts):
        got = [[None, None] for _ in parts]
        sent = []
        for step in range(self.half, 0, -1):
            for h, part in enumerate(parts):
                for way, reach in enumerate(self.reach(h)):
                    if step > reach:
                        continue
                    share = part(step if way == 0 else -step)
                    if got[h][way] is not None:
                        share = share + got[h][way].astype(F32)
                    share = share.astype(BF16)
                    if len(sent) >= len(parts):
                        share = after(share, sent[-len(parts)])
                    got[h][way] = self.shift(share, 1 if way == 0 else -1)
                sent.append([x for x in got[h] if x is not None])
        return [
            part(0) + got[h][0].astype(F32) + got[h][1].astype(F32) for h, part in enumerate(parts)
        ]


class Groups:
    def __init__(self, size):
        self.size = size
        self.chips = size // CORES

    def entry(self, index, group):
        chip = (group // CORES - index // CORES) % self.chips
        return (group % CORES ^ index % CORES) * self.chips + chip

    def swap(self, x):
        return lax.ppermute(x, "dp", [(i, i ^ 1) for i in range(self.size)])

    def shift(self, x, step):
        size = self.size
        return lax.ppermute(x, "dp", [(i, (i + CORES * step) % size) for i in range(size)])

    def gather_chips(self, block):
        return jnp.stack([block] + [self.shift(block, -d) for d in range(1, self.chips)])

    def gather_halves(self, block):
        mine = self.gather_chips(block)
        return mine, self.swap(mine)

    def gather(self, block):
        return jnp.concatenate(self.gather_halves(block), axis=0)


VMEM = pl.BlockSpec(memory_space=pltpu.VMEM)
SMEM = pl.BlockSpec(memory_space=pltpu.SMEM)


def choose_kernel(parents_ref, features_ref, out_ref):
    rows = features_ref.shape[0]
    from_row = lax.broadcasted_iota(jnp.int32, (rows, rows), 0)
    row = lax.broadcasted_iota(jnp.int32, (rows, rows), 1)
    chosen = from_row == row // TREE * TREE + parents_ref[...]
    out_ref[...] = lax.dot_general(
        chosen.astype(BF16),
        features_ref[...],
        (((0,), (0,)), ((), ())),
        preferred_element_type=F32,
    ).astype(BF16)


def choose(parents, features):
    return pl.pallas_call(
        choose_kernel,
        in_specs=[VMEM, VMEM],
        out_specs=VMEM,
        out_shape=jax.ShapeDtypeStruct(features.shape, BF16),
        compiler_params=pltpu.CompilerParams(vmem_limit_bytes=12 * 2**20),
        cost_estimate=pl.CostEstimate(
            flops=2 * features.shape[0] * features.size,
            bytes_accessed=4 * features.size,
            transcendentals=0,
        ),
    )(parents.reshape(1, -1), features)


def totals_kernel(logits_ref, out_ref):
    values = logits_ref[...].astype(F32).T
    top = jnp.max(values, axis=0, keepdims=True)
    out_ref[0:1, :] = top
    out_ref[1:2, :] = jnp.sum(jnp.exp(values - top), axis=0, keepdims=True)


def row_totals(logits):
    return pl.pallas_call(
        totals_kernel,
        in_specs=[VMEM],
        out_specs=VMEM,
        out_shape=jax.ShapeDtypeStruct((2, logits.shape[0]), F32),
        compiler_params=pltpu.CompilerParams(vmem_limit_bytes=12 * 2**20),
        cost_estimate=pl.CostEstimate(
            flops=4 * logits.size, bytes_accessed=2 * logits.size, transcendentals=logits.size
        ),
    )(logits)


def hold_kernel(weight_ref, held_ref, sems):
    tile = weight_ref.shape[0] // sems.shape[0]
    copies = [
        pltpu.make_async_copy(
            weight_ref.at[pl.ds(n * tile, tile), :], held_ref.at[pl.ds(n * tile, tile), :], sems.at[n]
        )
        for n in range(sems.shape[0])
    ]
    for copy in copies:
        copy.start()
    for copy in copies:
        copy.wait()


def hold(weight):
    return pl.pallas_call(
        hold_kernel,
        in_specs=[pl.BlockSpec(memory_space=pltpu.HBM)],
        out_specs=VMEM,
        out_shape=jax.ShapeDtypeStruct(weight.shape, weight.dtype),
        scratch_shapes=[pltpu.SemaphoreType.DMA((4,))],
        compiler_params=pltpu.CompilerParams(vmem_limit_bytes=12 * 2**20),
        cost_estimate=pl.CostEstimate(flops=0, bytes_accessed=2 * weight.size, transcendentals=0),
    )(weight)


def project_kernel(count, tile, index_ref, factor_ref, gain_ref, weight_ref, *refs):
    blocks, refs = refs[: CHUNKS * count], refs[CHUNKS * count :]
    keep_ref, send_ref = refs[:CORES]
    piece_refs = refs[CORES : CORES + CHUNKS]
    raw_ref, turned_ref = refs[CORES + CHUNKS :]
    rows, width = blocks[0].shape
    group_rows = CHUNKS * rows
    piece = piece_refs[0].shape[0]
    half = keep_ref.shape[0]
    step = pl.program_id(0)

    @pl.when(step == 0)
    def _():
        for k, ref in enumerate(blocks):
            h, at = k // count, k + k // count * count
            start = pl.multiple_of(index_ref[at] * group_rows + h * rows, rows)
            column = pl.multiple_of(index_ref[at + count] * width, width)
            raw_ref[pl.ds(start, rows), pl.ds(column, width)] = ref[...]
        slab = min(raw_ref.shape[1], 256)
        for g in range(factor_ref.shape[0]):
            group = pl.ds(g * group_rows, group_rows)
            for first in range(0, raw_ref.shape[1], slab):
                columns = pl.ds(first, slab)
                values = raw_ref[group, columns].astype(F32) * gain_ref[:, columns]
                turned_ref[columns, group] = (values.T * factor_ref[g : g + 1, :]).astype(BF16)
        for h, ref in enumerate(piece_refs):
            start = pl.multiple_of(index_ref[2 * CHUNKS * count + h] * piece, piece)
            ref[...] = raw_ref[pl.ds(start, piece), :]

    rows = pl.ds(pl.multiple_of(step * tile, tile), tile)
    logits = jnp.dot(weight_ref[rows, :], turned_ref[...], preferred_element_type=F32).T
    keep_ref[...] = logits[:half]
    send_ref[...] = logits[half:]


def project(index, blocks, factor, gain, weight, piece_rows):
    vocab, depth = weight.shape
    all_rows = factor.shape[0] * factor.shape[1]
    half = all_rows // CORES
    tile = min(vocab, 512)
    out = jax.ShapeDtypeStruct((half, vocab), F32)
    piece = jax.ShapeDtypeStruct((piece_rows, depth), BF16)
    return pl.pallas_call(
        functools.partial(project_kernel, len(blocks[0]), tile),
        grid=(vocab // tile,),
        in_specs=[SMEM] + [VMEM] * (3 + CHUNKS * len(blocks[0])),
        out_specs=[pl.BlockSpec((half, tile), lambda n: (0, n))] * CORES
        + [pl.BlockSpec((piece_rows, depth), lambda n: (0, 0))] * CHUNKS,
        out_shape=[out] * CORES + [piece] * CHUNKS,
        scratch_shapes=[
            pltpu.VMEM((all_rows, depth), BF16),
            pltpu.VMEM((depth, all_rows), BF16),
        ],
        compiler_params=pltpu.CompilerParams(vmem_limit_bytes=28 * 2**20),
        cost_estimate=pl.CostEstimate(
            flops=2 * all_rows * depth * vocab,
            bytes_accessed=2 * vocab * depth + all_rows * (2 * depth + 4 * vocab),
            transcendentals=0,
        ),
    )(index, factor, gain, weight, *[x for chunk in blocks for x in chunk])


def back_kernel(piece, tile, index_ref, mine_ref, other_ref, weight_ref, *refs):
    out_refs, grad_ref = refs[:-1], refs[-1]
    vocab = weight_ref.shape[0]
    rows, depth = out_refs[0].shape[0], out_refs[0].shape[1] - LANES
    step = pl.program_id(0)
    groups, group_rows = mine_ref.shape[:2]
    chunk_rows = group_rows // CHUNKS

    @pl.when(step == 0)
    def _():
        for h, out_ref in enumerate(out_refs):
            for k in range(rows // piece):
                entry, first = k * piece // chunk_rows, k * piece % chunk_rows
                ref = mine_ref if entry < groups else other_ref
                source = (entry % groups, pl.ds(h * chunk_rows + first, piece))
                start = pl.multiple_of(index_ref[k] * piece, piece)
                grad_ref[pl.ds(h * rows + start, piece), :] = ref[source + (slice(0, vocab),)]
                lanes = ref[source + (slice(vocab, vocab + LANES),)]
                out_ref[pl.ds(start, piece), pl.ds(depth, LANES)] = lanes.astype(F32)

    columns = pl.ds(pl.multiple_of(step * tile, tile), tile)
    product = jnp.dot(grad_ref[...], weight_ref[:, columns], preferred_element_type=F32)
    for h, out_ref in enumerate(out_refs):
        out_ref[:, columns] = product[h * rows : (h + 1) * rows]


def back(index, mine, other, weight, piece_rows):
    vocab, depth = weight.shape
    all_rows = 2 * mine.shape[0] * mine.shape[1]
    tile = min(depth, 512)
    shape = (all_rows // CHUNKS, depth + LANES)
    return pl.pallas_call(
        functools.partial(back_kernel, piece_rows, tile),
        grid=(depth // tile,),
        in_specs=[SMEM, VMEM, VMEM, VMEM],
        out_specs=[pl.BlockSpec(shape, lambda n: (0, 0))] * CHUNKS,
        out_shape=[jax.ShapeDtypeStruct(shape, F32)] * CHUNKS,
        scratch_shapes=[pltpu.VMEM((all_rows, vocab), BF16)],
        compiler_params=pltpu.CompilerParams(vmem_limit_bytes=28 * 2**20),
        cost_estimate=pl.CostEstimate(
            flops=2 * all_rows * depth * vocab,
            bytes_accessed=2 * vocab * depth + all_rows * (2 * vocab + 4 * depth),
            transcendentals=0,
        ),
    )(index, mine, other, weight)


def outer_kernel(count, copies, index_ref, chosen_ref, *refs):
    pieces, (out_ref, share_ref, grad_ref, held_ref, sems) = refs[:-5], refs[-5:]
    rows = pieces[0].shape[0]
    share = share_ref.shape[0]
    step = pl.program_id(0)
    steps = pl.num_programs(0)
    slots, tile = held_ref.shape[:2]
    part = tile // copies

    def copy(step, k):
        slot = lax.rem(step, slots)
        start = pl.multiple_of(step * tile + k * part, part)
        return pltpu.make_async_copy(
            held_ref.at[slot, pl.ds(k * part, part), :],
            out_ref.at[pl.ds(start, part), :],
            sems.at[slot, k],
        )

    @pl.when(step == 0)
    def _():
        for k, ref in enumerate(pieces):
            start = pl.multiple_of((k // count * count + index_ref[k]) * rows, rows)
            grad_ref[pl.ds(start, rows), :] = ref[...]
        start = pl.multiple_of(index_ref[len(pieces)] * share, share)
        share_ref[...] = grad_ref[pl.ds(start, share), :]

    @pl.when(step >= slots)
    def _():
        for k in range(copies):
            copy(step - slots, k).wait()

    columns = pl.ds(pl.multiple_of(step * tile, tile), tile)
    held_ref[lax.rem(step, slots)] = lax.dot_general(
        grad_ref[:, columns], chosen_ref[...], (((0,), (0,)), ((), ())), preferred_element_type=F32
    )
    for k in range(copies):
        copy(step, k).start()

    @pl.when(step == steps - 1)
    def _():
        for back in range(slots - 1, -1, -1):
            for k in range(copies):
                copy(step - back, k).wait()


def outer(index, chosen, chunks, share_rows):
    depth = chunks[0][0].shape[1]
    all_rows, joined = chosen.shape
    tile = min(depth // 4, 256)
    slots, copies = 3, 4
    pieces = [x for chunk in chunks for x in chunk]
    return pl.pallas_call(
        functools.partial(outer_kernel, len(chunks[0]), copies),
        grid=(depth // tile,),
        in_specs=[SMEM, VMEM] + [VMEM] * len(pieces),
        out_specs=[
            pl.BlockSpec(memory_space=pl.ANY),
            pl.BlockSpec((share_rows, depth), lambda n: (0, 0)),
        ],
        out_shape=[
            jax.ShapeDtypeStruct((depth, joined), F32),
            jax.ShapeDtypeStruct((share_rows, depth), BF16),
        ],
        scratch_shapes=[
            pltpu.VMEM((all_rows, depth), BF16),
            pltpu.VMEM((slots, tile, joined), F32),
            pltpu.SemaphoreType.DMA((slots, copies)),
        ],
        compiler_params=pltpu.CompilerParams(vmem_limit_bytes=32 * 2**20),
        cost_estimate=pl.CostEstimate(
            flops=2 * all_rows * depth * joined,
            bytes_accessed=4 * depth * joined + 2 * all_rows * (depth + joined),
            transcendentals=0,
        ),
    )(index, chosen, *pieces)


def device_table(groups, ring, slots, widths):
    group_rows, chunk_rows, piece_rows, slice_width = widths
    parts = ring.size
    step_rows = piece_rows * parts
    share_rows = group_rows // slots
    table = {}

    def add(name, values):
        table.setdefault(name, []).append(values)

    for g in range(groups.size):
        for v in range(parts):
            p = ring.place[v]
            place = []
            for h in range(CHUNKS):
                held = [ring.order[q] for q in ring.sources(v, h)]
                for i in held:
                    group = i // slots % groups.chips * CORES + i // slots // groups.chips
                    place.append(groups.entry(g, group))
                place += [i % slots for i in held]
            for h in range(CHUNKS):
                start = p * piece_rows
                start = start // chunk_rows * group_rows + h * chunk_rows + start % chunk_rows
                place.append(start // piece_rows)
            add("place", place)
            entry = groups.entry(g, v * share_rows // group_rows)
            first = v * share_rows % group_rows
            start = first // chunk_rows * step_rows + entry * chunk_rows + first % chunk_rows
            pieces = [q for h in range(CHUNKS) for q in ring.sources(v, h)]
            add("pieces", pieces + [start // share_rows])
            add("turn", [(k - p) % parts for k in range(parts)])
            start = p * piece_rows
            add("starts", [g * slice_width, start // chunk_rows, start % chunk_rows, 2 * p, 2 * p + 1])
    return {
        name: np.asarray(rows, np.int32).reshape(groups.size, parts, -1)
        for name, rows in table.items()
    }


def after(x, *others):
    return lax.optimization_barrier((x, others))[0]


def body(hidden, norm_gain, head_weight, target_logits, valid_rows, parents, features):
    groups = Groups(lax.axis_size("dp"))
    parts = lax.axis_size("vocab")
    ring = Ring(parts, groups.chips)
    group_rows, block_width = hidden.shape
    chunk_rows = group_rows // CHUNKS
    step_rows = groups.size * chunk_rows
    piece_rows = step_rows // parts
    model_width = block_width * parts
    slots = parts // groups.size
    slice_width = block_width * slots
    vocab_width = target_logits.shape[1]

    table = device_table(
        groups, ring, slots, (group_rows, chunk_rows, piece_rows, slice_width)
    )
    own = lax.dynamic_slice(
        jnp.asarray(np.concatenate(list(table.values()), axis=2)),
        (lax.axis_index("dp"), lax.axis_index("vocab"), 0),
        (1, 1, sum(rows.shape[2] for rows in table.values())),
    ).reshape(-1)
    index, first = {}, 0
    for name, rows in table.items():
        index[name] = own[first : first + rows.shape[2]]
        first += rows.shape[2]
    gain_start, own_entry, own_first, high_lane, low_lane = [
        index["starts"].astype(jnp.uint32)[k] for k in range(5)
    ]

    def chunk(x, h):
        return x[h * chunk_rows : (h + 1) * chunk_rows]

    def column_owner(g, v):
        far = g % CORES * groups.chips + g // CORES
        return v // slots * parts + far * slots + v % slots

    turn = [
        (g * parts + v, column_owner(g, v)) for g in range(groups.size) for v in range(parts)
    ]
    turned = lax.ppermute(hidden, ("dp", "vocab"), turn)

    weight = hold(head_weight)

    live_rows = (valid_rows == 1).astype(F32)
    squares = jnp.sum(jnp.square(hidden.astype(F32)), axis=1)[None]
    rounds = ring.meetings(lambda terms: sum(terms[1:], terms[0]))
    rounds.append(lambda x: groups.gather_chips(jnp.concatenate([x, live_rows[None]])))
    rounds.append(lambda x: jnp.concatenate([x, groups.swap(x)], axis=0))
    for round in rounds[:2]:
        squares = round(squares)
    turned = after(turned, squares, weight)
    late = rounds[2:]
    exchanged = [squares]

    def seen(step, arrivals):
        if step < len(late):
            exchanged.append(late[step](after(exchanged[-1], arrivals)))

    blocks = [ring.gather(chunk(turned, h), h, seen if h == 0 else None) for h in range(CHUNKS)]
    both = exchanged[-1]
    valid_count = jnp.sum(both[:, 1])
    row_factor = lax.rsqrt(both[:, 0] / model_width + 1e-05)

    targets = target_logits.astype(F32)
    target_totals = row_totals(target_logits)
    target_top = target_totals[0]

    def merge_totals(terms):
        top = functools.reduce(jnp.maximum, [x[0] for x in terms])
        return jnp.stack([top, sum(x[1] * jnp.exp(x[0] - top) for x in terms)])

    own_chosen = choose(parents, features)

    gain = lax.dynamic_slice(norm_gain, (gain_start,), (slice_width,)).reshape(1, slice_width)
    row_weight = 1048576.0 * live_rows / valid_count
    lane = lax.broadcasted_iota(jnp.uint32, (group_rows, LANES), 1)

    keep, send, *pieces = project(
        index["place"], blocks, row_factor, gain, weight, piece_rows
    )
    other = groups.swap(send)

    def chip_sum(d):
        rows = slice(d * group_rows, (d + 1) * group_rows)
        return keep[rows] + other[rows]

    def cross(x, d):
        largest = jnp.maximum(jnp.max(jnp.abs(x), axis=1), 1e-30)
        code = jnp.round(x * (32767.0 / largest)[:, None]).astype(jnp.int16)
        scale = groups.shift(largest, d) / 32767.0
        return groups.shift(code, d).astype(F32) * scale[:, None]

    logits = sum([cross(chip_sum(d), d) for d in range(1, groups.chips)], chip_sum(0))
    top = jnp.max(logits, axis=1)
    total = jnp.sum(jnp.exp(logits - top[:, None]), axis=1)
    mine = jnp.concatenate([jnp.stack([top, total]), target_totals], axis=1)
    met = ring.meet(mine, merge_totals)
    scale = jnp.exp(mine[0] - met[0]) / met[1]
    draft_scale, target_scale = scale[:group_rows], scale[group_rows:]

    draft_probs = jnp.exp(logits - top[:, None]) * draft_scale[:, None]
    target_probs = jnp.exp(targets - target_top[:, None]) * target_scale[:, None]
    logit_grad = row_weight[:, None] * (draft_probs - target_probs)
    logit_grad = lax.reduce_precision(logit_grad, 8, 7)
    dot_part = jnp.sum(logit_grad * logits, axis=1)
    dot_high = lax.reduce_precision(dot_part, 8, 7)
    dot_low = dot_part - dot_high
    lanes = jnp.where(lane == high_lane, dot_high[:, None], 0.0) + jnp.where(
        lane == low_lane, dot_low[:, None], 0.0
    )
    mine, other = groups.gather_halves(
        jnp.concatenate([logit_grad.astype(BF16), lanes.astype(BF16)], axis=1)
    )
    products = back(index["turn"], mine, other, weight, piece_rows)
    chosen = after(own_chosen, products).reshape(CHUNKS, chunk_rows, -1)
    chosen = groups.gather(chosen).transpose(1, 0, 2, 3).reshape(CHUNKS * step_rows, -1)

    def shares(product):
        return lambda t: product[t % parts * piece_rows :][:piece_rows]

    grads = []
    for h, summed in enumerate(ring.scatter_sums([shares(x) for x in products])):
        factor = row_factor[:, h * chunk_rows : (h + 1) * chunk_rows]
        own_factor = lax.dynamic_slice(factor, (own_entry, own_first), (1, piece_rows))[0]
        row_dot = jnp.sum(summed[:, slice_width:], axis=1) / own_factor
        grad_piece = (
            own_factor[:, None] * gain * summed[:, :slice_width]
            - pieces[h].astype(F32) * (own_factor**3 * row_dot / model_width)[:, None]
        ).astype(BF16)
        grads.append(ring.gather(grad_piece, h))

    grad_joining, grad_share = outer(index["pieces"], chosen, grads, group_rows // slots)
    return (grad_share, grad_joining)


def solution(mesh):
    placed = (
        P("dp", "vocab"),
        P(),
        P("vocab", "dp"),
        P("dp", "vocab"),
        P("dp"),
        P("dp"),
        P("dp", "vocab"),
    )
    return jax.shard_map(
        body,
        mesh=mesh,
        in_specs=placed,
        out_specs=(P("vocab", "dp"), P("dp", "vocab")),
        check_vma=False,
    )
```

```python
import functools

import jax
import jax.numpy as jnp
import numpy as np
from jax import lax
from jax.experimental import pallas as pl
from jax.experimental.pallas import tpu as pltpu
from jax.sharding import PartitionSpec as P

TREE = 64
CORES = 2
LANES = 128
CHUNKS = 2
F32 = jnp.float32
BF16 = jnp.bfloat16


def ring_order(rows, columns):
    if columns == 1 or rows == 1:
        return list(range(rows * columns))
    order = [r * columns for r in range(rows)]
    for step in range(rows):
        r = rows - 1 - step
        line = [r * columns + c for c in range(1, columns)]
        order += line if step % 2 == 0 else line[::-1]
    return order


class Ring:
    def __init__(self, size, columns):
        self.size = size
        self.columns = columns
        self.half = size // 2
        self.order = ring_order(size // columns, columns)
        self.place = [0] * size
        for position, index in enumerate(self.order):
            self.place[index] = position

    def shift(self, x, step):
        size, order = self.size, self.order
        return lax.ppermute(
            x, "vocab", [(order[p], order[(p + step) % size]) for p in range(size)]
        )

    def partner(self, x, bit):
        return lax.ppermute(x, "vocab", [(v, v ^ bit) for v in range(self.size)])

    def meetings(self, merge):
        near = [bit for bit in range(1, self.columns)]
        far = [bit for bit in range(self.columns, self.size, self.columns)]
        return [
            lambda x, bits=bits: merge([x] + [self.partner(x, bit) for bit in bits])
            for bits in (near, far)
        ]

    def meet(self, x, merge):
        for round in self.meetings(merge):
            x = round(x)
        return x

    def reach(self, h):
        return (self.half, self.half - 1) if h % 2 == 0 else (self.half - 1, self.half)

    def gather(self, block, h, seen=None):
        far_ahead, far_behind = self.reach(h)
        ahead, behind = [block], [block]
        for step in range(self.half):
            if step < far_ahead:
                ahead.append(self.shift(ahead[-1], 1))
            if step < far_behind:
                behind.append(self.shift(behind[-1], -1))
            if seen:
                seen(step, (ahead[-1], behind[-1]))
        return ahead[1:][::-1] + [block] + behind[1:]

    def sources(self, vocab, h):
        p, far_ahead = self.place[vocab], self.reach(h)[0]
        return [(p + k - far_ahead) % self.size for k in range(self.size)]

    def scatter_sums(self, parts):
        got = [[None, None] for _ in parts]
        sent = []
        for step in range(self.half, 0, -1):
            for h, part in enumerate(parts):
                for way, reach in enumerate(self.reach(h)):
                    if step > reach:
                        continue
                    share = part(step if way == 0 else -step)
                    if got[h][way] is not None:
                        share = share + got[h][way].astype(F32)
                    share = share.astype(BF16)
                    if len(sent) >= len(parts):
                        share = after(share, sent[-len(parts)])
                    got[h][way] = self.shift(share, 1 if way == 0 else -1)
                sent.append([x for x in got[h] if x is not None])
        return [
            part(0) + got[h][0].astype(F32) + got[h][1].astype(F32) for h, part in enumerate(parts)
        ]


class Groups:
    def __init__(self, size):
        self.size = size
        self.chips = size // CORES

    def entry(self, index, group):
        chip = (group // CORES - index // CORES) % self.chips
        return (group % CORES ^ index % CORES) * self.chips + chip

    def swap(self, x):
        return lax.ppermute(x, "dp", [(i, i ^ 1) for i in range(self.size)])

    def shift(self, x, step):
        size = self.size
        return lax.ppermute(x, "dp", [(i, (i + CORES * step) % size) for i in range(size)])

    def gather_chips(self, block):
        return jnp.stack([block] + [self.shift(block, -d) for d in range(1, self.chips)])

    def gather_halves(self, block):
        mine = self.gather_chips(block)
        return mine, self.swap(mine)

    def gather(self, block):
        return jnp.concatenate(self.gather_halves(block), axis=0)


VMEM = pl.BlockSpec(memory_space=pltpu.VMEM)
SMEM = pl.BlockSpec(memory_space=pltpu.SMEM)


def choose_kernel(parents_ref, features_ref, out_ref):
    rows = features_ref.shape[0]
    from_row = lax.broadcasted_iota(jnp.int32, (rows, rows), 0)
    row = lax.broadcasted_iota(jnp.int32, (rows, rows), 1)
    chosen = from_row == row // TREE * TREE + parents_ref[...]
    out_ref[...] = lax.dot_general(
        chosen.astype(BF16),
        features_ref[...],
        (((0,), (0,)), ((), ())),
        preferred_element_type=F32,
    ).astype(BF16)


def choose(parents, features):
    return pl.pallas_call(
        choose_kernel,
        in_specs=[VMEM, VMEM],
        out_specs=VMEM,
        out_shape=jax.ShapeDtypeStruct(features.shape, BF16),
        compiler_params=pltpu.CompilerParams(vmem_limit_bytes=12 * 2**20),
        cost_estimate=pl.CostEstimate(
            flops=2 * features.shape[0] * features.size,
            bytes_accessed=4 * features.size,
            transcendentals=0,
        ),
    )(parents.reshape(1, -1), features)


def totals_kernel(logits_ref, out_ref):
    values = logits_ref[...].astype(F32).T
    top = jnp.max(values, axis=0, keepdims=True)
    out_ref[0:1, :] = top
    out_ref[1:2, :] = jnp.sum(jnp.exp(values - top), axis=0, keepdims=True)


def row_totals(logits):
    return pl.pallas_call(
        totals_kernel,
        in_specs=[VMEM],
        out_specs=VMEM,
        out_shape=jax.ShapeDtypeStruct((2, logits.shape[0]), F32),
        compiler_params=pltpu.CompilerParams(vmem_limit_bytes=12 * 2**20),
        cost_estimate=pl.CostEstimate(
            flops=4 * logits.size, bytes_accessed=2 * logits.size, transcendentals=logits.size
        ),
    )(logits)


def hold_kernel(weight_ref, held_ref, sems):
    tile = weight_ref.shape[0] // sems.shape[0]
    copies = [
        pltpu.make_async_copy(
            weight_ref.at[pl.ds(n * tile, tile), :], held_ref.at[pl.ds(n * tile, tile), :], sems.at[n]
        )
        for n in range(sems.shape[0])
    ]
    for copy in copies:
        copy.start()
    for copy in copies:
        copy.wait()


def hold(weight):
    return pl.pallas_call(
        hold_kernel,
        in_specs=[pl.BlockSpec(memory_space=pltpu.HBM)],
        out_specs=VMEM,
        out_shape=jax.ShapeDtypeStruct(weight.shape, weight.dtype),
        scratch_shapes=[pltpu.SemaphoreType.DMA((4,))],
        compiler_params=pltpu.CompilerParams(vmem_limit_bytes=12 * 2**20),
        cost_estimate=pl.CostEstimate(flops=0, bytes_accessed=2 * weight.size, transcendentals=0),
    )(weight)


def project_kernel(count, tile, index_ref, factor_ref, gain_ref, weight_ref, *refs):
    blocks, refs = refs[: CHUNKS * count], refs[CHUNKS * count :]
    send_ref, turned_ref = refs[:2]
    piece_refs = refs[2 : 2 + CHUNKS]
    raw_ref, other_ref = refs[2 + CHUNKS :]
    rows, width = blocks[0].shape
    group_rows = CHUNKS * rows
    groups = factor_ref.shape[0]
    piece = piece_refs[0].shape[0]
    step = pl.program_id(0)

    @pl.when(step == 0)
    def _():
        for k, ref in enumerate(blocks):
            h, at = k // count, k + k // count * count
            start = pl.multiple_of(index_ref[at] * group_rows + h * rows, rows)
            column = pl.multiple_of(index_ref[at + count] * width, width)
            raw_ref[pl.ds(start, rows), pl.ds(column, width)] = ref[...]
        slab = min(raw_ref.shape[1], 256)
        for g in range(groups):
            half_ref = turned_ref if g < groups // CORES else other_ref
            place = pl.ds(g % (groups // CORES) * group_rows, group_rows)
            for first in range(0, raw_ref.shape[1], slab):
                columns = pl.ds(first, slab)
                values = raw_ref[pl.ds(g * group_rows, group_rows), columns].astype(F32)
                values = (values * gain_ref[:, columns]).T * factor_ref[g : g + 1, :]
                half_ref[columns, place] = values.astype(BF16)
        for h, ref in enumerate(piece_refs):
            start = pl.multiple_of(index_ref[2 * CHUNKS * count + h] * piece, piece)
            ref[...] = raw_ref[pl.ds(start, piece), :]

    rows = pl.ds(pl.multiple_of(step * tile, tile), tile)
    send_ref[...] = jnp.dot(
        weight_ref[rows, :], other_ref[...], preferred_element_type=F32
    ).T


def project_own_kernel(tile, weight_ref, turned_ref, keep_ref):
    rows = pl.ds(pl.multiple_of(pl.program_id(0) * tile, tile), tile)
    keep_ref[...] = jnp.dot(
        weight_ref[rows, :], turned_ref[...], preferred_element_type=F32
    ).T


def project(index, blocks, factor, gain, weight, piece_rows):
    vocab, depth = weight.shape
    all_rows = factor.shape[0] * factor.shape[1]
    half = all_rows // CORES
    tile = min(vocab, 512)
    out = jax.ShapeDtypeStruct((half, vocab), F32)
    out_spec = pl.BlockSpec((half, tile), lambda n: (0, n))
    piece = jax.ShapeDtypeStruct((piece_rows, depth), BF16)
    whole = lambda rows, columns: pl.BlockSpec((rows, columns), lambda n: (0, 0))
    cost = pl.CostEstimate(
        flops=2 * half * depth * vocab,
        bytes_accessed=2 * vocab * depth + half * (4 * depth + 4 * vocab),
        transcendentals=0,
    )
    send, turned, *pieces = pl.pallas_call(
        functools.partial(project_kernel, len(blocks[0]), tile),
        grid=(vocab // tile,),
        in_specs=[SMEM] + [VMEM] * (3 + CHUNKS * len(blocks[0])),
        out_specs=[out_spec, whole(depth, half)] + [whole(piece_rows, depth)] * CHUNKS,
        out_shape=[out, jax.ShapeDtypeStruct((depth, half), BF16)] + [piece] * CHUNKS,
        scratch_shapes=[pltpu.VMEM((all_rows, depth), BF16), pltpu.VMEM((depth, half), BF16)],
        compiler_params=pltpu.CompilerParams(vmem_limit_bytes=28 * 2**20),
        cost_estimate=cost,
    )(index, factor, gain, weight, *[x for chunk in blocks for x in chunk])
    keep = pl.pallas_call(
        functools.partial(project_own_kernel, tile),
        grid=(vocab // tile,),
        in_specs=[VMEM, VMEM],
        out_specs=out_spec,
        out_shape=out,
        compiler_params=pltpu.CompilerParams(vmem_limit_bytes=20 * 2**20),
        cost_estimate=cost,
    )(weight, turned)
    return [keep, send] + pieces


def back_kernel(piece, tile, index_ref, mine_ref, other_ref, weight_ref, *refs):
    out_refs, grad_ref = refs[:-1], refs[-1]
    vocab = weight_ref.shape[0]
    rows, depth = out_refs[0].shape[0], out_refs[0].shape[1] - LANES
    step = pl.program_id(0)
    groups, group_rows = mine_ref.shape[:2]
    chunk_rows = group_rows // CHUNKS

    @pl.when(step == 0)
    def _():
        for h, out_ref in enumerate(out_refs):
            for k in range(rows // piece):
                entry, first = k * piece // chunk_rows, k * piece % chunk_rows
                ref = mine_ref if entry < groups else other_ref
                source = (entry % groups, pl.ds(h * chunk_rows + first, piece))
                start = pl.multiple_of(index_ref[k] * piece, piece)
                grad_ref[pl.ds(h * rows + start, piece), :] = ref[source + (slice(0, vocab),)]
                lanes = ref[source + (slice(vocab, vocab + LANES),)]
                out_ref[pl.ds(start, piece), pl.ds(depth, LANES)] = lanes.astype(F32)

    columns = pl.ds(pl.multiple_of(step * tile, tile), tile)
    product = jnp.dot(grad_ref[...], weight_ref[:, columns], preferred_element_type=F32)
    for h, out_ref in enumerate(out_refs):
        out_ref[:, columns] = product[h * rows : (h + 1) * rows]


def back(index, mine, other, weight, piece_rows):
    vocab, depth = weight.shape
    all_rows = 2 * mine.shape[0] * mine.shape[1]
    tile = min(depth, 512)
    shape = (all_rows // CHUNKS, depth + LANES)
    return pl.pallas_call(
        functools.partial(back_kernel, piece_rows, tile),
        grid=(depth // tile,),
        in_specs=[SMEM, VMEM, VMEM, VMEM],
        out_specs=[pl.BlockSpec(shape, lambda n: (0, 0))] * CHUNKS,
        out_shape=[jax.ShapeDtypeStruct(shape, F32)] * CHUNKS,
        scratch_shapes=[pltpu.VMEM((all_rows, vocab), BF16)],
        compiler_params=pltpu.CompilerParams(vmem_limit_bytes=28 * 2**20),
        cost_estimate=pl.CostEstimate(
            flops=2 * all_rows * depth * vocab,
            bytes_accessed=2 * vocab * depth + all_rows * (2 * vocab + 4 * depth),
            transcendentals=0,
        ),
    )(index, mine, other, weight)


def outer_kernel(count, copies, index_ref, chosen_ref, *refs):
    pieces, (out_ref, share_ref, grad_ref, held_ref, sems) = refs[:-5], refs[-5:]
    rows = pieces[0].shape[0]
    share = share_ref.shape[0]
    step = pl.program_id(0)
    steps = pl.num_programs(0)
    slots, tile = held_ref.shape[:2]
    part = tile // copies

    def copy(step, k):
        slot = lax.rem(step, slots)
        start = pl.multiple_of(step * tile + k * part, part)
        return pltpu.make_async_copy(
            held_ref.at[slot, pl.ds(k * part, part), :],
            out_ref.at[pl.ds(start, part), :],
            sems.at[slot, k],
        )

    @pl.when(step == 0)
    def _():
        for k, ref in enumerate(pieces):
            start = pl.multiple_of((k // count * count + index_ref[k]) * rows, rows)
            grad_ref[pl.ds(start, rows), :] = ref[...]
        start = pl.multiple_of(index_ref[len(pieces)] * share, share)
        share_ref[...] = grad_ref[pl.ds(start, share), :]

    @pl.when(step >= slots)
    def _():
        for k in range(copies):
            copy(step - slots, k).wait()

    columns = pl.ds(pl.multiple_of(step * tile, tile), tile)
    held_ref[lax.rem(step, slots)] = lax.dot_general(
        grad_ref[:, columns], chosen_ref[...], (((0,), (0,)), ((), ())), preferred_element_type=F32
    )
    for k in range(copies):
        copy(step, k).start()

    @pl.when(step == steps - 1)
    def _():
        for back in range(slots - 1, -1, -1):
            for k in range(copies):
                copy(step - back, k).wait()


def outer(index, chosen, chunks, share_rows):
    depth = chunks[0][0].shape[1]
    all_rows, joined = chosen.shape
    tile = min(depth // 4, 256)
    slots, copies = 3, 4
    pieces = [x for chunk in chunks for x in chunk]
    return pl.pallas_call(
        functools.partial(outer_kernel, len(chunks[0]), copies),
        grid=(depth // tile,),
        in_specs=[SMEM, VMEM] + [VMEM] * len(pieces),
        out_specs=[
            pl.BlockSpec(memory_space=pl.ANY),
            pl.BlockSpec((share_rows, depth), lambda n: (0, 0)),
        ],
        out_shape=[
            jax.ShapeDtypeStruct((depth, joined), F32),
            jax.ShapeDtypeStruct((share_rows, depth), BF16),
        ],
        scratch_shapes=[
            pltpu.VMEM((all_rows, depth), BF16),
            pltpu.VMEM((slots, tile, joined), F32),
            pltpu.SemaphoreType.DMA((slots, copies)),
        ],
        compiler_params=pltpu.CompilerParams(vmem_limit_bytes=32 * 2**20),
        cost_estimate=pl.CostEstimate(
            flops=2 * all_rows * depth * joined,
            bytes_accessed=4 * depth * joined + 2 * all_rows * (depth + joined),
            transcendentals=0,
        ),
    )(index, chosen, *pieces)


def device_table(groups, ring, slots, widths):
    group_rows, chunk_rows, piece_rows, slice_width = widths
    parts = ring.size
    step_rows = piece_rows * parts
    share_rows = group_rows // slots
    table = {}

    def add(name, values):
        table.setdefault(name, []).append(values)

    for g in range(groups.size):
        for v in range(parts):
            p = ring.place[v]
            place = []
            for h in range(CHUNKS):
                held = [ring.order[q] for q in ring.sources(v, h)]
                for i in held:
                    group = i // slots % groups.chips * CORES + i // slots // groups.chips
                    place.append(groups.entry(g, group))
                place += [i % slots for i in held]
            for h in range(CHUNKS):
                start = p * piece_rows
                start = start // chunk_rows * group_rows + h * chunk_rows + start % chunk_rows
                place.append(start // piece_rows)
            add("place", place)
            entry = groups.entry(g, v * share_rows // group_rows)
            first = v * share_rows % group_rows
            start = first // chunk_rows * step_rows + entry * chunk_rows + first % chunk_rows
            pieces = [q for h in range(CHUNKS) for q in ring.sources(v, h)]
            add("pieces", pieces + [start // share_rows])
            add("turn", [(k - p) % parts for k in range(parts)])
            start = p * piece_rows
            add("starts", [g * slice_width, start // chunk_rows, start % chunk_rows, 2 * p, 2 * p + 1])
    return {
        name: np.asarray(rows, np.int32).reshape(groups.size, parts, -1)
        for name, rows in table.items()
    }


def after(x, *others):
    return lax.optimization_barrier((x, others))[0]


def body(hidden, norm_gain, head_weight, target_logits, valid_rows, parents, features):
    groups = Groups(lax.axis_size("dp"))
    parts = lax.axis_size("vocab")
    ring = Ring(parts, groups.chips)
    group_rows, block_width = hidden.shape
    chunk_rows = group_rows // CHUNKS
    step_rows = groups.size * chunk_rows
    piece_rows = step_rows // parts
    model_width = block_width * parts
    slots = parts // groups.size
    slice_width = block_width * slots
    vocab_width = target_logits.shape[1]

    table = device_table(
        groups, ring, slots, (group_rows, chunk_rows, piece_rows, slice_width)
    )
    own = lax.dynamic_slice(
        jnp.asarray(np.concatenate(list(table.values()), axis=2)),
        (lax.axis_index("dp"), lax.axis_index("vocab"), 0),
        (1, 1, sum(rows.shape[2] for rows in table.values())),
    ).reshape(-1)
    index, first = {}, 0
    for name, rows in table.items():
        index[name] = own[first : first + rows.shape[2]]
        first += rows.shape[2]
    gain_start, own_entry, own_first, high_lane, low_lane = [
        index["starts"].astype(jnp.uint32)[k] for k in range(5)
    ]

    def chunk(x, h):
        return x[h * chunk_rows : (h + 1) * chunk_rows]

    def column_owner(g, v):
        far = g % CORES * groups.chips + g // CORES
        return v // slots * parts + far * slots + v % slots

    turn = [
        (g * parts + v, column_owner(g, v)) for g in range(groups.size) for v in range(parts)
    ]
    turned = lax.ppermute(hidden, ("dp", "vocab"), turn)

    weight = hold(head_weight)

    live_rows = (valid_rows == 1).astype(F32)
    squares = jnp.sum(jnp.square(hidden.astype(F32)), axis=1)[None]
    rounds = ring.meetings(lambda terms: sum(terms[1:], terms[0]))
    rounds.append(lambda x: groups.gather_chips(jnp.concatenate([x, live_rows[None]])))
    rounds.append(lambda x: jnp.concatenate([x, groups.swap(x)], axis=0))
    for round in rounds[:2]:
        squares = round(squares)
    turned = after(turned, squares, weight)
    late = rounds[2:]
    exchanged = [squares]

    def seen(step, arrivals):
        if step < len(late):
            exchanged.append(late[step](after(exchanged[-1], arrivals)))

    blocks = [ring.gather(chunk(turned, h), h, seen if h == 0 else None) for h in range(CHUNKS)]
    both = exchanged[-1]
    valid_count = jnp.sum(both[:, 1])
    row_factor = lax.rsqrt(both[:, 0] / model_width + 1e-05)

    targets = target_logits.astype(F32)
    target_totals = row_totals(target_logits)
    target_top = target_totals[0]

    def merge_totals(terms):
        top = functools.reduce(jnp.maximum, [x[0] for x in terms])
        return jnp.stack([top, sum(x[1] * jnp.exp(x[0] - top) for x in terms)])

    own_chosen = choose(parents, features)

    gain = lax.dynamic_slice(norm_gain, (gain_start,), (slice_width,)).reshape(1, slice_width)
    row_weight = 1048576.0 * live_rows / valid_count
    lane = lax.broadcasted_iota(jnp.uint32, (group_rows, LANES), 1)

    keep, send, *pieces = project(
        index["place"], blocks, row_factor, gain, weight, piece_rows
    )
    other = groups.swap(send)

    def chip_sum(d):
        rows = slice(d * group_rows, (d + 1) * group_rows)
        return keep[rows] + other[rows]

    def cross(x, d):
        largest = jnp.maximum(jnp.max(jnp.abs(x), axis=1), 1e-30)
        code = jnp.round(x * (32767.0 / largest)[:, None]).astype(jnp.int16)
        scale = groups.shift(largest, d) / 32767.0
        return groups.shift(code, d).astype(F32) * scale[:, None]

    logits = sum([cross(chip_sum(d), d) for d in range(1, groups.chips)], chip_sum(0))
    top = jnp.max(logits, axis=1)
    total = jnp.sum(jnp.exp(logits - top[:, None]), axis=1)
    mine = jnp.concatenate([jnp.stack([top, total]), target_totals], axis=1)
    met = ring.meet(mine, merge_totals)
    scale = jnp.exp(mine[0] - met[0]) / met[1]
    draft_scale, target_scale = scale[:group_rows], scale[group_rows:]

    draft_probs = jnp.exp(logits - top[:, None]) * draft_scale[:, None]
    target_probs = jnp.exp(targets - target_top[:, None]) * target_scale[:, None]
    logit_grad = row_weight[:, None] * (draft_probs - target_probs)
    logit_grad = lax.reduce_precision(logit_grad, 8, 7)
    dot_part = jnp.sum(logit_grad * logits, axis=1)
    dot_high = lax.reduce_precision(dot_part, 8, 7)
    dot_low = dot_part - dot_high
    lanes = jnp.where(lane == high_lane, dot_high[:, None], 0.0) + jnp.where(
        lane == low_lane, dot_low[:, None], 0.0
    )
    mine, other = groups.gather_halves(
        jnp.concatenate([logit_grad.astype(BF16), lanes.astype(BF16)], axis=1)
    )
    products = back(index["turn"], mine, other, weight, piece_rows)
    chosen = after(own_chosen, products).reshape(CHUNKS, chunk_rows, -1)
    chosen = groups.gather(chosen).transpose(1, 0, 2, 3).reshape(CHUNKS * step_rows, -1)

    def shares(product):
        return lambda t: product[t % parts * piece_rows :][:piece_rows]

    grads = []
    for h, summed in enumerate(ring.scatter_sums([shares(x) for x in products])):
        factor = row_factor[:, h * chunk_rows : (h + 1) * chunk_rows]
        own_factor = lax.dynamic_slice(factor, (own_entry, own_first), (1, piece_rows))[0]
        row_dot = jnp.sum(summed[:, slice_width:], axis=1) / own_factor
        grad_piece = (
            own_factor[:, None] * gain * summed[:, :slice_width]
            - pieces[h].astype(F32) * (own_factor**3 * row_dot / model_width)[:, None]
        ).astype(BF16)
        grads.append(ring.gather(grad_piece, h))

    grad_joining, grad_share = outer(index["pieces"], chosen, grads, group_rows // slots)
    return (grad_share, grad_joining)


def solution(mesh):
    placed = (
        P("dp", "vocab"),
        P(),
        P("vocab", "dp"),
        P("dp", "vocab"),
        P("dp"),
        P("dp"),
        P("dp", "vocab"),
    )
    return jax.shard_map(
        body,
        mesh=mesh,
        in_specs=placed,
        out_specs=(P("vocab", "dp"), P("dp", "vocab")),
        check_vma=False,
    )
```

```python
import functools

import jax
import jax.numpy as jnp
import numpy as np
from jax import lax
from jax.experimental import pallas as pl
from jax.experimental.pallas import tpu as pltpu
from jax.sharding import PartitionSpec as P

TREE = 64
CORES = 2
LANES = 128
CHUNKS = 2
F32 = jnp.float32
BF16 = jnp.bfloat16


def ring_order(rows, columns):
    if columns == 1 or rows == 1:
        return list(range(rows * columns))
    order = [r * columns for r in range(rows)]
    for step in range(rows):
        r = rows - 1 - step
        line = [r * columns + c for c in range(1, columns)]
        order += line if step % 2 == 0 else line[::-1]
    return order


class Ring:
    def __init__(self, size, columns):
        self.size = size
        self.columns = columns
        self.half = size // 2
        self.order = ring_order(size // columns, columns)
        self.place = [0] * size
        for position, index in enumerate(self.order):
            self.place[index] = position

    def shift(self, x, step):
        size, order = self.size, self.order
        return lax.ppermute(
            x, "vocab", [(order[p], order[(p + step) % size]) for p in range(size)]
        )

    def partner(self, x, bit):
        return lax.ppermute(x, "vocab", [(v, v ^ bit) for v in range(self.size)])

    def meetings(self, merge):
        near = [bit for bit in range(1, self.columns)]
        far = [bit for bit in range(self.columns, self.size, self.columns)]
        return [
            lambda x, bits=bits: merge([x] + [self.partner(x, bit) for bit in bits])
            for bits in (near, far)
        ]

    def meet(self, x, merge):
        for round in self.meetings(merge):
            x = round(x)
        return x

    def reach(self, h):
        return (self.half, self.half - 1) if h % 2 == 0 else (self.half - 1, self.half)

    def gather(self, block, h, seen=None):
        far_ahead, far_behind = self.reach(h)
        ahead, behind = [block], [block]
        for step in range(self.half):
            if step < far_ahead:
                ahead.append(self.shift(ahead[-1], 1))
            if step < far_behind:
                behind.append(self.shift(behind[-1], -1))
            if seen:
                seen(step, (ahead[-1], behind[-1]))
        return ahead[1:][::-1] + [block] + behind[1:]

    def sources(self, vocab, h):
        p, far_ahead = self.place[vocab], self.reach(h)[0]
        return [(p + k - far_ahead) % self.size for k in range(self.size)]

    def scatter_sums(self, parts):
        got = [[None, None] for _ in parts]
        sent = []
        for step in range(self.half, 0, -1):
            for h, part in enumerate(parts):
                for way, reach in enumerate(self.reach(h)):
                    if step > reach:
                        continue
                    share = part(step if way == 0 else -step)
                    if got[h][way] is not None:
                        share = share + got[h][way].astype(F32)
                    share = share.astype(BF16)
                    if len(sent) >= len(parts):
                        share = after(share, sent[-len(parts)])
                    got[h][way] = self.shift(share, 1 if way == 0 else -1)
                sent.append([x for x in got[h] if x is not None])
        return [
            part(0) + got[h][0].astype(F32) + got[h][1].astype(F32) for h, part in enumerate(parts)
        ]


class Groups:
    def __init__(self, size):
        self.size = size
        self.chips = size // CORES

    def entry(self, index, group):
        chip = (group // CORES - index // CORES) % self.chips
        return (group % CORES ^ index % CORES) * self.chips + chip

    def swap(self, x):
        return lax.ppermute(x, "dp", [(i, i ^ 1) for i in range(self.size)])

    def shift(self, x, step):
        size = self.size
        return lax.ppermute(x, "dp", [(i, (i + CORES * step) % size) for i in range(size)])

    def gather_chips(self, block):
        return jnp.stack([block] + [self.shift(block, -d) for d in range(1, self.chips)])

    def gather_halves(self, block):
        mine = self.gather_chips(block)
        return mine, self.swap(mine)

    def gather(self, block):
        return jnp.concatenate(self.gather_halves(block), axis=0)


VMEM = pl.BlockSpec(memory_space=pltpu.VMEM)
SMEM = pl.BlockSpec(memory_space=pltpu.SMEM)


def choose_kernel(parents_ref, features_ref, out_ref):
    rows = features_ref.shape[0]
    from_row = lax.broadcasted_iota(jnp.int32, (rows, rows), 0)
    row = lax.broadcasted_iota(jnp.int32, (rows, rows), 1)
    chosen = from_row == row // TREE * TREE + parents_ref[...]
    out_ref[...] = lax.dot_general(
        chosen.astype(BF16),
        features_ref[...],
        (((0,), (0,)), ((), ())),
        preferred_element_type=F32,
    ).astype(BF16)


def choose(parents, features):
    return pl.pallas_call(
        choose_kernel,
        in_specs=[VMEM, VMEM],
        out_specs=VMEM,
        out_shape=jax.ShapeDtypeStruct(features.shape, BF16),
        compiler_params=pltpu.CompilerParams(vmem_limit_bytes=12 * 2**20),
        cost_estimate=pl.CostEstimate(
            flops=2 * features.shape[0] * features.size,
            bytes_accessed=4 * features.size,
            transcendentals=0,
        ),
    )(parents.reshape(1, -1), features)


def totals_kernel(logits_ref, out_ref):
    values = logits_ref[...].astype(F32).T
    top = jnp.max(values, axis=0, keepdims=True)
    out_ref[0:1, :] = top
    out_ref[1:2, :] = jnp.sum(jnp.exp(values - top), axis=0, keepdims=True)


def row_totals(logits):
    return pl.pallas_call(
        totals_kernel,
        in_specs=[VMEM],
        out_specs=VMEM,
        out_shape=jax.ShapeDtypeStruct((2, logits.shape[0]), F32),
        compiler_params=pltpu.CompilerParams(vmem_limit_bytes=12 * 2**20),
        cost_estimate=pl.CostEstimate(
            flops=4 * logits.size, bytes_accessed=2 * logits.size, transcendentals=logits.size
        ),
    )(logits)


def project_kernel(count, tile, index_ref, factor_ref, gain_ref, weight_ref, *refs):
    blocks, refs = refs[: CHUNKS * count], refs[CHUNKS * count :]
    send_ref, turned_ref, held_ref = refs[:3]
    piece_refs = refs[3 : 3 + CHUNKS]
    raw_ref, other_ref, sems = refs[3 + CHUNKS :]
    rows, width = blocks[0].shape
    depth = raw_ref.shape[1]
    group_rows = CHUNKS * rows
    groups = factor_ref.shape[0]
    piece = piece_refs[0].shape[0]
    step = pl.program_id(0)

    def fetch(n):
        tile_rows = pl.ds(pl.multiple_of(n * tile, tile), tile)
        return pltpu.make_async_copy(
            weight_ref.at[tile_rows, :], held_ref.at[tile_rows, :], sems.at[n]
        )

    @pl.when(step == 0)
    def _():
        for n in range(sems.shape[0]):
            fetch(n).start()
        for k, ref in enumerate(blocks):
            h, at = k // count, k + k // count * count
            start = pl.multiple_of(index_ref[at] * group_rows + h * rows, rows)
            column = pl.multiple_of(index_ref[at + count] * width, width)
            raw_ref[pl.ds(start, rows), pl.ds(column, width)] = ref[...]
        slab = min(depth, 256)
        gain_start = index_ref[2 * CHUNKS * count + CHUNKS] * depth
        for g in range(groups):
            half_ref = turned_ref if g < groups // CORES else other_ref
            place = pl.ds(g % (groups // CORES) * group_rows, group_rows)
            for first in range(0, depth, slab):
                columns = pl.ds(first, slab)
                gain = gain_ref[:, pl.ds(pl.multiple_of(gain_start + first, slab), slab)]
                values = raw_ref[pl.ds(g * group_rows, group_rows), columns].astype(F32)
                values = (values * gain).T * factor_ref[g : g + 1, :]
                half_ref[columns, place] = values.astype(BF16)
        for h, ref in enumerate(piece_refs):
            start = pl.multiple_of(index_ref[2 * CHUNKS * count + h] * piece, piece)
            ref[...] = raw_ref[pl.ds(start, piece), :]

    fetch(step).wait()
    rows = pl.ds(pl.multiple_of(step * tile, tile), tile)
    send_ref[...] = jnp.dot(
        held_ref[rows, :], other_ref[...], preferred_element_type=F32
    ).T


def project_own_kernel(tile, weight_ref, turned_ref, keep_ref):
    rows = pl.ds(pl.multiple_of(pl.program_id(0) * tile, tile), tile)
    keep_ref[...] = jnp.dot(
        weight_ref[rows, :], turned_ref[...], preferred_element_type=F32
    ).T


def project(index, blocks, factor, gain, weight, piece_rows):
    vocab, depth = weight.shape
    all_rows = factor.shape[0] * factor.shape[1]
    half = all_rows // CORES
    tile = min(vocab, 512)
    out = jax.ShapeDtypeStruct((half, vocab), F32)
    out_spec = pl.BlockSpec((half, tile), lambda n: (0, n))
    piece = jax.ShapeDtypeStruct((piece_rows, depth), BF16)
    whole = lambda rows, columns: pl.BlockSpec((rows, columns), lambda n: (0, 0))
    cost = pl.CostEstimate(
        flops=2 * half * depth * vocab,
        bytes_accessed=2 * vocab * depth + half * (4 * depth + 4 * vocab),
        transcendentals=0,
    )
    send, turned, held, *pieces = pl.pallas_call(
        functools.partial(project_kernel, len(blocks[0]), tile),
        grid=(vocab // tile,),
        in_specs=[SMEM, VMEM, VMEM, pl.BlockSpec(memory_space=pltpu.HBM)]
        + [VMEM] * (CHUNKS * len(blocks[0])),
        out_specs=[out_spec, whole(depth, half), VMEM] + [whole(piece_rows, depth)] * CHUNKS,
        out_shape=[
            out,
            jax.ShapeDtypeStruct((depth, half), BF16),
            jax.ShapeDtypeStruct(weight.shape, BF16),
        ]
        + [piece] * CHUNKS,
        scratch_shapes=[
            pltpu.VMEM((all_rows, depth), BF16),
            pltpu.VMEM((depth, half), BF16),
            pltpu.SemaphoreType.DMA((vocab // tile,)),
        ],
        compiler_params=pltpu.CompilerParams(vmem_limit_bytes=36 * 2**20),
        cost_estimate=cost,
    )(index, factor, gain, weight, *[x for chunk in blocks for x in chunk])
    keep = pl.pallas_call(
        functools.partial(project_own_kernel, tile),
        grid=(vocab // tile,),
        in_specs=[VMEM, VMEM],
        out_specs=out_spec,
        out_shape=out,
        compiler_params=pltpu.CompilerParams(vmem_limit_bytes=20 * 2**20),
        cost_estimate=cost,
    )(held, turned)
    return [keep, send, held] + pieces


def back_kernel(piece, tile, index_ref, mine_ref, other_ref, weight_ref, *refs):
    out_refs, grad_ref = refs[:-1], refs[-1]
    vocab = weight_ref.shape[0]
    rows, depth = out_refs[0].shape[0], out_refs[0].shape[1] - LANES
    step = pl.program_id(0)
    groups, group_rows = mine_ref.shape[:2]
    chunk_rows = group_rows // CHUNKS

    @pl.when(step == 0)
    def _():
        for h, out_ref in enumerate(out_refs):
            for k in range(rows // piece):
                entry, first = k * piece // chunk_rows, k * piece % chunk_rows
                ref = mine_ref if entry < groups else other_ref
                source = (entry % groups, pl.ds(h * chunk_rows + first, piece))
                start = pl.multiple_of(index_ref[k] * piece, piece)
                grad_ref[pl.ds(h * rows + start, piece), :] = ref[source + (slice(0, vocab),)]
                lanes = ref[source + (slice(vocab, vocab + LANES),)]
                out_ref[pl.ds(start, piece), pl.ds(depth, LANES)] = lanes.astype(F32)

    columns = pl.ds(pl.multiple_of(step * tile, tile), tile)
    product = jnp.dot(grad_ref[...], weight_ref[:, columns], preferred_element_type=F32)
    for h, out_ref in enumerate(out_refs):
        out_ref[:, columns] = product[h * rows : (h + 1) * rows]


def back(index, mine, other, weight, piece_rows):
    vocab, depth = weight.shape
    all_rows = 2 * mine.shape[0] * mine.shape[1]
    tile = min(depth, 512)
    shape = (all_rows // CHUNKS, depth + LANES)
    return pl.pallas_call(
        functools.partial(back_kernel, piece_rows, tile),
        grid=(depth // tile,),
        in_specs=[SMEM, VMEM, VMEM, VMEM],
        out_specs=[pl.BlockSpec(shape, lambda n: (0, 0))] * CHUNKS,
        out_shape=[jax.ShapeDtypeStruct(shape, F32)] * CHUNKS,
        scratch_shapes=[pltpu.VMEM((all_rows, vocab), BF16)],
        compiler_params=pltpu.CompilerParams(vmem_limit_bytes=28 * 2**20),
        cost_estimate=pl.CostEstimate(
            flops=2 * all_rows * depth * vocab,
            bytes_accessed=2 * vocab * depth + all_rows * (2 * vocab + 4 * depth),
            transcendentals=0,
        ),
    )(index, mine, other, weight)


def outer_kernel(count, copies, index_ref, chosen_ref, *refs):
    pieces, (out_ref, share_ref, grad_ref, held_ref, sems) = refs[:-5], refs[-5:]
    rows = pieces[0].shape[0]
    share = share_ref.shape[0]
    step = pl.program_id(0)
    steps = pl.num_programs(0)
    slots, tile = held_ref.shape[:2]
    part = tile // copies

    def copy(step, k):
        slot = lax.rem(step, slots)
        start = pl.multiple_of(step * tile + k * part, part)
        return pltpu.make_async_copy(
            held_ref.at[slot, pl.ds(k * part, part), :],
            out_ref.at[pl.ds(start, part), :],
            sems.at[slot, k],
        )

    @pl.when(step == 0)
    def _():
        for k, ref in enumerate(pieces):
            start = pl.multiple_of((k // count * count + index_ref[k]) * rows, rows)
            grad_ref[pl.ds(start, rows), :] = ref[...]
        start = pl.multiple_of(index_ref[len(pieces)] * share, share)
        share_ref[...] = grad_ref[pl.ds(start, share), :]

    @pl.when(step >= slots)
    def _():
        for k in range(copies):
            copy(step - slots, k).wait()

    columns = pl.ds(pl.multiple_of(step * tile, tile), tile)
    held_ref[lax.rem(step, slots)] = lax.dot_general(
        grad_ref[:, columns], chosen_ref[...], (((0,), (0,)), ((), ())), preferred_element_type=F32
    )
    for k in range(copies):
        copy(step, k).start()

    @pl.when(step == steps - 1)
    def _():
        for back in range(slots - 1, -1, -1):
            for k in range(copies):
                copy(step - back, k).wait()


def outer(index, chosen, chunks, share_rows):
    depth = chunks[0][0].shape[1]
    all_rows, joined = chosen.shape
    tile = min(depth // 4, 256)
    slots, copies = 3, 4
    pieces = [x for chunk in chunks for x in chunk]
    return pl.pallas_call(
        functools.partial(outer_kernel, len(chunks[0]), copies),
        grid=(depth // tile,),
        in_specs=[SMEM, VMEM] + [VMEM] * len(pieces),
        out_specs=[
            pl.BlockSpec(memory_space=pl.ANY),
            pl.BlockSpec((share_rows, depth), lambda n: (0, 0)),
        ],
        out_shape=[
            jax.ShapeDtypeStruct((depth, joined), F32),
            jax.ShapeDtypeStruct((share_rows, depth), BF16),
        ],
        scratch_shapes=[
            pltpu.VMEM((all_rows, depth), BF16),
            pltpu.VMEM((slots, tile, joined), F32),
            pltpu.SemaphoreType.DMA((slots, copies)),
        ],
        compiler_params=pltpu.CompilerParams(vmem_limit_bytes=32 * 2**20),
        cost_estimate=pl.CostEstimate(
            flops=2 * all_rows * depth * joined,
            bytes_accessed=4 * depth * joined + 2 * all_rows * (depth + joined),
            transcendentals=0,
        ),
    )(index, chosen, *pieces)


def device_table(groups, ring, slots, widths):
    group_rows, chunk_rows, piece_rows, slice_width = widths
    parts = ring.size
    step_rows = piece_rows * parts
    share_rows = group_rows // slots
    table = {}

    def add(name, values):
        table.setdefault(name, []).append(values)

    for g in range(groups.size):
        for v in range(parts):
            p = ring.place[v]
            place = []
            for h in range(CHUNKS):
                held = [ring.order[q] for q in ring.sources(v, h)]
                for i in held:
                    group = i // slots % groups.chips * CORES + i // slots // groups.chips
                    place.append(groups.entry(g, group))
                place += [i % slots for i in held]
            for h in range(CHUNKS):
                start = p * piece_rows
                start = start // chunk_rows * group_rows + h * chunk_rows + start % chunk_rows
                place.append(start // piece_rows)
            place.append(g)
            add("place", place)
            entry = groups.entry(g, v * share_rows // group_rows)
            first = v * share_rows % group_rows
            start = first // chunk_rows * step_rows + entry * chunk_rows + first % chunk_rows
            pieces = [q for h in range(CHUNKS) for q in ring.sources(v, h)]
            add("pieces", pieces + [start // share_rows])
            add("turn", [(k - p) % parts for k in range(parts)])
            start = p * piece_rows
            add("starts", [g * slice_width, start // chunk_rows, start % chunk_rows, 2 * p, 2 * p + 1])
    return {
        name: np.asarray(rows, np.int32).reshape(groups.size, parts, -1)
        for name, rows in table.items()
    }


def after(x, *others):
    return lax.optimization_barrier((x, others))[0]


def body(hidden, norm_gain, head_weight, target_logits, valid_rows, parents, features):
    groups = Groups(lax.axis_size("dp"))
    parts = lax.axis_size("vocab")
    ring = Ring(parts, groups.chips)
    group_rows, block_width = hidden.shape
    chunk_rows = group_rows // CHUNKS
    step_rows = groups.size * chunk_rows
    piece_rows = step_rows // parts
    model_width = block_width * parts
    slots = parts // groups.size
    slice_width = block_width * slots
    vocab_width = target_logits.shape[1]

    table = device_table(
        groups, ring, slots, (group_rows, chunk_rows, piece_rows, slice_width)
    )
    own = lax.dynamic_slice(
        jnp.asarray(np.concatenate(list(table.values()), axis=2)),
        (lax.axis_index("dp"), lax.axis_index("vocab"), 0),
        (1, 1, sum(rows.shape[2] for rows in table.values())),
    ).reshape(-1)
    index, first = {}, 0
    for name, rows in table.items():
        index[name] = own[first : first + rows.shape[2]]
        first += rows.shape[2]
    gain_start, own_entry, own_first, high_lane, low_lane = [
        index["starts"].astype(jnp.uint32)[k] for k in range(5)
    ]

    def chunk(x, h):
        return x[h * chunk_rows : (h + 1) * chunk_rows]

    def column_owner(g, v):
        far = g % CORES * groups.chips + g // CORES
        return v // slots * parts + far * slots + v % slots

    turn = [
        (g * parts + v, column_owner(g, v)) for g in range(groups.size) for v in range(parts)
    ]
    turned = lax.ppermute(hidden, ("dp", "vocab"), turn)

    live_rows = (valid_rows == 1).astype(F32)
    squares = jnp.sum(jnp.square(hidden.astype(F32)), axis=1)[None]
    rounds = ring.meetings(lambda terms: sum(terms[1:], terms[0]))
    rounds.append(lambda x: groups.gather_chips(jnp.concatenate([x, live_rows[None]])))
    rounds.append(lambda x: jnp.concatenate([x, groups.swap(x)], axis=0))
    for round in rounds[:2]:
        squares = round(squares)
    turned = after(turned, squares)
    late = rounds[2:]
    exchanged = [squares]

    def seen(step, arrivals):
        if step < len(late):
            exchanged.append(late[step](after(exchanged[-1], arrivals)))

    blocks = [ring.gather(chunk(turned, h), h, seen if h == 0 else None) for h in range(CHUNKS)]
    both = exchanged[-1]
    valid_count = jnp.sum(both[:, 1])
    row_factor = lax.rsqrt(both[:, 0] / model_width + 1e-05)

    targets = target_logits.astype(F32)
    target_totals = row_totals(target_logits)
    target_top = target_totals[0]

    def merge_totals(terms):
        top = functools.reduce(jnp.maximum, [x[0] for x in terms])
        return jnp.stack([top, sum(x[1] * jnp.exp(x[0] - top) for x in terms)])

    own_chosen = choose(parents, features)

    gain = lax.dynamic_slice(norm_gain, (gain_start,), (slice_width,)).reshape(1, slice_width)
    row_weight = 1048576.0 * live_rows / valid_count
    lane = lax.broadcasted_iota(jnp.uint32, (group_rows, LANES), 1)

    keep, send, weight, *pieces = project(
        index["place"], blocks, row_factor, norm_gain.reshape(1, -1), head_weight, piece_rows
    )
    other = groups.swap(send)

    def chip_sum(d):
        rows = slice(d * group_rows, (d + 1) * group_rows)
        return keep[rows] + other[rows]

    def cross(x, d):
        largest = jnp.maximum(jnp.max(jnp.abs(x), axis=1), 1e-30)
        code = jnp.round(x * (32767.0 / largest)[:, None]).astype(jnp.int16)
        scale = groups.shift(largest, d) / 32767.0
        return groups.shift(code, d).astype(F32) * scale[:, None]

    logits = sum([cross(chip_sum(d), d) for d in range(1, groups.chips)], chip_sum(0))
    top = jnp.max(logits, axis=1)
    total = jnp.sum(jnp.exp(logits - top[:, None]), axis=1)
    mine = jnp.concatenate([jnp.stack([top, total]), target_totals], axis=1)
    met = ring.meet(mine, merge_totals)
    scale = jnp.exp(mine[0] - met[0]) / met[1]
    draft_scale, target_scale = scale[:group_rows], scale[group_rows:]

    draft_probs = jnp.exp(logits - top[:, None]) * draft_scale[:, None]
    target_probs = jnp.exp(targets - target_top[:, None]) * target_scale[:, None]
    logit_grad = row_weight[:, None] * (draft_probs - target_probs)
    logit_grad = lax.reduce_precision(logit_grad, 8, 7)
    dot_part = jnp.sum(logit_grad * logits, axis=1)
    dot_high = lax.reduce_precision(dot_part, 8, 7)
    dot_low = dot_part - dot_high
    lanes = jnp.where(lane == high_lane, dot_high[:, None], 0.0) + jnp.where(
        lane == low_lane, dot_low[:, None], 0.0
    )
    mine, other = groups.gather_halves(
        jnp.concatenate([logit_grad.astype(BF16), lanes.astype(BF16)], axis=1)
    )
    products = back(index["turn"], mine, other, weight, piece_rows)
    chosen = after(own_chosen, products).reshape(CHUNKS, chunk_rows, -1)
    chosen = groups.gather(chosen).transpose(1, 0, 2, 3).reshape(CHUNKS * step_rows, -1)

    def shares(product):
        return lambda t: product[t % parts * piece_rows :][:piece_rows]

    weights, turns = [], []
    for h in range(CHUNKS):
        factor = row_factor[:, h * chunk_rows : (h + 1) * chunk_rows]
        own_factor = lax.dynamic_slice(factor, (own_entry, own_first), (1, piece_rows))[0]
        weights.append(own_factor[:, None] * gain)
        turns.append(pieces[h].astype(F32) * (own_factor**2 / model_width)[:, None])
    weights, turns = lax.optimization_barrier((weights, turns))

    grads = []
    for h, summed in enumerate(ring.scatter_sums([shares(x) for x in products])):
        dot = jnp.sum(summed[:, slice_width:], axis=1, keepdims=True)
        grad_piece = (weights[h] * summed[:, :slice_width] - turns[h] * dot).astype(BF16)
        grads.append(ring.gather(grad_piece, h))

    grad_joining, grad_share = outer(index["pieces"], chosen, grads, group_rows // slots)
    return (grad_share, grad_joining)


def solution(mesh):
    placed = (
        P("dp", "vocab"),
        P(),
        P("vocab", "dp"),
        P("dp", "vocab"),
        P("dp"),
        P("dp"),
        P("dp", "vocab"),
    )
    return jax.shard_map(
        body,
        mesh=mesh,
        in_specs=placed,
        out_specs=(P("vocab", "dp"), P("dp", "vocab")),
        check_vma=False,
    )
```

```python
import functools

import jax
import jax.numpy as jnp
import numpy as np
from jax import lax
from jax.experimental import pallas as pl
from jax.experimental.pallas import tpu as pltpu
from jax.sharding import PartitionSpec as P

TREE = 64
CORES = 2
LANES = 128
CHUNKS = 2
F32 = jnp.float32
BF16 = jnp.bfloat16


def ring_order(rows, columns):
    if columns == 1 or rows == 1:
        return list(range(rows * columns))
    order = [r * columns for r in range(rows)]
    for step in range(rows):
        r = rows - 1 - step
        line = [r * columns + c for c in range(1, columns)]
        order += line if step % 2 == 0 else line[::-1]
    return order


class Ring:
    def __init__(self, size, columns):
        self.size = size
        self.columns = columns
        self.half = size // 2
        self.order = ring_order(size // columns, columns)
        self.place = [0] * size
        for position, index in enumerate(self.order):
            self.place[index] = position

    def shift(self, x, step):
        size, order = self.size, self.order
        return lax.ppermute(
            x, "vocab", [(order[p], order[(p + step) % size]) for p in range(size)]
        )

    def partner(self, x, bit):
        return lax.ppermute(x, "vocab", [(v, v ^ bit) for v in range(self.size)])

    def meetings(self, merge):
        near = [bit for bit in range(1, self.columns)]
        far = [bit for bit in range(self.columns, self.size, self.columns)]
        return [
            lambda x, bits=bits: merge([x] + [self.partner(x, bit) for bit in bits])
            for bits in (near, far)
        ]

    def meet(self, x, merge):
        for round in self.meetings(merge):
            x = round(x)
        return x

    def reach(self, h):
        return (self.half, self.half - 1) if h % 2 == 0 else (self.half - 1, self.half)

    def gather(self, block, h, seen=None):
        far_ahead, far_behind = self.reach(h)
        ahead, behind = [block], [block]
        for step in range(self.half):
            if step < far_ahead:
                ahead.append(self.shift(ahead[-1], 1))
            if step < far_behind:
                behind.append(self.shift(behind[-1], -1))
            if seen:
                seen(step, (ahead[-1], behind[-1]))
        return ahead[1:][::-1] + [block] + behind[1:]

    def sources(self, vocab, h):
        p, far_ahead = self.place[vocab], self.reach(h)[0]
        return [(p + k - far_ahead) % self.size for k in range(self.size)]

    def scatter_sums(self, parts):
        got = [[None, None] for _ in parts]
        sent = []
        for step in range(self.half, 0, -1):
            for h, part in enumerate(parts):
                for way, reach in enumerate(self.reach(h)):
                    if step > reach:
                        continue
                    share = part(step if way == 0 else -step)
                    if got[h][way] is not None:
                        share = share + got[h][way].astype(F32)
                    share = share.astype(BF16)
                    if len(sent) >= len(parts):
                        share = after(share, sent[-len(parts)])
                    got[h][way] = self.shift(share, 1 if way == 0 else -1)
                sent.append([x for x in got[h] if x is not None])
        return [
            part(0) + got[h][0].astype(F32) + got[h][1].astype(F32) for h, part in enumerate(parts)
        ]


class Groups:
    def __init__(self, size):
        self.size = size
        self.chips = size // CORES

    def entry(self, index, group):
        chip = (group // CORES - index // CORES) % self.chips
        return (group % CORES ^ index % CORES) * self.chips + chip

    def swap(self, x):
        return lax.ppermute(x, "dp", [(i, i ^ 1) for i in range(self.size)])

    def shift(self, x, step):
        size = self.size
        return lax.ppermute(x, "dp", [(i, (i + CORES * step) % size) for i in range(size)])

    def gather_chips(self, block):
        return jnp.stack([block] + [self.shift(block, -d) for d in range(1, self.chips)])

    def gather_halves(self, block):
        mine = self.gather_chips(block)
        return mine, self.swap(mine)

    def gather(self, block):
        return jnp.concatenate(self.gather_halves(block), axis=0)


VMEM = pl.BlockSpec(memory_space=pltpu.VMEM)
SMEM = pl.BlockSpec(memory_space=pltpu.SMEM)


def choose_kernel(parents_ref, features_ref, out_ref):
    rows = features_ref.shape[0]
    from_row = lax.broadcasted_iota(jnp.int32, (rows, rows), 0)
    row = lax.broadcasted_iota(jnp.int32, (rows, rows), 1)
    chosen = from_row == row // TREE * TREE + parents_ref[...]
    out_ref[...] = lax.dot_general(
        chosen.astype(BF16),
        features_ref[...],
        (((0,), (0,)), ((), ())),
        preferred_element_type=F32,
    ).astype(BF16)


def choose(parents, features):
    return pl.pallas_call(
        choose_kernel,
        in_specs=[VMEM, VMEM],
        out_specs=VMEM,
        out_shape=jax.ShapeDtypeStruct(features.shape, BF16),
        compiler_params=pltpu.CompilerParams(vmem_limit_bytes=12 * 2**20),
        cost_estimate=pl.CostEstimate(
            flops=2 * features.shape[0] * features.size,
            bytes_accessed=4 * features.size,
            transcendentals=0,
        ),
    )(parents.reshape(1, -1), features)


def totals_kernel(logits_ref, out_ref):
    values = logits_ref[...].astype(F32).T
    top = jnp.max(values, axis=0, keepdims=True)
    out_ref[0:1, :] = top
    out_ref[1:2, :] = jnp.sum(jnp.exp(values - top), axis=0, keepdims=True)


def row_totals(logits):
    return pl.pallas_call(
        totals_kernel,
        in_specs=[VMEM],
        out_specs=VMEM,
        out_shape=jax.ShapeDtypeStruct((2, logits.shape[0]), F32),
        compiler_params=pltpu.CompilerParams(vmem_limit_bytes=12 * 2**20),
        cost_estimate=pl.CostEstimate(
            flops=4 * logits.size, bytes_accessed=2 * logits.size, transcendentals=logits.size
        ),
    )(logits)


def project_kernel(count, tile, index_ref, factor_ref, gain_ref, weight_ref, *refs):
    blocks, refs = refs[: CHUNKS * count], refs[CHUNKS * count :]
    send_ref, turned_ref, held_ref = refs[:3]
    piece_refs = refs[3 : 3 + CHUNKS]
    raw_ref, other_ref, sems = refs[3 + CHUNKS :]
    rows, width = blocks[0].shape
    depth = raw_ref.shape[1]
    group_rows = CHUNKS * rows
    groups = factor_ref.shape[0]
    piece = piece_refs[0].shape[0]
    step = pl.program_id(0)

    def fetch(n):
        tile_rows = pl.ds(pl.multiple_of(n * tile, tile), tile)
        return pltpu.make_async_copy(
            weight_ref.at[tile_rows, :], held_ref.at[tile_rows, :], sems.at[n]
        )

    @pl.when(step == 0)
    def _():
        for n in range(sems.shape[0]):
            fetch(n).start()
        for k, ref in enumerate(blocks):
            h, at = k // count, k + k // count * count
            start = pl.multiple_of(index_ref[at] * group_rows + h * rows, rows)
            column = pl.multiple_of(index_ref[at + count] * width, width)
            raw_ref[pl.ds(start, rows), pl.ds(column, width)] = ref[...]
        slab = min(depth, 256)
        gain_start = index_ref[2 * CHUNKS * count + CHUNKS] * depth
        for g in range(groups):
            half_ref = turned_ref if g < groups // CORES else other_ref
            place = pl.ds(g % (groups // CORES) * group_rows, group_rows)
            for first in range(0, depth, slab):
                columns = pl.ds(first, slab)
                gain = gain_ref[:, pl.ds(pl.multiple_of(gain_start + first, slab), slab)]
                values = raw_ref[pl.ds(g * group_rows, group_rows), columns].astype(F32)
                values = (values * gain).T * factor_ref[g : g + 1, :]
                half_ref[columns, place] = values.astype(BF16)
        for h, ref in enumerate(piece_refs):
            start = pl.multiple_of(index_ref[2 * CHUNKS * count + h] * piece, piece)
            ref[...] = raw_ref[pl.ds(start, piece), :]

    fetch(step).wait()
    rows = pl.ds(pl.multiple_of(step * tile, tile), tile)
    send_ref[...] = jnp.dot(
        held_ref[rows, :], other_ref[...], preferred_element_type=F32
    ).T


def project_own_kernel(tile, weight_ref, turned_ref, keep_ref):
    rows = pl.ds(pl.multiple_of(pl.program_id(0) * tile, tile), tile)
    keep_ref[...] = jnp.dot(
        weight_ref[rows, :], turned_ref[...], preferred_element_type=F32
    ).T


def project(index, blocks, factor, gain, weight, piece_rows):
    vocab, depth = weight.shape
    all_rows = factor.shape[0] * factor.shape[1]
    half = all_rows // CORES
    tile = min(vocab, 512)
    out = jax.ShapeDtypeStruct((half, vocab), F32)
    out_spec = pl.BlockSpec((half, tile), lambda n: (0, n))
    piece = jax.ShapeDtypeStruct((piece_rows, depth), BF16)
    whole = lambda rows, columns: pl.BlockSpec((rows, columns), lambda n: (0, 0))
    cost = pl.CostEstimate(
        flops=2 * half * depth * vocab,
        bytes_accessed=2 * vocab * depth + half * (4 * depth + 4 * vocab),
        transcendentals=0,
    )
    send, turned, held, *pieces = pl.pallas_call(
        functools.partial(project_kernel, len(blocks[0]), tile),
        grid=(vocab // tile,),
        in_specs=[SMEM, VMEM, VMEM, pl.BlockSpec(memory_space=pltpu.HBM)]
        + [VMEM] * (CHUNKS * len(blocks[0])),
        out_specs=[out_spec, whole(depth, half), VMEM] + [whole(piece_rows, depth)] * CHUNKS,
        out_shape=[
            out,
            jax.ShapeDtypeStruct((depth, half), BF16),
            jax.ShapeDtypeStruct(weight.shape, BF16),
        ]
        + [piece] * CHUNKS,
        scratch_shapes=[
            pltpu.VMEM((all_rows, depth), BF16),
            pltpu.VMEM((depth, half), BF16),
            pltpu.SemaphoreType.DMA((vocab // tile,)),
        ],
        compiler_params=pltpu.CompilerParams(vmem_limit_bytes=36 * 2**20),
        cost_estimate=cost,
    )(index, factor, gain, weight, *[x for chunk in blocks for x in chunk])
    keep = pl.pallas_call(
        functools.partial(project_own_kernel, tile),
        grid=(vocab // tile,),
        in_specs=[VMEM, VMEM],
        out_specs=out_spec,
        out_shape=out,
        compiler_params=pltpu.CompilerParams(vmem_limit_bytes=20 * 2**20),
        cost_estimate=cost,
    )(held, turned)
    return [keep, send, held] + pieces


def back_kernel(piece, tile, index_ref, mine_ref, other_ref, weight_ref, *refs):
    out_refs, grad_ref = refs[:-1], refs[-1]
    vocab = weight_ref.shape[0]
    rows, depth = out_refs[0].shape[0], out_refs[0].shape[1] - LANES
    step = pl.program_id(0)
    groups, group_rows = mine_ref.shape[:2]
    chunk_rows = group_rows // CHUNKS

    @pl.when(step == 0)
    def _():
        for h, out_ref in enumerate(out_refs):
            for k in range(rows // piece):
                entry, first = k * piece // chunk_rows, k * piece % chunk_rows
                ref = mine_ref if entry < groups else other_ref
                source = (entry % groups, pl.ds(h * chunk_rows + first, piece))
                start = pl.multiple_of(index_ref[k] * piece, piece)
                grad_ref[pl.ds(h * rows + start, piece), :] = ref[source + (slice(0, vocab),)]
                lanes = ref[source + (slice(vocab, vocab + LANES),)]
                out_ref[pl.ds(start, piece), pl.ds(depth, LANES)] = lanes.astype(F32)

    columns = pl.ds(pl.multiple_of(step * tile, tile), tile)
    product = jnp.dot(grad_ref[...], weight_ref[:, columns], preferred_element_type=F32)
    for h, out_ref in enumerate(out_refs):
        out_ref[:, columns] = product[h * rows : (h + 1) * rows]


def back(index, mine, other, weight, piece_rows):
    vocab, depth = weight.shape
    all_rows = 2 * mine.shape[0] * mine.shape[1]
    tile = min(depth, 512)
    shape = (all_rows // CHUNKS, depth + LANES)
    return pl.pallas_call(
        functools.partial(back_kernel, piece_rows, tile),
        grid=(depth // tile,),
        in_specs=[SMEM, VMEM, VMEM, VMEM],
        out_specs=[pl.BlockSpec(shape, lambda n: (0, 0))] * CHUNKS,
        out_shape=[jax.ShapeDtypeStruct(shape, F32)] * CHUNKS,
        scratch_shapes=[pltpu.VMEM((all_rows, vocab), BF16)],
        compiler_params=pltpu.CompilerParams(vmem_limit_bytes=28 * 2**20),
        cost_estimate=pl.CostEstimate(
            flops=2 * all_rows * depth * vocab,
            bytes_accessed=2 * vocab * depth + all_rows * (2 * vocab + 4 * depth),
            transcendentals=0,
        ),
    )(index, mine, other, weight)


def outer_kernel(count, copies, index_ref, chosen_ref, *refs):
    pieces, (out_ref, share_ref, grad_ref, held_ref, sems) = refs[:-5], refs[-5:]
    rows = pieces[0].shape[0]
    share = share_ref.shape[0]
    step = pl.program_id(0)
    steps = pl.num_programs(0)
    slots, tile = held_ref.shape[:2]
    part = tile // copies

    def copy(step, k):
        slot = lax.rem(step, slots)
        start = pl.multiple_of(step * tile + k * part, part)
        return pltpu.make_async_copy(
            held_ref.at[slot, pl.ds(k * part, part), :],
            out_ref.at[pl.ds(start, part), :],
            sems.at[slot, k],
        )

    @pl.when(step == 0)
    def _():
        for k, ref in enumerate(pieces):
            start = pl.multiple_of((k // count * count + index_ref[k]) * rows, rows)
            grad_ref[pl.ds(start, rows), :] = ref[...]
        start = pl.multiple_of(index_ref[len(pieces)] * share, share)
        share_ref[...] = grad_ref[pl.ds(start, share), :]

    @pl.when(step >= slots)
    def _():
        for k in range(copies):
            copy(step - slots, k).wait()

    columns = pl.ds(pl.multiple_of(step * tile, tile), tile)
    held_ref[lax.rem(step, slots)] = lax.dot_general(
        grad_ref[:, columns], chosen_ref[...], (((0,), (0,)), ((), ())), preferred_element_type=F32
    )
    for k in range(copies):
        copy(step, k).start()

    @pl.when(step == steps - 1)
    def _():
        for back in range(slots - 1, -1, -1):
            for k in range(copies):
                copy(step - back, k).wait()


def outer(index, chosen, chunks, share_rows):
    depth = chunks[0][0].shape[1]
    all_rows, joined = chosen.shape
    tile = min(depth // 4, 256)
    slots, copies = 3, 4
    pieces = [x for chunk in chunks for x in chunk]
    return pl.pallas_call(
        functools.partial(outer_kernel, len(chunks[0]), copies),
        grid=(depth // tile,),
        in_specs=[SMEM, VMEM] + [VMEM] * len(pieces),
        out_specs=[
            pl.BlockSpec(memory_space=pl.ANY),
            pl.BlockSpec((share_rows, depth), lambda n: (0, 0)),
        ],
        out_shape=[
            jax.ShapeDtypeStruct((depth, joined), F32),
            jax.ShapeDtypeStruct((share_rows, depth), BF16),
        ],
        scratch_shapes=[
            pltpu.VMEM((all_rows, depth), BF16),
            pltpu.VMEM((slots, tile, joined), F32),
            pltpu.SemaphoreType.DMA((slots, copies)),
        ],
        compiler_params=pltpu.CompilerParams(vmem_limit_bytes=32 * 2**20),
        cost_estimate=pl.CostEstimate(
            flops=2 * all_rows * depth * joined,
            bytes_accessed=4 * depth * joined + 2 * all_rows * (depth + joined),
            transcendentals=0,
        ),
    )(index, chosen, *pieces)


def device_table(groups, ring, slots, widths):
    group_rows, chunk_rows, piece_rows, slice_width = widths
    parts = ring.size
    step_rows = piece_rows * parts
    share_rows = group_rows // slots
    table = {}

    def add(name, values):
        table.setdefault(name, []).append(values)

    for g in range(groups.size):
        for v in range(parts):
            p = ring.place[v]
            place = []
            for h in range(CHUNKS):
                held = [ring.order[q] for q in ring.sources(v, h)]
                for i in held:
                    group = i // slots % groups.chips * CORES + i // slots // groups.chips
                    place.append(groups.entry(g, group))
                place += [i % slots for i in held]
            for h in range(CHUNKS):
                start = p * piece_rows
                start = start // chunk_rows * group_rows + h * chunk_rows + start % chunk_rows
                place.append(start // piece_rows)
            place.append(g)
            add("place", place)
            entry = groups.entry(g, v * share_rows // group_rows)
            first = v * share_rows % group_rows
            start = first // chunk_rows * step_rows + entry * chunk_rows + first % chunk_rows
            pieces = [q for h in range(CHUNKS) for q in ring.sources(v, h)]
            add("pieces", pieces + [start // share_rows])
            add("turn", [(k - p) % parts for k in range(parts)])
            start = p * piece_rows
            add("starts", [g * slice_width, start // chunk_rows, start % chunk_rows, 2 * p, 2 * p + 1])
    return {
        name: np.asarray(rows, np.int32).reshape(groups.size, parts, -1)
        for name, rows in table.items()
    }


def after(x, *others):
    return lax.optimization_barrier((x, others))[0]


def body(hidden, norm_gain, head_weight, target_logits, valid_rows, parents, features):
    groups = Groups(lax.axis_size("dp"))
    parts = lax.axis_size("vocab")
    ring = Ring(parts, groups.chips)
    group_rows, block_width = hidden.shape
    chunk_rows = group_rows // CHUNKS
    step_rows = groups.size * chunk_rows
    piece_rows = step_rows // parts
    model_width = block_width * parts
    slots = parts // groups.size
    slice_width = block_width * slots
    vocab_width = target_logits.shape[1]

    table = device_table(
        groups, ring, slots, (group_rows, chunk_rows, piece_rows, slice_width)
    )
    own = lax.dynamic_slice(
        jnp.asarray(np.concatenate(list(table.values()), axis=2)),
        (lax.axis_index("dp"), lax.axis_index("vocab"), 0),
        (1, 1, sum(rows.shape[2] for rows in table.values())),
    ).reshape(-1)
    index, first = {}, 0
    for name, rows in table.items():
        index[name] = own[first : first + rows.shape[2]]
        first += rows.shape[2]
    gain_start, own_entry, own_first, high_lane, low_lane = [
        index["starts"].astype(jnp.uint32)[k] for k in range(5)
    ]

    def chunk(x, h):
        return x[h * chunk_rows : (h + 1) * chunk_rows]

    def column_owner(g, v):
        far = g % CORES * groups.chips + g // CORES
        return v // slots * parts + far * slots + v % slots

    turn = [
        (g * parts + v, column_owner(g, v)) for g in range(groups.size) for v in range(parts)
    ]
    turned = lax.ppermute(hidden, ("dp", "vocab"), turn)

    live_rows = (valid_rows == 1).astype(F32)
    squares = jnp.sum(jnp.square(hidden.astype(F32)), axis=1)[None]
    rounds = ring.meetings(lambda terms: sum(terms[1:], terms[0]))[::-1]
    rounds.append(lambda x: groups.gather_chips(jnp.concatenate([x, live_rows[None]])))
    rounds.append(lambda x: jnp.concatenate([x, groups.swap(x)], axis=0))
    squares = rounds[0](squares)
    turned = after(turned, squares)
    late = rounds[1:]
    exchanged = [squares]

    def seen(step, arrivals):
        if step < len(late):
            exchanged.append(late[step](after(exchanged[-1], arrivals)))

    blocks = [ring.gather(chunk(turned, h), h, seen if h == 0 else None) for h in range(CHUNKS)]
    both = exchanged[-1]
    valid_count = jnp.sum(both[:, 1])
    row_factor = lax.rsqrt(both[:, 0] / model_width + 1e-05)

    targets = target_logits.astype(F32)
    target_totals = row_totals(target_logits)
    target_top = target_totals[0]

    def merge_totals(terms):
        top = functools.reduce(jnp.maximum, [x[0] for x in terms])
        return jnp.stack([top, sum(x[1] * jnp.exp(x[0] - top) for x in terms)])

    own_chosen = choose(parents, features)

    gain = lax.dynamic_slice(norm_gain, (gain_start,), (slice_width,)).reshape(1, slice_width)
    row_weight = 1048576.0 * live_rows / valid_count
    lane = lax.broadcasted_iota(jnp.uint32, (group_rows, LANES), 1)

    keep, send, weight, *pieces = project(
        index["place"], blocks, row_factor, norm_gain.reshape(1, -1), head_weight, piece_rows
    )
    other = groups.swap(send)

    def chip_sum(d):
        rows = slice(d * group_rows, (d + 1) * group_rows)
        return keep[rows] + other[rows]

    def cross(x, d):
        largest = jnp.maximum(jnp.max(jnp.abs(x), axis=1), 1e-30)
        code = jnp.round(x * (32767.0 / largest)[:, None]).astype(jnp.int16)
        scale = groups.shift(largest, d) / 32767.0
        return groups.shift(code, d).astype(F32) * scale[:, None]

    logits = sum([cross(chip_sum(d), d) for d in range(1, groups.chips)], chip_sum(0))
    top = jnp.max(logits, axis=1)
    total = jnp.sum(jnp.exp(logits - top[:, None]), axis=1)
    mine = jnp.concatenate([jnp.stack([top, total]), target_totals], axis=1)
    met = ring.meet(mine, merge_totals)
    scale = jnp.exp(mine[0] - met[0]) / met[1]
    draft_scale, target_scale = scale[:group_rows], scale[group_rows:]

    draft_probs = jnp.exp(logits - top[:, None]) * draft_scale[:, None]
    target_probs = jnp.exp(targets - target_top[:, None]) * target_scale[:, None]
    logit_grad = row_weight[:, None] * (draft_probs - target_probs)
    logit_grad = lax.reduce_precision(logit_grad, 8, 7)
    dot_part = jnp.sum(logit_grad * logits, axis=1)
    dot_high = lax.reduce_precision(dot_part, 8, 7)
    dot_low = dot_part - dot_high
    lanes = jnp.where(lane == high_lane, dot_high[:, None], 0.0) + jnp.where(
        lane == low_lane, dot_low[:, None], 0.0
    )
    mine, other = groups.gather_halves(
        jnp.concatenate([logit_grad.astype(BF16), lanes.astype(BF16)], axis=1)
    )
    products = back(index["turn"], mine, other, weight, piece_rows)
    chosen = after(own_chosen, products).reshape(CHUNKS, chunk_rows, -1)
    chosen = groups.gather(chosen).transpose(1, 0, 2, 3).reshape(CHUNKS * step_rows, -1)

    def shares(product):
        return lambda t: product[t % parts * piece_rows :][:piece_rows]

    weights, turns = [], []
    for h in range(CHUNKS):
        factor = row_factor[:, h * chunk_rows : (h + 1) * chunk_rows]
        own_factor = lax.dynamic_slice(factor, (own_entry, own_first), (1, piece_rows))[0]
        weights.append(own_factor[:, None] * gain)
        turns.append(pieces[h].astype(F32) * (own_factor**2 / model_width)[:, None])
    weights, turns = lax.optimization_barrier((weights, turns))

    grads = []
    for h, summed in enumerate(ring.scatter_sums([shares(x) for x in products])):
        dot = jnp.sum(summed[:, slice_width:], axis=1, keepdims=True)
        grad_piece = (weights[h] * summed[:, :slice_width] - turns[h] * dot).astype(BF16)
        grads.append(ring.gather(grad_piece, h))

    grad_joining, grad_share = outer(index["pieces"], chosen, grads, group_rows // slots)
    return (grad_share, grad_joining)


def solution(mesh):
    placed = (
        P("dp", "vocab"),
        P(),
        P("vocab", "dp"),
        P("dp", "vocab"),
        P("dp"),
        P("dp"),
        P("dp", "vocab"),
    )
    return jax.shard_map(
        body,
        mesh=mesh,
        in_specs=placed,
        out_specs=(P("vocab", "dp"), P("dp", "vocab")),
        check_vma=False,
    )
```

```python
import functools

import jax
import jax.numpy as jnp
import numpy as np
from jax import lax
from jax.experimental import pallas as pl
from jax.experimental.pallas import tpu as pltpu
from jax.sharding import PartitionSpec as P

TREE = 64
CORES = 2
LANES = 128
CHUNKS = 2
F32 = jnp.float32
BF16 = jnp.bfloat16


def ring_order(rows, columns):
    if columns == 1 or rows == 1:
        return list(range(rows * columns))
    order = [r * columns for r in range(rows)]
    for step in range(rows):
        r = rows - 1 - step
        line = [r * columns + c for c in range(1, columns)]
        order += line if step % 2 == 0 else line[::-1]
    return order


class Ring:
    def __init__(self, size, columns):
        self.size = size
        self.columns = columns
        self.half = size // 2
        self.order = ring_order(size // columns, columns)
        self.place = [0] * size
        for position, index in enumerate(self.order):
            self.place[index] = position

    def shift(self, x, step):
        size, order = self.size, self.order
        return lax.ppermute(
            x, "vocab", [(order[p], order[(p + step) % size]) for p in range(size)]
        )

    def partner(self, x, bit):
        return lax.ppermute(x, "vocab", [(v, v ^ bit) for v in range(self.size)])

    def meetings(self, merge):
        near = [bit for bit in range(1, self.columns)]
        far = [bit for bit in range(self.columns, self.size, self.columns)]
        return [
            lambda x, bits=bits: merge([x] + [self.partner(x, bit) for bit in bits])
            for bits in (near, far)
        ]

    def meet(self, x, merge):
        for round in self.meetings(merge):
            x = round(x)
        return x

    def reach(self, h):
        return (self.half, self.half - 1) if h % 2 == 0 else (self.half - 1, self.half)

    def gather(self, block, h, seen=None):
        far_ahead, far_behind = self.reach(h)
        ahead, behind = [block], [block]
        for step in range(self.half):
            if step < far_ahead:
                ahead.append(self.shift(ahead[-1], 1))
            if step < far_behind:
                behind.append(self.shift(behind[-1], -1))
            if seen:
                seen(step, (ahead[-1], behind[-1]))
        return ahead[1:][::-1] + [block] + behind[1:]

    def sources(self, vocab, h):
        p, far_ahead = self.place[vocab], self.reach(h)[0]
        return [(p + k - far_ahead) % self.size for k in range(self.size)]

    def scatter_sums(self, parts):
        got = [[None, None] for _ in parts]
        sent = []
        for step in range(self.half, 0, -1):
            for h, part in enumerate(parts):
                for way, reach in enumerate(self.reach(h)):
                    if step > reach:
                        continue
                    share = part(step if way == 0 else -step)
                    if got[h][way] is not None:
                        share = share + got[h][way].astype(F32)
                    share = share.astype(BF16)
                    if len(sent) >= len(parts):
                        share = after(share, sent[-len(parts)])
                    got[h][way] = self.shift(share, 1 if way == 0 else -1)
                sent.append([x for x in got[h] if x is not None])
        return [
            part(0) + got[h][0].astype(F32) + got[h][1].astype(F32) for h, part in enumerate(parts)
        ]


class Groups:
    def __init__(self, size):
        self.size = size
        self.chips = size // CORES

    def entry(self, index, group):
        chip = (group // CORES - index // CORES) % self.chips
        return (group % CORES ^ index % CORES) * self.chips + chip

    def swap(self, x):
        return lax.ppermute(x, "dp", [(i, i ^ 1) for i in range(self.size)])

    def shift(self, x, step):
        size = self.size
        return lax.ppermute(x, "dp", [(i, (i + CORES * step) % size) for i in range(size)])

    def gather_chips(self, block):
        return jnp.stack([block] + [self.shift(block, -d) for d in range(1, self.chips)])

    def gather_halves(self, block):
        mine = self.gather_chips(block)
        return mine, self.swap(mine)

    def gather(self, block):
        return jnp.concatenate(self.gather_halves(block), axis=0)


VMEM = pl.BlockSpec(memory_space=pltpu.VMEM)
SMEM = pl.BlockSpec(memory_space=pltpu.SMEM)


def choose_kernel(parents_ref, features_ref, out_ref):
    rows = features_ref.shape[0]
    from_row = lax.broadcasted_iota(jnp.int32, (rows, rows), 0)
    row = lax.broadcasted_iota(jnp.int32, (rows, rows), 1)
    chosen = from_row == row // TREE * TREE + parents_ref[...]
    out_ref[...] = lax.dot_general(
        chosen.astype(BF16),
        features_ref[...],
        (((0,), (0,)), ((), ())),
        preferred_element_type=F32,
    ).astype(BF16)


def choose(parents, features):
    return pl.pallas_call(
        choose_kernel,
        in_specs=[VMEM, VMEM],
        out_specs=VMEM,
        out_shape=jax.ShapeDtypeStruct(features.shape, BF16),
        compiler_params=pltpu.CompilerParams(vmem_limit_bytes=12 * 2**20),
        cost_estimate=pl.CostEstimate(
            flops=2 * features.shape[0] * features.size,
            bytes_accessed=4 * features.size,
            transcendentals=0,
        ),
    )(parents.reshape(1, -1), features)


def totals_kernel(logits_ref, out_ref):
    values = logits_ref[...].astype(F32).T
    top = jnp.max(values, axis=0, keepdims=True)
    out_ref[0:1, :] = top
    out_ref[1:2, :] = jnp.sum(jnp.exp(values - top), axis=0, keepdims=True)


def row_totals(logits):
    return pl.pallas_call(
        totals_kernel,
        in_specs=[VMEM],
        out_specs=VMEM,
        out_shape=jax.ShapeDtypeStruct((2, logits.shape[0]), F32),
        compiler_params=pltpu.CompilerParams(vmem_limit_bytes=12 * 2**20),
        cost_estimate=pl.CostEstimate(
            flops=4 * logits.size, bytes_accessed=2 * logits.size, transcendentals=logits.size
        ),
    )(logits)


def project_kernel(count, tile, index_ref, factor_ref, gain_ref, weight_ref, *refs):
    blocks, refs = refs[: CHUNKS * count], refs[CHUNKS * count :]
    send_ref, turned_ref, held_ref = refs[:3]
    piece_refs = refs[3 : 3 + CHUNKS]
    raw_ref, other_ref, sems = refs[3 + CHUNKS :]
    rows, width = blocks[0].shape
    depth = raw_ref.shape[1]
    group_rows = CHUNKS * rows
    groups = factor_ref.shape[0]
    piece = piece_refs[0].shape[0]
    step = pl.program_id(0)

    def fetch(n):
        tile_rows = pl.ds(pl.multiple_of(n * tile, tile), tile)
        return pltpu.make_async_copy(
            weight_ref.at[tile_rows, :], held_ref.at[tile_rows, :], sems.at[n]
        )

    @pl.when(step == 0)
    def _():
        for n in range(sems.shape[0]):
            fetch(n).start()
        for k, ref in enumerate(blocks):
            h, at = k // count, k + k // count * count
            start = pl.multiple_of(index_ref[at] * group_rows + h * rows, rows)
            column = pl.multiple_of(index_ref[at + count] * width, width)
            raw_ref[pl.ds(start, rows), pl.ds(column, width)] = ref[...]
        slab = min(depth, 256)
        gain_start = index_ref[2 * CHUNKS * count + CHUNKS] * depth
        for g in range(groups):
            half_ref = turned_ref if g < groups // CORES else other_ref
            place = pl.ds(g % (groups // CORES) * group_rows, group_rows)
            for first in range(0, depth, slab):
                columns = pl.ds(first, slab)
                gain = gain_ref[:, pl.ds(pl.multiple_of(gain_start + first, slab), slab)]
                values = raw_ref[pl.ds(g * group_rows, group_rows), columns].astype(F32)
                values = (values * gain).T * factor_ref[g : g + 1, :]
                half_ref[columns, place] = values.astype(BF16)
        for h, ref in enumerate(piece_refs):
            start = pl.multiple_of(index_ref[2 * CHUNKS * count + h] * piece, piece)
            ref[...] = raw_ref[pl.ds(start, piece), :]

    fetch(step).wait()
    rows = pl.ds(pl.multiple_of(step * tile, tile), tile)
    send_ref[...] = jnp.dot(
        held_ref[rows, :], other_ref[...], preferred_element_type=F32
    ).T


def project_own_kernel(tile, weight_ref, turned_ref, keep_ref):
    rows = pl.ds(pl.multiple_of(pl.program_id(0) * tile, tile), tile)
    keep_ref[...] = jnp.dot(
        weight_ref[rows, :], turned_ref[...], preferred_element_type=F32
    ).T


def project(index, blocks, factor, gain, weight, piece_rows):
    vocab, depth = weight.shape
    all_rows = factor.shape[0] * factor.shape[1]
    half = all_rows // CORES
    tile = min(vocab, 512)
    out = jax.ShapeDtypeStruct((half, vocab), F32)
    out_spec = pl.BlockSpec((half, tile), lambda n: (0, n))
    piece = jax.ShapeDtypeStruct((piece_rows, depth), BF16)
    whole = lambda rows, columns: pl.BlockSpec((rows, columns), lambda n: (0, 0))
    cost = pl.CostEstimate(
        flops=2 * half * depth * vocab,
        bytes_accessed=2 * vocab * depth + half * (4 * depth + 4 * vocab),
        transcendentals=0,
    )
    send, turned, held, *pieces = pl.pallas_call(
        functools.partial(project_kernel, len(blocks[0]), tile),
        grid=(vocab // tile,),
        in_specs=[SMEM, VMEM, VMEM, pl.BlockSpec(memory_space=pltpu.HBM)]
        + [VMEM] * (CHUNKS * len(blocks[0])),
        out_specs=[out_spec, whole(depth, half), VMEM] + [whole(piece_rows, depth)] * CHUNKS,
        out_shape=[
            out,
            jax.ShapeDtypeStruct((depth, half), BF16),
            jax.ShapeDtypeStruct(weight.shape, BF16),
        ]
        + [piece] * CHUNKS,
        scratch_shapes=[
            pltpu.VMEM((all_rows, depth), BF16),
            pltpu.VMEM((depth, half), BF16),
            pltpu.SemaphoreType.DMA((vocab // tile,)),
        ],
        compiler_params=pltpu.CompilerParams(vmem_limit_bytes=36 * 2**20),
        cost_estimate=cost,
    )(index, factor, gain, weight, *[x for chunk in blocks for x in chunk])
    keep = pl.pallas_call(
        functools.partial(project_own_kernel, tile),
        grid=(vocab // tile,),
        in_specs=[VMEM, VMEM],
        out_specs=out_spec,
        out_shape=out,
        compiler_params=pltpu.CompilerParams(vmem_limit_bytes=20 * 2**20),
        cost_estimate=cost,
    )(held, turned)
    return [keep, send, held] + pieces


def back_kernel(piece, tile, index_ref, mine_ref, other_ref, weight_ref, *refs):
    out_refs, grad_ref = refs[:-1], refs[-1]
    vocab = weight_ref.shape[0]
    rows, depth = out_refs[0].shape[0], out_refs[0].shape[1] - LANES
    step = pl.program_id(0)
    groups, group_rows = mine_ref.shape[:2]
    chunk_rows = group_rows // CHUNKS

    @pl.when(step == 0)
    def _():
        for h, out_ref in enumerate(out_refs):
            for k in range(rows // piece):
                entry, first = k * piece // chunk_rows, k * piece % chunk_rows
                ref = mine_ref if entry < groups else other_ref
                source = (entry % groups, pl.ds(h * chunk_rows + first, piece))
                start = pl.multiple_of(index_ref[k] * piece, piece)
                grad_ref[pl.ds(h * rows + start, piece), :] = ref[source + (slice(0, vocab),)]
                lanes = ref[source + (slice(vocab, vocab + LANES),)]
                out_ref[pl.ds(start, piece), pl.ds(depth, LANES)] = lanes.astype(F32)

    columns = pl.ds(pl.multiple_of(step * tile, tile), tile)
    product = jnp.dot(grad_ref[...], weight_ref[:, columns], preferred_element_type=F32)
    for h, out_ref in enumerate(out_refs):
        out_ref[:, columns] = product[h * rows : (h + 1) * rows]


def back(index, mine, other, weight, piece_rows):
    vocab, depth = weight.shape
    all_rows = 2 * mine.shape[0] * mine.shape[1]
    tile = min(depth, 512)
    shape = (all_rows // CHUNKS, depth + LANES)
    return pl.pallas_call(
        functools.partial(back_kernel, piece_rows, tile),
        grid=(depth // tile,),
        in_specs=[SMEM, VMEM, VMEM, VMEM],
        out_specs=[pl.BlockSpec(shape, lambda n: (0, 0))] * CHUNKS,
        out_shape=[jax.ShapeDtypeStruct(shape, F32)] * CHUNKS,
        scratch_shapes=[pltpu.VMEM((all_rows, vocab), BF16)],
        compiler_params=pltpu.CompilerParams(vmem_limit_bytes=28 * 2**20),
        cost_estimate=pl.CostEstimate(
            flops=2 * all_rows * depth * vocab,
            bytes_accessed=2 * vocab * depth + all_rows * (2 * vocab + 4 * depth),
            transcendentals=0,
        ),
    )(index, mine, other, weight)


def outer_kernel(count, copies, index_ref, chosen_ref, *refs):
    pieces, (out_ref, share_ref, grad_ref, held_ref, sems) = refs[:-5], refs[-5:]
    rows = pieces[0].shape[0]
    share = share_ref.shape[0]
    step = pl.program_id(0)
    steps = pl.num_programs(0)
    slots, tile = held_ref.shape[:2]
    part = tile // copies

    def copy(step, k):
        slot = lax.rem(step, slots)
        start = pl.multiple_of(step * tile + k * part, part)
        return pltpu.make_async_copy(
            held_ref.at[slot, pl.ds(k * part, part), :],
            out_ref.at[pl.ds(start, part), :],
            sems.at[slot, k],
        )

    @pl.when(step == 0)
    def _():
        for k, ref in enumerate(pieces):
            start = pl.multiple_of((k // count * count + index_ref[k]) * rows, rows)
            grad_ref[pl.ds(start, rows), :] = ref[...]
        start = pl.multiple_of(index_ref[len(pieces)] * share, share)
        share_ref[...] = grad_ref[pl.ds(start, share), :]

    @pl.when(step >= slots)
    def _():
        for k in range(copies):
            copy(step - slots, k).wait()

    columns = pl.ds(pl.multiple_of(step * tile, tile), tile)
    held_ref[lax.rem(step, slots)] = lax.dot_general(
        grad_ref[:, columns], chosen_ref[...], (((0,), (0,)), ((), ())), preferred_element_type=F32
    )
    for k in range(copies):
        copy(step, k).start()

    @pl.when(step == steps - 1)
    def _():
        for back in range(slots - 1, -1, -1):
            for k in range(copies):
                copy(step - back, k).wait()


def outer(index, chosen, chunks, share_rows):
    depth = chunks[0][0].shape[1]
    all_rows, joined = chosen.shape
    tile = min(depth // 4, 512)
    slots, copies = 2, 8
    pieces = [x for chunk in chunks for x in chunk]
    return pl.pallas_call(
        functools.partial(outer_kernel, len(chunks[0]), copies),
        grid=(depth // tile,),
        in_specs=[SMEM, VMEM] + [VMEM] * len(pieces),
        out_specs=[
            pl.BlockSpec(memory_space=pl.ANY),
            pl.BlockSpec((share_rows, depth), lambda n: (0, 0)),
        ],
        out_shape=[
            jax.ShapeDtypeStruct((depth, joined), F32),
            jax.ShapeDtypeStruct((share_rows, depth), BF16),
        ],
        scratch_shapes=[
            pltpu.VMEM((all_rows, depth), BF16),
            pltpu.VMEM((slots, tile, joined), F32),
            pltpu.SemaphoreType.DMA((slots, copies)),
        ],
        compiler_params=pltpu.CompilerParams(vmem_limit_bytes=40 * 2**20),
        cost_estimate=pl.CostEstimate(
            flops=2 * all_rows * depth * joined,
            bytes_accessed=4 * depth * joined + 2 * all_rows * (depth + joined),
            transcendentals=0,
        ),
    )(index, chosen, *pieces)


def device_table(groups, ring, slots, widths):
    group_rows, chunk_rows, piece_rows, slice_width = widths
    parts = ring.size
    step_rows = piece_rows * parts
    share_rows = group_rows // slots
    table = {}

    def add(name, values):
        table.setdefault(name, []).append(values)

    for g in range(groups.size):
        for v in range(parts):
            p = ring.place[v]
            place = []
            for h in range(CHUNKS):
                held = [ring.order[q] for q in ring.sources(v, h)]
                for i in held:
                    group = i // slots % groups.chips * CORES + i // slots // groups.chips
                    place.append(groups.entry(g, group))
                place += [i % slots for i in held]
            for h in range(CHUNKS):
                start = p * piece_rows
                start = start // chunk_rows * group_rows + h * chunk_rows + start % chunk_rows
                place.append(start // piece_rows)
            place.append(g)
            add("place", place)
            entry = groups.entry(g, v * share_rows // group_rows)
            first = v * share_rows % group_rows
            start = first // chunk_rows * step_rows + entry * chunk_rows + first % chunk_rows
            pieces = [q for h in range(CHUNKS) for q in ring.sources(v, h)]
            add("pieces", pieces + [start // share_rows])
            add("turn", [(k - p) % parts for k in range(parts)])
            start = p * piece_rows
            add("starts", [g * slice_width, start // chunk_rows, start % chunk_rows, 2 * p, 2 * p + 1])
    return {
        name: np.asarray(rows, np.int32).reshape(groups.size, parts, -1)
        for name, rows in table.items()
    }


def after(x, *others):
    return lax.optimization_barrier((x, others))[0]


def body(hidden, norm_gain, head_weight, target_logits, valid_rows, parents, features):
    groups = Groups(lax.axis_size("dp"))
    parts = lax.axis_size("vocab")
    ring = Ring(parts, groups.chips)
    group_rows, block_width = hidden.shape
    chunk_rows = group_rows // CHUNKS
    step_rows = groups.size * chunk_rows
    piece_rows = step_rows // parts
    model_width = block_width * parts
    slots = parts // groups.size
    slice_width = block_width * slots
    vocab_width = target_logits.shape[1]

    table = device_table(
        groups, ring, slots, (group_rows, chunk_rows, piece_rows, slice_width)
    )
    own = lax.dynamic_slice(
        jnp.asarray(np.concatenate(list(table.values()), axis=2)),
        (lax.axis_index("dp"), lax.axis_index("vocab"), 0),
        (1, 1, sum(rows.shape[2] for rows in table.values())),
    ).reshape(-1)
    index, first = {}, 0
    for name, rows in table.items():
        index[name] = own[first : first + rows.shape[2]]
        first += rows.shape[2]
    gain_start, own_entry, own_first, high_lane, low_lane = [
        index["starts"].astype(jnp.uint32)[k] for k in range(5)
    ]

    def chunk(x, h):
        return x[h * chunk_rows : (h + 1) * chunk_rows]

    def column_owner(g, v):
        far = g % CORES * groups.chips + g // CORES
        return v // slots * parts + far * slots + v % slots

    turn = [
        (g * parts + v, column_owner(g, v)) for g in range(groups.size) for v in range(parts)
    ]
    turned = lax.ppermute(hidden, ("dp", "vocab"), turn)

    live_rows = (valid_rows == 1).astype(F32)
    squares = jnp.sum(jnp.square(hidden.astype(F32)), axis=1)[None]
    rounds = ring.meetings(lambda terms: sum(terms[1:], terms[0]))
    rounds.append(lambda x: groups.gather_chips(jnp.concatenate([x, live_rows[None]])))
    rounds.append(lambda x: jnp.concatenate([x, groups.swap(x)], axis=0))
    for round in rounds[:2]:
        squares = round(squares)
    turned = after(turned, squares)
    late = rounds[2:]
    exchanged = [squares]

    def seen(step, arrivals):
        if step < len(late):
            exchanged.append(late[step](after(exchanged[-1], arrivals)))

    blocks = [ring.gather(chunk(turned, h), h, seen if h == 0 else None) for h in range(CHUNKS)]
    both = exchanged[-1]
    valid_count = jnp.sum(both[:, 1])
    row_factor = lax.rsqrt(both[:, 0] / model_width + 1e-05)

    targets = target_logits.astype(F32)
    target_totals = row_totals(target_logits)
    target_top = target_totals[0]

    def merge_totals(terms):
        top = functools.reduce(jnp.maximum, [x[0] for x in terms])
        return jnp.stack([top, sum(x[1] * jnp.exp(x[0] - top) for x in terms)])

    own_chosen = choose(parents, features)

    gain = lax.dynamic_slice(norm_gain, (gain_start,), (slice_width,)).reshape(1, slice_width)
    row_weight = 1048576.0 * live_rows / valid_count
    lane = lax.broadcasted_iota(jnp.uint32, (group_rows, LANES), 1)

    keep, send, weight, *pieces = project(
        index["place"], blocks, row_factor, norm_gain.reshape(1, -1), head_weight, piece_rows
    )
    other = groups.swap(send)

    def chip_sum(d):
        rows = slice(d * group_rows, (d + 1) * group_rows)
        return keep[rows] + other[rows]

    def cross(x, d):
        largest = jnp.maximum(jnp.max(jnp.abs(x), axis=1), 1e-30)
        code = jnp.round(x * (32767.0 / largest)[:, None]).astype(jnp.int16)
        scale = groups.shift(largest, d) / 32767.0
        return groups.shift(code, d).astype(F32) * scale[:, None]

    logits = sum([cross(chip_sum(d), d) for d in range(1, groups.chips)], chip_sum(0))
    top = jnp.max(logits, axis=1)
    total = jnp.sum(jnp.exp(logits - top[:, None]), axis=1)
    mine = jnp.concatenate([jnp.stack([top, total]), target_totals], axis=1)
    met = ring.meet(mine, merge_totals)
    scale = jnp.exp(mine[0] - met[0]) / met[1]
    draft_scale, target_scale = scale[:group_rows], scale[group_rows:]

    draft_probs = jnp.exp(logits - top[:, None]) * draft_scale[:, None]
    target_probs = jnp.exp(targets - target_top[:, None]) * target_scale[:, None]
    logit_grad = row_weight[:, None] * (draft_probs - target_probs)
    logit_grad = lax.reduce_precision(logit_grad, 8, 7)
    dot_part = jnp.sum(logit_grad * logits, axis=1)
    dot_high = lax.reduce_precision(dot_part, 8, 7)
    dot_low = dot_part - dot_high
    lanes = jnp.where(lane == high_lane, dot_high[:, None], 0.0) + jnp.where(
        lane == low_lane, dot_low[:, None], 0.0
    )
    mine, other = groups.gather_halves(
        jnp.concatenate([logit_grad.astype(BF16), lanes.astype(BF16)], axis=1)
    )
    products = back(index["turn"], mine, other, weight, piece_rows)
    chosen = after(own_chosen, products).reshape(CHUNKS, chunk_rows, -1)
    chosen = groups.gather(chosen).transpose(1, 0, 2, 3).reshape(CHUNKS * step_rows, -1)

    def shares(product):
        return lambda t: product[t % parts * piece_rows :][:piece_rows]

    weights, turns = [], []
    for h in range(CHUNKS):
        factor = row_factor[:, h * chunk_rows : (h + 1) * chunk_rows]
        own_factor = lax.dynamic_slice(factor, (own_entry, own_first), (1, piece_rows))[0]
        weights.append(own_factor[:, None] * gain)
        turns.append(pieces[h].astype(F32) * (own_factor**2 / model_width)[:, None])
    weights, turns = lax.optimization_barrier((weights, turns))

    grads = []
    for h, summed in enumerate(ring.scatter_sums([shares(x) for x in products])):
        dot = jnp.sum(summed[:, slice_width:], axis=1, keepdims=True)
        grad_piece = (weights[h] * summed[:, :slice_width] - turns[h] * dot).astype(BF16)
        grads.append(ring.gather(grad_piece, h))

    grad_joining, grad_share = outer(index["pieces"], chosen, grads, group_rows // slots)
    return (grad_share, grad_joining)


def solution(mesh):
    placed = (
        P("dp", "vocab"),
        P(),
        P("vocab", "dp"),
        P("dp", "vocab"),
        P("dp"),
        P("dp"),
        P("dp", "vocab"),
    )
    return jax.shard_map(
        body,
        mesh=mesh,
        in_specs=placed,
        out_specs=(P("vocab", "dp"), P("dp", "vocab")),
        check_vma=False,
    )
```
